512 devices in a mesh: section: 32 (over z, y_hi), tensor: 8 (over x, core), dp: 2 (over y_lo).
Axes of the slice: x: 4, y: 4 (y_hi: 2, y_lo: 2; y = y_hi * 2 + y_lo), z: 16, core: 2. Of those that a mesh axis runs over, the one named last changes fastest.
Arguments:
- weight: bfloat16 [32, 6144, 6144], P('section', 'tensor', 'dp'), may hold values from -0.078125 to 0.078125
- adapter_down_map: bfloat16 [32, 6144, 16], P('section', 'tensor'), may hold values from -0.078125 to 0.078125
- adapter_up_map: bfloat16 [32, 16, 6144], P('section', None, 'tensor'), may hold values from -1.5 to 1.5
- gain: float32 [32, 6144], P('section', 'tensor'), may hold values from 0.5 to 1.5
- prior_epoch_input: bfloat16 [32, 2, 2, 48, 6144], P('section', 'dp', None, None, 'tensor'), as said below
- prior_epoch_output: bfloat16 [32, 2, 2, 48, 6144], P('section', 'dp', None, None, 'tensor'), as said below
- initial_step_inputs: bfloat16 [32, 96, 6144], P('section', 'dp', 'tensor'), may hold values from -6 to 6
- initial_step_gradients: bfloat16 [32, 96, 6144], P('section', 'dp', 'tensor'), may hold values from -6 to 6
- sample_numbers: int32 [32, 2, 4], P('section', 'dp'), may hold values from 0 to 1
Outputs:
- grad_down: bfloat16 [32, 6144, 16], P('section', 'tensor')
- grad_up: bfloat16 [32, 16, 6144], P('section', None, 'tensor')
The draws below stay inside these ranges and needn't reach their ends.
Inputs may be any that keep to these rules, and one draw needn't show every extreme that they name: prior_epoch_input[s] equals prior_epoch_output[s-1] for every section s >= 1. `prior_epoch_output`: stored activations of order one.
All inputs are finite; a program needn't handle non-finite values. Where the reference program divides by a largest or mean magnitude, that divisor is 1e-20 or more.
Results may differ from the reference program's by a relative error of at most 0.03.
Values may be sent and summed in bfloat16 or wider, within the bound.
No kernel may reach another device: no remote copies, remote signals or barrier semaphores. Data moves between devices by JAX's collectives and lax.ppermute only.
A program may use at most 64 MiB of HBM per device.

```python
import jax
import jax.numpy as jnp
from jax import lax

MODEL_WIDTH = 6144
ADAPTER_RANK = 16
QBLOCK = 128
TOK = 48
TICKS = 4
SAMPLES = 2
N_SECTION = 32
N_DP = 2


def boundary_values(key):
    values = jax.random.normal(key, (N_SECTION + 1, N_DP, SAMPLES, TOK, MODEL_WIDTH), jnp.float32)
    return values


def draw_prior_epoch_output(key, part):
    values = boundary_values(key)
    return values[1:].astype(jnp.bfloat16)


def draw_prior_epoch_input(key, part):
    values = boundary_values(key)
    return values[:-1].astype(jnp.bfloat16)


def plant(array, rng, low, high):
    longest = array.shape.index(max(array.shape))
    spots = []
    for shift in (0, 1):
        where = [jax.random.randint(jax.random.fold_in(rng, axis), (), 0, length) for axis, length in enumerate(array.shape)]
        where[longest] = (where[longest] + shift) % array.shape[longest]
        spots.append(tuple(where))
    return array.at[spots[0]].set(low).at[spots[1]].set(high)


def block_levels(rng, shape, pieces, smallest, largest):
    def one(axis_at, shards_of):
        draws = jax.random.uniform(jax.random.fold_in(jax.random.fold_in(rng, 6), axis_at), (shards_of,), jnp.float32, smallest / len(pieces), largest / len(pieces))
        return jnp.repeat(jnp.exp(draws), shape[axis_at] // shards_of).reshape((-1,) + (1,) * (len(shape) - axis_at - 1))

    loudness = one(*pieces[0])
    for cut in pieces[1:]:
        loudness = loudness * one(*cut)
    return loudness


def normal_values(stream_key, extent, deviation, most, cuts=(), held_as=jnp.bfloat16):
    loudness = block_levels(stream_key, extent, cuts, -0.22, 0.18) if cuts else 1.0
    values = jax.random.normal(stream_key, extent, jnp.float32) * deviation * loudness
    return jnp.minimum(jnp.maximum(values, -most), most).astype(held_as)


def setup_inputs(seed: int = 0) -> dict:
    seeds = jax.random.split(jax.random.key(seed), 10)
    return {
        "weight": normal_values(seeds[0], (N_SECTION, MODEL_WIDTH, MODEL_WIDTH), MODEL_WIDTH ** -0.5, 0.078125, ((0, 32), (1, 8), (2, 2))),
        "adapter_down_map": normal_values(seeds[1], (N_SECTION, MODEL_WIDTH, ADAPTER_RANK), MODEL_WIDTH ** -0.5, 0.078125, ((0, 32), (1, 8))),
        "adapter_up_map": normal_values(seeds[2], (N_SECTION, ADAPTER_RANK, MODEL_WIDTH), ADAPTER_RANK ** -0.5, 1.5, ((0, 32), (2, 8))),
        "gain": jnp.clip(1.0 + 0.1 * jax.random.normal(seeds[3], (N_SECTION, MODEL_WIDTH), jnp.float32), 0.5, 1.5),
        "prior_epoch_input": draw_prior_epoch_input(jax.random.fold_in(seeds[9], 71), 0),
        "prior_epoch_output": draw_prior_epoch_output(jax.random.fold_in(seeds[9], 71), 0),
        "initial_step_inputs": normal_values(seeds[6], (N_SECTION, N_DP * TOK, MODEL_WIDTH), 1.0, 6.0, ((0, 32), (1, 2), (2, 8))),
        "initial_step_gradients": normal_values(seeds[7], (N_SECTION, N_DP * TOK, MODEL_WIDTH), 1.0, 6.0, ((0, 32), (1, 2), (2, 8))),
        "sample_numbers": plant(jax.random.randint(seeds[8], (N_SECTION, N_DP, TICKS), 0, SAMPLES), jax.random.fold_in(seeds[8], 1), 0, SAMPLES - 1).astype(jnp.int32),
    }


def encode_delta(values, base):
    delta = values - base.astype(jnp.float32)
    shape = delta.shape
    blocks = delta.reshape(shape[:-1] + (shape[-1] // QBLOCK, QBLOCK))
    scales = (lax.optimization_barrier(jnp.max(jnp.abs(blocks), axis=-1)) + 1e-06).astype(jnp.bfloat16)
    coded = (blocks / scales.astype(jnp.float32)[..., None]).astype(jnp.bfloat16)
    return (coded, scales)

def decode_delta(coded, scales):
    blocks = coded.astype(jnp.float32) * scales.astype(jnp.float32)[..., None]
    return blocks.reshape(coded.shape[:-2] + (coded.shape[-2] * QBLOCK,))

def layer_update(inputs):
    w_layer, a_layer, b_layer, layer_gradient, section_input, g_in, is_last = inputs
    highest = lax.Precision.HIGHEST
    a_wide = a_layer.astype(jnp.float32)
    average_value = lax.optimization_barrier(jnp.mean(section_input, axis=-1, keepdims=True))
    var_val = lax.optimization_barrier(jnp.mean(section_input * section_input, axis=-1, keepdims=True)) - average_value * average_value
    inverse_deviation = lax.rsqrt(var_val + 1e-05)
    centered_scaled_input = (section_input - average_value) * inverse_deviation
    normalized_rows = centered_scaled_input * layer_gradient
    normed_b = normalized_rows.astype(jnp.bfloat16)
    zlow = jnp.dot(normalized_rows, a_wide, precision=highest).astype(jnp.bfloat16)
    out = section_input + jnp.dot(normed_b, w_layer, preferred_element_type=jnp.float32) + jnp.dot(zlow, b_layer, preferred_element_type=jnp.float32)
    bias_gradient = jnp.where(is_last, out.astype(jnp.bfloat16), g_in)
    dz = jnp.dot(bias_gradient, b_layer.T, preferred_element_type=jnp.float32)
    du = jnp.dot(bias_gradient, w_layer.T, preferred_element_type=jnp.float32) + jnp.dot(dz, a_wide.T, precision=highest)
    hidden_gradient = du * layer_gradient
    first_moment = lax.optimization_barrier(jnp.mean(hidden_gradient, axis=-1, keepdims=True))
    second_moment = lax.optimization_barrier(jnp.mean(hidden_gradient * centered_scaled_input, axis=-1, keepdims=True))
    input_gradient = bias_gradient.astype(jnp.float32) + inverse_deviation * (hidden_gradient - first_moment - centered_scaled_input * second_moment)
    first_portion = jnp.dot(normalized_rows.T, dz, precision=highest)
    second_portion = jnp.dot(zlow.T, bias_gradient, preferred_element_type=jnp.float32)
    return (out, input_gradient, first_portion, second_portion)

def reference(weight, adapter_down_map, adapter_up_map, gain, prior_epoch_input, prior_epoch_output, initial_step_inputs, initial_step_gradients, sample_numbers):
    nlayer = weight.shape[0]
    nrep = sample_numbers.shape[1]
    layer_ids = jnp.arange(nlayer)
    replicas = jnp.arange(nrep)
    carry_state_list = initial_step_inputs.astype(jnp.float32)
    gradient_list = initial_step_gradients
    sids = sample_numbers[:, :, 0]
    final_section_flag = layer_ids == nlayer - 1
    acc_a = jnp.zeros((nlayer, MODEL_WIDTH, ADAPTER_RANK), jnp.float32)
    acc_b = jnp.zeros((nlayer, ADAPTER_RANK, MODEL_WIDTH), jnp.float32)
    for tick in range(TICKS):
        output_list, input_gradient_list, first_portion, second_portion = lax.map(layer_update, (weight, adapter_down_map, adapter_up_map, gain, carry_state_list, gradient_list, final_section_flag))
        acc_a = acc_a + first_portion
        acc_b = acc_b + second_portion
        if tick < TICKS - 1:
            base = prior_epoch_output[layer_ids[:, None], replicas[None, :], sids]
            coded, scales = encode_delta(output_list.reshape(nlayer, nrep, TOK, MODEL_WIDTH), base)
            received = decode_delta(coded, scales)
            new_sids = jnp.concatenate([sample_numbers[0:1, :, tick + 1], sids[:-1]], axis=0)
            inbase = prior_epoch_input[layer_ids[:, None], replicas[None, :], new_sids].astype(jnp.float32)
            shifted = jnp.concatenate([jnp.zeros_like(received[:1]), received[:-1]], axis=0)
            carry_state_list = (inbase + shifted).reshape(nlayer, nrep * TOK, MODEL_WIDTH)
            gradient_list = jnp.concatenate([input_gradient_list[1:], jnp.zeros_like(input_gradient_list[:1])], axis=0).astype(jnp.bfloat16)
            sids = new_sids
    denom = jnp.float32(nrep * TOK)
    return ((acc_a / denom).astype(jnp.bfloat16), (acc_b / denom).astype(jnp.bfloat16))
```

```python
import jax
import jax.numpy as jnp
from jax import lax
from jax.sharding import PartitionSpec as P

TICKS = 4
CHIPS = 4
EPS = 1e-05
AXES = ("section", "tensor", "dp")
HIGHEST = lax.Precision.HIGHEST
BF = jnp.bfloat16
F32 = jnp.float32


def flat(section, tensor, dp):
    return (section * 2 * CHIPS + tensor) * 2 + dp


def owner(block, core):
    return 2 * (block % CHIPS) + core, block // CHIPS


def to_owner(array, sections, back):
    route = []
    for s in range(sections):
        for block in range(2 * CHIPS):
            for half in range(2):
                if s - back >= 0:
                    route.append((flat(s, block, half), flat(s - back, *owner(block, half))))
    return lax.ppermute(array, AXES, route)


def to_next(array, sections):
    route = []
    for s in range(sections - 1):
        for block in range(2 * CHIPS):
            for half in range(2):
                route.append((flat(s, *owner(block, half)), flat(s + 1, block, half)))
    return lax.ppermute(array, AXES, route)


def swap_cores(array):
    return lax.ppermute(array, "tensor", [(i, i ^ 1) for i in range(2 * CHIPS)])


def over_chips(array):
    groups = [[2 * i for i in range(CHIPS)], [2 * i + 1 for i in range(CHIPS)]]
    return lax.all_to_all(array, "tensor", 0, 0, axis_index_groups=groups)


def split(values, parts=3):
    out = []
    for _ in range(parts):
        high = lax.reduce_precision(values, 8, 7)
        out.append(high.astype(BF))
        values = values - high
    return jnp.concatenate(out, axis=-1)


def join(pieces, width, parts=3):
    total = pieces[..., :width].astype(F32)
    for i in range(1, parts):
        total = total + pieces[..., i * width : (i + 1) * width].astype(F32)
    return total


def pad_to(array, width):
    return jnp.pad(array, [(0, 0)] * (array.ndim - 1) + [(0, width - array.shape[-1])])


def dot(a, b, **kw):
    return jnp.dot(a, b, preferred_element_type=F32, **kw)


def dot_t(a, b, **kw):
    return lax.dot_general(a, b, (((1,), (1,)), ((), ())), preferred_element_type=F32, **kw)


def t_dot(a, b, **kw):
    return lax.dot_general(a, b, (((0,), (0,)), ((), ())), preferred_element_type=F32, **kw)


def on_device(
    weight,
    adapter_down_map,
    adapter_up_map,
    gain,
    prior_epoch_input,
    prior_epoch_output,
    initial_step_inputs,
    initial_step_gradients,
    sample_numbers,
):
    del prior_epoch_output
    w = weight[0]
    down = adapter_down_map[0].astype(F32)
    gains = gain[0]
    order = sample_numbers[0, 0]
    sections = lax.axis_size("section")
    section = lax.axis_index("section")
    tensor = lax.axis_index("tensor")
    half = lax.axis_index("dp")
    core = tensor % 2
    is_first = section == 0
    is_last = section == sections - 1
    toks, feats = initial_step_inputs.shape[1:]
    rank = down.shape[1]
    width = feats * 2 * CHIPS
    rows = 2 * toks

    def both_replicas(mine, theirs):
        return jnp.where(
            half == 0,
            jnp.concatenate([mine, theirs], axis=-2),
            jnp.concatenate([theirs, mine], axis=-2),
        )

    mine = initial_step_inputs[0]
    x = both_replicas(mine, lax.ppermute(mine, "dp", [(0, 1), (1, 0)]))
    given = to_owner(
        jnp.concatenate([initial_step_gradients[0], adapter_up_map[0]], axis=0), sections, 0
    )
    zeros = jnp.zeros((toks, feats), BF)
    grad_part = jnp.where(
        core == 0,
        jnp.concatenate([given[:toks], zeros]),
        jnp.concatenate([zeros, given[:toks]]),
    )
    up = given[toks:]
    chosen = jnp.take(prior_epoch_input[0, 0], order[1:], axis=0)
    theirs = lax.ppermute(
        chosen,
        AXES,
        [(flat(0, t, d), flat(0, t, 1 - d)) for t in range(2 * CHIPS) for d in range(2)],
    )
    first_x = both_replicas(chosen, theirs)

    n_small = rank + 2 + rank + 2
    small_width = 128
    acc_down = jnp.zeros((rank, feats), F32)
    acc_up = jnp.zeros((rank, feats), F32)
    before = None
    dots = None
    for tick in range(TICKS):
        wide = x.astype(F32)
        mid = jnp.mean(wide, axis=1, keepdims=True)
        centered = wide - mid
        square = jnp.sum(centered * centered, axis=1, keepdims=True)
        scaled = centered * gains
        low_part = dot(scaled, down, precision=HIGHEST)
        left = scaled.astype(BF)
        small = [mid, square, low_part]
        x_owned = to_owner(x, sections, 0)
        if tick == 0:
            gain_rows = split(gains[None, :]).reshape(3, feats)
            gain_low = dot(gains[None, :], down, precision=HIGHEST)
            product = dot(jnp.concatenate([left, pad_rows(gain_rows, 16)]), w)
            gain_w = jnp.sum(product[rows:], axis=0, keepdims=True)
            gain_w = split(gain_w.reshape(CHIPS, 1, feats)).reshape(CHIPS, 3, feats)
            gain_low = split(gain_low).reshape(3, rank)
            tail = jnp.concatenate(
                [gain_w, jnp.broadcast_to(pad_to(gain_low, small_width), (CHIPS, 3, small_width))],
                axis=2,
            )
            product = product[:rows]
        else:
            product = dot(left, w)
        product = product.astype(BF).reshape(rows, CHIPS, feats).transpose(1, 0, 2)
        if tick:
            small.append(dots)
            extra = [jnp.broadcast_to(grad_part, (CHIPS, rows, feats))]
        else:
            extra = []
        small = pad_to(split(jnp.concatenate(small, axis=1)), small_width)
        parcel = jnp.concatenate(
            [product] + extra + [jnp.broadcast_to(small, (CHIPS, rows, small_width))], axis=2
        )
        if tick == 0:
            parcel = jnp.concatenate([parcel, jnp.pad(tail, ((0, 0), (0, 13), (0, 0)))], axis=1)
        got = over_chips(parcel)
        if tick == 0:
            tail = got[:, rows : rows + 3].astype(F32).sum(1)
            got = got[:, :rows]
        summed = jnp.sum(got[:, :, :feats].astype(F32), axis=0).astype(BF)
        n_now = 2 + rank + (rank + 2 if tick else 0)
        values = join(got[:, :, -small_width:], n_now)
        packed = [values[:, :, 0].T, values[:, :, 1].T, jnp.sum(values[:, :, 2:], axis=0)]
        packed = jnp.concatenate(packed, axis=1)
        n_packed = packed.shape[1]
        parts = [summed, pad_to(split(packed), small_width)]
        if tick:
            parts.append(got[:, :, feats : 2 * feats].transpose(1, 0, 2).reshape(rows, CHIPS * feats))
        if tick == 0:
            extra_rows = jnp.concatenate(
                [
                    split(tail[:, :feats].reshape(1, -1)).reshape(3 * CHIPS, feats),
                    jnp.broadcast_to(
                        pad_to(split(tail[:, feats : feats + rank]), small_width)[None],
                        (3, CHIPS, small_width),
                    ).reshape(3 * CHIPS, small_width),
                ],
                axis=1,
            )
            parts = [jnp.concatenate([jnp.concatenate(parts, 1), pad_rows(extra_rows, 16)], 0)]
        other = swap_cores(jnp.concatenate(parts, axis=1))
        if tick == 0:
            tail_other = other[rows:]
            gain_w = jnp.concatenate(
                [
                    tail[:, :feats],
                    jnp.sum(
                        tail_other[: 3 * CHIPS, :feats].astype(F32).reshape(3, CHIPS, feats), axis=0
                    ),
                ]
            )
            gain_low = jnp.concatenate(
                [
                    tail[:, feats : feats + rank],
                    join(tail_other[:CHIPS, feats:], rank),
                ]
            )
            gain_w_all = jnp.sum(gain_w, axis=0, keepdims=True)
            gain_low_all = jnp.sum(gain_low, axis=0, keepdims=True)
            other = other[:rows]
        packed_other = join(other[:, feats : feats + small_width], n_packed)
        both = packed + packed_other
        mids = jnp.concatenate([packed[:, :CHIPS], packed_other[:, :CHIPS]], axis=1)
        mean = jnp.sum(mids, axis=1, keepdims=True) / (2 * CHIPS)
        off = mids - mean
        var = (
            jnp.sum(both[:, CHIPS : 2 * CHIPS], axis=1, keepdims=True)
            + feats * jnp.sum(off * off, axis=1, keepdims=True)
        ) / width
        inv = lax.rsqrt(var + EPS)
        mixed = inv * (
            summed.astype(F32)
            + other[:, :feats].astype(F32)
            + dot(off, gain_w, precision=HIGHEST)
        )
        low = inv * (
            both[:, 2 * CHIPS : 2 * CHIPS + rank] + dot(off, gain_low, precision=HIGHEST)
        )
        low_b = low.astype(BF)
        output = (x_owned.astype(F32) + mixed + dot(low_b, up)).astype(BF)
        if tick < TICKS - 1:
            arrived = to_next(output, sections)
        now = (x, mean, inv, low)
        if tick:
            x_was, mean_was, inv_was, low_was = before
            low_grad = both[:, 2 * CHIPS + rank : 2 * CHIPS + 2 * rank]
            first = both[:, 2 * CHIPS + 2 * rank : 2 * CHIPS + 2 * rank + 1]
            second = both[:, 2 * CHIPS + 2 * rank + 1 : 2 * CHIPS + 2 * rank + 2]
            first = (first + jnp.sum(low_grad * gain_low_all, axis=1, keepdims=True)) / width
            second = (second + jnp.sum(low_grad * low_was, axis=1, keepdims=True)) / width
            grads = (
                parts[2].astype(F32) + other[:, feats + small_width :].astype(F32)
            ).astype(BF)
            xhat = (x_was.astype(F32) - mean_was) * inv_was
            acc_down = acc_down + t_dot(low_grad, xhat * gains, precision=HIGHEST)
            grad_norm = dot_t(grads, w) + dot_t(low_grad, down, precision=HIGHEST)
            here = lax.dynamic_slice_in_dim(grads, (tensor % CHIPS) * feats, feats, axis=1)
            here = jnp.where(tensor // CHIPS == half, here.astype(F32), 0.0)
            grad_x = here + inv_was * (grad_norm * gains - first - xhat * second)
            grad_part = to_owner(grad_x.astype(BF), sections, 1)
        grad_part = jnp.where(
            is_last, jnp.where(core == 0, output, jnp.zeros_like(output)), grad_part
        )
        low_grad_part = dot_t(grad_part, up)
        acc_up = acc_up + t_dot(low_b, grad_part)
        if tick < TICKS - 1:
            wide_grad = grad_part.astype(F32)
            dots = jnp.concatenate(
                [
                    low_grad_part,
                    jnp.sum(wide_grad * gain_w_all, axis=1, keepdims=True),
                    jnp.sum(wide_grad * mixed, axis=1, keepdims=True),
                ],
                axis=1,
            )
            x = jnp.where(is_first, first_x[tick], arrived)
        before = now

    acc_other = lax.ppermute(acc_down, "dp", [(0, 1), (1, 0)])
    turned = pad_to(low_grad_part.T, 128)
    parcel = jnp.concatenate([acc_up.astype(BF), split(turned)], axis=1)
    got = lax.all_to_all(
        jnp.broadcast_to(parcel, (4 * CHIPS,) + parcel.shape), ("tensor", "dp"), 0, 0
    )
    low_grad = jnp.sum(join(got[:, :, feats:], 128), axis=0)[:, :rows]
    x_was, mean_was, inv_was, _ = before
    normed = (x_was.astype(F32) - mean_was) * inv_was * gains
    total_down = acc_down + acc_other + dot(low_grad, normed, precision=HIGHEST)
    block = 2 * (2 * (tensor % CHIPS)) + tensor // CHIPS
    total_up = lax.dynamic_index_in_dim(got, block, 0, False)[:, :feats].astype(F32)
    total_up = total_up + lax.dynamic_index_in_dim(got, block + 2, 0, False)[:, :feats].astype(F32)
    return ((total_down / rows).T.astype(BF)[None], (total_up / rows).astype(BF)[None])


def pad_rows(array, count):
    return jnp.pad(array, ((0, count - array.shape[0]), (0, 0)))


def solution(mesh):
    in_specs = (
        P("section", "tensor", "dp"),
        P("section", "tensor", None),
        P("section", None, "tensor"),
        P("section", "tensor"),
        P("section", "dp", None, None, "tensor"),
        P("section", "dp", None, None, "tensor"),
        P("section", "dp", "tensor"),
        P("section", "dp", "tensor"),
        P("section", "dp", None),
    )
    out_specs = (P("section", "tensor", None), P("section", None, "tensor"))
    return jax.shard_map(
        on_device, mesh=mesh, in_specs=in_specs, out_specs=out_specs, check_vma=False
    )
```

```python
import functools

import jax
import jax.numpy as jnp
from jax import lax
from jax.experimental import pallas as pl
from jax.experimental.pallas import tpu as pltpu
from jax.sharding import PartitionSpec as P

TICKS = 4
CHIPS = 4
EPS = 1e-05
AXES = ("section", "tensor", "dp")
HIGHEST = lax.Precision.HIGHEST
BF = jnp.bfloat16
F32 = jnp.float32

LANES = 128
SQUARE = 8
LOW = 16
GRAD = 32
FIRST = 48
SECOND = 49


def flat(section, tensor, dp):
    return (section * 2 * CHIPS + tensor) * 2 + dp


def owner(block, core):
    return 2 * (block % CHIPS) + core, block // CHIPS


def to_owner(array, sections, back):
    route = []
    for s in range(sections):
        for block in range(2 * CHIPS):
            for half in range(2):
                if s - back >= 0:
                    route.append((flat(s, block, half), flat(s - back, *owner(block, half))))
    return lax.ppermute(array, AXES, route)


def to_next(array, sections):
    route = []
    for s in range(sections - 1):
        for block in range(2 * CHIPS):
            for half in range(2):
                route.append((flat(s, *owner(block, half)), flat(s + 1, block, half)))
    return lax.ppermute(array, AXES, route)


def swap_cores(array):
    return lax.ppermute(array, "tensor", [(i, i ^ 1) for i in range(2 * CHIPS)])


def over_chips(array):
    groups = [[2 * i for i in range(CHIPS)], [2 * i + 1 for i in range(CHIPS)]]
    return lax.all_to_all(array, "tensor", 0, 0, axis_index_groups=groups)


def dot(a, b, **kw):
    return jnp.dot(a, b, preferred_element_type=F32, **kw)


def dot_t(a, b, **kw):
    return lax.dot_general(a, b, (((1,), (1,)), ((), ())), preferred_element_type=F32, **kw)


def t_dot(a, b, **kw):
    return lax.dot_general(a, b, (((0,), (0,)), ((), ())), preferred_element_type=F32, **kw)


def lane(rows):
    return lax.broadcasted_iota(jnp.int32, (rows, LANES), 1)


def between(values, low, high):
    at = lane(values.shape[0])
    return jnp.where((at >= low) & (at < high), values, 0.0)


def pick(values, low, high):
    return jnp.sum(between(values, low, high), axis=1, keepdims=True)


def split(values):
    high = values.astype(BF).astype(F32)
    rest = pltpu.roll(values - high, LANES // 2, 1)
    return jnp.where(lane(values.shape[0]) < LANES // 2, high, rest).astype(BF)


def join(halves):
    wide = halves.astype(F32)
    return wide + pltpu.roll(wide, LANES // 2, 1)


def call(kernel, out, *args, scalars=(), vmem=24):
    return pl.pallas_call(
        kernel,
        out_shape=out,
        in_specs=[pl.BlockSpec(memory_space=pltpu.SMEM)] * len(scalars)
        + [pl.BlockSpec(memory_space=pltpu.VMEM)] * len(args),
        out_specs=jax.tree.map(lambda _: pl.BlockSpec(memory_space=pltpu.VMEM), out),
        compiler_params=pltpu.CompilerParams(vmem_limit_bytes=vmem * 2**20),
    )(*scalars, *args)


def shape(*dims, dtype=F32):
    return jax.ShapeDtypeStruct(dims, dtype)


def forward_kernel(start, flags, arrived, given, gains, w, down, x_out, product, small):
    place = flags[1]
    if start:
        x = given[...]
    else:
        x = jnp.where(flags[0] == 1, given[...], arrived[...])
    x_out[...] = x
    rows, feats = x.shape
    wide = x.astype(F32)
    mid = jnp.sum(wide, axis=1, keepdims=True) / feats
    centered = wide - mid
    square = jnp.sum(centered * centered, axis=1, keepdims=True)
    scaled = centered * gains[...]
    at = lane(rows)
    low = dot(scaled, down[...], precision=HIGHEST)
    low = jnp.where(at == place, mid, low)
    small[0:rows] = jnp.where(at == SQUARE + place, square, low)
    left = scaled.astype(BF)
    if start:
        row = lax.broadcasted_iota(jnp.int32, (2 * CHIPS, feats), 0)
        gain_rows = jnp.where(row == place, gains[...], 0.0)
        high = gain_rows.astype(BF).astype(F32)
        left = jnp.concatenate([left, jnp.concatenate([high, gain_rows - high]).astype(BF)])
        small[rows:] = jnp.concatenate(
            [dot(gain_rows, down[...], precision=HIGHEST), jnp.zeros((2 * CHIPS, LANES), F32)]
        )
    for j in range(CHIPS):
        part = dot(left, w[:, j * feats : (j + 1) * feats])
        if start:
            tail = part[rows : rows + 2 * CHIPS] + part[rows + 2 * CHIPS :]
            high = tail.astype(BF).astype(F32)
            part = jnp.concatenate([part[:rows], high, tail - high])
        product[j] = part.astype(BF)


def pack_kernel(start, flags, product, small, *refs):
    rows, feats = product.shape[1:]
    values = small[...]
    if start:
        parcel = refs[-1]
        columns = feats
    else:
        arrived, output, up, gain_w, mixed, grad_out, parcel = refs
        columns = 2 * feats
        kept = jnp.where(flags[1] == 0, output[...], jnp.zeros((rows, feats), BF))
        grad = jnp.where(flags[0] == 1, kept, arrived[...])
        grad_out[...] = grad
        wide = grad.astype(F32)
        first = jnp.sum(wide * jnp.sum(gain_w[...], axis=0, keepdims=True), axis=1, keepdims=True)
        second = jnp.sum(wide * mixed[...], axis=1, keepdims=True)
        at = lane(rows)
        values = values + pltpu.roll(dot_t(grad, up[...]), GRAD - LOW, 1)
        values = jnp.where(at == FIRST, first, values)
        values = jnp.where(at == SECOND, second, values)
        for j in range(CHIPS):
            parcel[j, :, feats : 2 * feats] = grad
    halves = split(values)
    for j in range(CHIPS):
        parcel[j, :, :feats] = product[j]
        parcel[j, :, columns:] = halves


def gather_kernel(start, got, out):
    feats = (got.shape[2] - LANES) // (1 if start else 2)
    total = got[0, :, :feats].astype(F32)
    values = join(got[0, :, -LANES:])
    for j in range(1, CHIPS):
        total = total + got[j, :, :feats].astype(F32)
        values = values + join(got[j, :, -LANES:])
    out[:, :feats] = total.astype(BF)
    out[:, feats : feats + LANES] = split(values)
    if not start:
        for j in range(CHIPS):
            at = feats + LANES + j * feats
            out[:, at : at + feats] = got[j, :, feats : 2 * feats]


def output_kernel(start, mine, theirs, x, up, *refs):
    rows, feats = x.shape
    if start:
        gain_w, gain_low, output, mixed, stats, sums = refs
        tail = mine[rows:, :feats].astype(F32) + theirs[rows:, :feats].astype(F32)
        gain_w[...] = tail[: 2 * CHIPS] + tail[2 * CHIPS :]
        tail = join(mine[rows:, feats:]) + join(theirs[rows:, feats:])
        gain_low[...] = between(tail[: 2 * CHIPS], LOW, GRAD)
    else:
        gain_w, gain_low, output, mixed, stats, sums = refs
    values = join(mine[:rows, feats : feats + LANES]) + join(theirs[:rows, feats : feats + LANES])
    values = between(values, 0, LANES // 2)
    sums[...] = values
    at = lane(rows)
    width = feats * 2 * CHIPS
    mean = pick(values, 0, SQUARE) / (2 * CHIPS)
    off = jnp.where(at < 2 * CHIPS, values - mean, 0.0)
    square = pick(values, SQUARE, LOW) + feats * jnp.sum(off * off, axis=1, keepdims=True)
    inv = lax.rsqrt(square / width + EPS)
    total = mine[:rows, :feats].astype(F32) + theirs[:rows, :feats].astype(F32)
    low = values
    for j in range(2 * CHIPS):
        total = total + off[:, j : j + 1] * gain_w[j : j + 1, :]
        low = low + off[:, j : j + 1] * gain_low[j : j + 1, :]
    total = inv * total
    low = between(inv * low, LOW, GRAD)
    mixed[...] = total
    stats[...] = jnp.where(at == 0, mean, jnp.where(at == 1, inv, low))
    output[...] = (x[...].astype(F32) + total + dot(low.astype(BF), up[...])).astype(BF)


def backward_kernel(flags, mine, theirs, sums, x, stats, gains, gain_low, w, down, grad_out):
    rows, feats = x.shape
    width = feats * 2 * CHIPS
    values = sums[...]
    low_grad = pltpu.roll(between(values, GRAD, FIRST), LANES - (GRAD - LOW), 1)
    low = between(stats[...], LOW, GRAD)
    low_all = jnp.sum(gain_low[...], axis=0, keepdims=True)
    first = pick(values, FIRST, FIRST + 1) + jnp.sum(low_grad * low_all, axis=1, keepdims=True)
    second = pick(values, SECOND, SECOND + 1) + jnp.sum(low_grad * low, axis=1, keepdims=True)
    mean, inv = pick(stats[...], 0, 1), pick(stats[...], 1, 2)
    xhat = (x[...].astype(F32) - mean) * inv
    grad_norm = dot_t(low_grad, down[...], precision=HIGHEST)
    here = jnp.zeros((rows, feats), F32)
    for j in range(CHIPS):
        at = feats + LANES + j * feats
        grad = mine[:, at : at + feats].astype(F32) + theirs[:, at : at + feats].astype(F32)
        grad = grad.astype(BF)
        grad_norm = grad_norm + dot_t(grad, w[:, j * feats : (j + 1) * feats])
        here = here + jnp.where(flags[0] == j, grad.astype(F32), 0.0)
    grad_x = here + inv * (grad_norm * gains[...] - first / width - xhat * (second / width))
    grad_out[...] = grad_x.astype(BF)


def on_device(
    weight,
    adapter_down_map,
    adapter_up_map,
    gain,
    prior_epoch_input,
    prior_epoch_output,
    initial_step_inputs,
    initial_step_gradients,
    sample_numbers,
):
    del prior_epoch_output
    w = weight[0]
    gains = gain
    order = sample_numbers[0, 0]
    sections = lax.axis_size("section")
    section = lax.axis_index("section")
    tensor = lax.axis_index("tensor")
    half = lax.axis_index("dp")
    core = tensor % 2
    is_first = section == 0
    is_last = section == sections - 1
    toks, feats = initial_step_inputs.shape[1:]
    rank = adapter_up_map.shape[1]
    rows = 2 * toks
    down = jnp.pad(adapter_down_map[0].astype(F32), ((0, 0), (LOW, LANES - LOW - rank)))
    flags_forward = jnp.stack([is_first, tensor]).astype(jnp.int32)
    flags_pack = jnp.stack([is_last, core]).astype(jnp.int32)
    flags_backward = jnp.where(tensor // CHIPS == half, tensor % CHIPS, -1).astype(jnp.int32)[None]

    def both_replicas(mine, theirs):
        return jnp.where(
            half == 0,
            jnp.concatenate([mine, theirs], axis=-2),
            jnp.concatenate([theirs, mine], axis=-2),
        )

    mine = initial_step_inputs[0]
    x = both_replicas(mine, lax.ppermute(mine, "dp", [(0, 1), (1, 0)]))
    given = to_owner(
        jnp.concatenate([initial_step_gradients[0], adapter_up_map[0]], axis=0), sections, 0
    )
    zeros = jnp.zeros((toks, feats), BF)
    grad_arrived = jnp.where(
        core == 0,
        jnp.concatenate([given[:toks], zeros]),
        jnp.concatenate([zeros, given[:toks]]),
    )
    up = jnp.pad(given[toks:], ((LOW, LANES - LOW - rank), (0, 0)))
    chosen = jnp.take(prior_epoch_input[0, 0], order[1:], axis=0)
    theirs = lax.ppermute(
        chosen,
        AXES,
        [(flat(0, t, d), flat(0, t, 1 - d)) for t in range(2 * CHIPS) for d in range(2)],
    )
    first_x = both_replicas(chosen, theirs)

    acc_down = jnp.zeros((LANES, feats), F32)
    acc_up = jnp.zeros((rank, feats), F32)
    block = shape(rows, feats, dtype=BF)
    values = shape(rows, LANES)
    arrived = x
    before = None
    for tick in range(TICKS):
        start = tick == 0
        more = 4 * CHIPS if start else 0
        x, product, small = call(
            functools.partial(forward_kernel, start),
            [block, shape(CHIPS, rows + more, feats, dtype=BF), shape(rows + more, LANES)],
            arrived,
            x if start else first_x[tick - 1],
            gains,
            w,
            down,
            scalars=(flags_forward,),
        )
        x_owned = to_owner(x, sections, 0)
        columns = (1 if start else 2) * feats + LANES
        parcel = shape(CHIPS, rows + more, columns, dtype=BF)
        if start:
            parcel = call(
                functools.partial(pack_kernel, start), parcel, product, small, scalars=(flags_pack,)
            )
        else:
            grad_part, parcel = call(
                functools.partial(pack_kernel, start),
                [block, parcel],
                product,
                small,
                grad_arrived,
                output,
                up,
                gain_w,
                mixed,
                scalars=(flags_pack,),
            )
            acc_up = acc_up + t_dot(low_b, grad_part)
        got = over_chips(parcel)
        own = call(
            functools.partial(gather_kernel, start),
            shape(rows + more, feats + LANES + (0 if start else CHIPS * feats), dtype=BF),
            got,
        )
        other = swap_cores(own)
        out = [block, shape(rows, feats), values, values]
        if start:
            gain_w, gain_low, output, mixed, stats, sums = call(
                functools.partial(output_kernel, start),
                [shape(2 * CHIPS, feats), shape(2 * CHIPS, LANES)] + out,
                own,
                other,
                x_owned,
                up,
            )
        else:
            output, mixed, stats, sums = call(
                functools.partial(output_kernel, start),
                out,
                own,
                other,
                x_owned,
                up,
                gain_w,
                gain_low,
            )
        if tick < TICKS - 1:
            arrived = to_next(output, sections)
        low_b = stats[:, LOW : LOW + rank].astype(BF)
        if not start:
            x_was, stats_was = before
            grad_x = call(
                backward_kernel,
                block,
                own,
                other,
                sums,
                x_was,
                stats_was,
                gains,
                gain_low,
                w,
                down,
                scalars=(flags_backward,),
            )
            grad_arrived = to_owner(grad_x, sections, 1)
            normed = (x_was.astype(F32) - stats_was[:, 0:1]) * stats_was[:, 1:2] * gains
            acc_down = acc_down + t_dot(sums, normed, precision=HIGHEST)
        before = (x, stats)

    acc_down = acc_down[GRAD : GRAD + rank]
    acc_other = lax.ppermute(acc_down, "dp", [(0, 1), (1, 0)])
    kept = jnp.where(core == 0, output, jnp.zeros_like(output))
    grad_part = jnp.where(is_last, kept, grad_arrived)
    acc_up = acc_up + t_dot(low_b, grad_part)
    turned = jnp.pad(dot_t(up[LOW : LOW + rank], grad_part), ((0, 0), (0, LANES - rows)))
    high = lax.reduce_precision(turned, 8, 7)
    parcel = jnp.concatenate([acc_up.astype(BF), high.astype(BF), (turned - high).astype(BF)], 1)
    got = lax.all_to_all(
        jnp.broadcast_to(parcel, (4 * CHIPS,) + parcel.shape), ("tensor", "dp"), 0, 0
    )
    turned = jnp.sum(got[:, :, feats:].astype(F32), axis=0)
    low_grad = (turned[:, :LANES] + turned[:, LANES:])[:, :rows]
    normed = (x.astype(F32) - stats[:, 0:1]) * stats[:, 1:2] * gains
    total_down = acc_down + acc_other + dot(low_grad, normed, precision=HIGHEST)
    at = 2 * (2 * (tensor % CHIPS)) + tensor // CHIPS
    total_up = lax.dynamic_index_in_dim(got, at, 0, False)[:, :feats].astype(F32)
    total_up = total_up + lax.dynamic_index_in_dim(got, at + 2, 0, False)[:, :feats].astype(F32)
    return ((total_down / rows).T.astype(BF)[None], (total_up / rows).astype(BF)[None])


def solution(mesh):
    in_specs = (
        P("section", "tensor", "dp"),
        P("section", "tensor", None),
        P("section", None, "tensor"),
        P("section", "tensor"),
        P("section", "dp", None, None, "tensor"),
        P("section", "dp", None, None, "tensor"),
        P("section", "dp", "tensor"),
        P("section", "dp", "tensor"),
        P("section", "dp", None),
    )
    out_specs = (P("section", "tensor", None), P("section", None, "tensor"))
    return jax.shard_map(
        on_device, mesh=mesh, in_specs=in_specs, out_specs=out_specs, check_vma=False
    )
```

```python
import functools

import jax
import jax.numpy as jnp
from jax import lax
from jax.experimental import pallas as pl
from jax.experimental.pallas import tpu as pltpu
from jax.sharding import PartitionSpec as P

TICKS = 4
CHIPS = 4
EPS = 1e-05
AXES = ("section", "tensor", "dp")
HIGHEST = lax.Precision.HIGHEST
BF = jnp.bfloat16
F32 = jnp.float32

LANES = 128
SQUARE = 8
LOW = 16
GRAD = 32
FIRST = 48
SECOND = 49


def flat(section, tensor, dp):
    return (section * 2 * CHIPS + tensor) * 2 + dp


def owner(block, core):
    return 2 * (block % CHIPS) + core, block // CHIPS


def to_owner(array, sections, back):
    route = []
    for s in range(sections):
        for block in range(2 * CHIPS):
            for half in range(2):
                if s - back >= 0:
                    route.append((flat(s, block, half), flat(s - back, *owner(block, half))))
    return lax.ppermute(array, AXES, route)


def to_next(array, sections):
    route = []
    for s in range(sections - 1):
        for block in range(2 * CHIPS):
            for half in range(2):
                route.append((flat(s, *owner(block, half)), flat(s + 1, block, half)))
    return lax.ppermute(array, AXES, route)


def swap_cores(array):
    return lax.ppermute(array, "tensor", [(i, i ^ 1) for i in range(2 * CHIPS)])


def over_chips(array):
    groups = [[2 * i for i in range(CHIPS)], [2 * i + 1 for i in range(CHIPS)]]
    return lax.all_to_all(array, "tensor", 0, 0, axis_index_groups=groups)


def dot(a, b, **kw):
    return jnp.dot(a, b, preferred_element_type=F32, **kw)


def dot_t(a, b, **kw):
    return lax.dot_general(a, b, (((1,), (1,)), ((), ())), preferred_element_type=F32, **kw)


def t_dot(a, b, **kw):
    return lax.dot_general(a, b, (((0,), (0,)), ((), ())), preferred_element_type=F32, **kw)


def lane(rows):
    return lax.broadcasted_iota(jnp.int32, (rows, LANES), 1)


def between(values, low, high):
    at = lane(values.shape[0])
    return jnp.where((at >= low) & (at < high), values, 0.0)


def pick(values, low, high):
    return jnp.sum(between(values, low, high), axis=1, keepdims=True)


def split(values):
    high = values.astype(BF).astype(F32)
    rest = pltpu.roll(values - high, LANES // 2, 1)
    return jnp.where(lane(values.shape[0]) < LANES // 2, high, rest).astype(BF)


def join(halves):
    wide = halves.astype(F32)
    return wide + pltpu.roll(wide, LANES // 2, 1)


def call(kernel, out, *args, scalars=(), vmem=16):
    return pl.pallas_call(
        kernel,
        out_shape=out,
        in_specs=[pl.BlockSpec(memory_space=pltpu.SMEM)] * len(scalars)
        + [pl.BlockSpec(memory_space=pltpu.VMEM)] * len(args),
        out_specs=jax.tree.map(lambda _: pl.BlockSpec(memory_space=pltpu.VMEM), out),
        compiler_params=pltpu.CompilerParams(vmem_limit_bytes=vmem * 2**20),
    )(*scalars, *args)


def shape(*dims, dtype=F32):
    return jax.ShapeDtypeStruct(dims, dtype)


FIRST_SECTION, TENSOR, LAST_SECTION, CORE, OWN_BLOCK, REPLICA, ORDER = range(7)


def replicas(flags, mine, theirs):
    half = flags[REPLICA] == 0
    return jnp.concatenate([jnp.where(half, mine, theirs), jnp.where(half, theirs, mine)])


def prepare_kernel(flags, grads, up, stored, packed, chosen):
    toks = grads.shape[0]
    packed[:toks] = grads[...]
    packed[toks:] = up[...]
    for j in range(TICKS - 1):
        chosen[j] = jnp.where(flags[ORDER + j] == 0, stored[0], stored[1])


def forward_kernel(start, flags, *refs):
    place = flags[TENSOR]
    if start:
        mine, theirs, gains, w, down_rows, x_out, product, small, down = refs
        x = replicas(flags, mine[...], theirs[...])
        rank, feats = down_rows.shape
        down[:LOW] = jnp.zeros((LOW, feats), F32)
        down[LOW : LOW + rank] = down_rows[...].astype(F32)
        down[LOW + rank :] = jnp.zeros((LANES - LOW - rank, feats), F32)
    else:
        tick, arrived, mine, theirs, gains, w, down, x_out, product, small = refs
        given = replicas(flags, mine[tick - 1], theirs[tick - 1])
        x = jnp.where(flags[FIRST_SECTION] == 1, given, arrived[...])
    x_out[...] = x
    rows, feats = x.shape
    wide = x.astype(F32)
    mid = jnp.sum(wide, axis=1, keepdims=True) / feats
    centered = wide - mid
    square = jnp.sum(centered * centered, axis=1, keepdims=True)
    scaled = centered * gains[...]
    at = lane(rows)
    low = dot_t(scaled, down[...], precision=HIGHEST)
    low = jnp.where(at == place, mid, low)
    small[0:rows] = jnp.where(at == SQUARE + place, square, low)
    left = scaled.astype(BF)
    if start:
        row = lax.broadcasted_iota(jnp.int32, (2 * CHIPS, feats), 0)
        gain_rows = jnp.where(row == place, gains[...], 0.0)
        high = gain_rows.astype(BF).astype(F32)
        left = jnp.concatenate([left, jnp.concatenate([high, gain_rows - high]).astype(BF)])
        small[rows:] = jnp.concatenate(
            [dot_t(gain_rows, down[...], precision=HIGHEST), jnp.zeros((2 * CHIPS, LANES), F32)]
        )
    for j in range(CHIPS):
        part = dot(left, w[:, j * feats : (j + 1) * feats])
        if start:
            tail = part[rows : rows + 2 * CHIPS] + part[rows + 2 * CHIPS :]
            high = tail.astype(BF).astype(F32)
            part = jnp.concatenate([part[:rows], high, tail - high])
        product[j] = part.astype(BF)


def chosen_grad(flags, arrived, output):
    kept = jnp.where(flags[CORE] == 0, output[...], jnp.zeros(output.shape, BF))
    return jnp.where(flags[LAST_SECTION] == 1, kept, arrived[...])


def pack_kernel(start, flags, product, small, x_owned, *refs):
    rows, feats = product.shape[1:]
    values = small[...]
    if start:
        given, theirs, parcel, up, grad_out = refs
        columns = feats
        toks = theirs.shape[1]
        rank = given.shape[0] - toks
        up[:LOW] = jnp.zeros((LOW, feats), BF)
        up[LOW : LOW + rank] = given[toks:]
        up[LOW + rank :] = jnp.zeros((LANES - LOW - rank, feats), BF)
        zeros = jnp.zeros((toks, feats), BF)
        grad_out[:toks] = jnp.where(flags[CORE] == 0, given[:toks], zeros)
        grad_out[toks:] = jnp.where(flags[CORE] == 0, zeros, given[:toks])
    else:
        arrived, output, up, gain_w, mixed, parcel, grad_out = refs
        columns = 2 * feats
        grad = chosen_grad(flags, arrived, output)
        grad_out[...] = grad
        wide = grad.astype(F32)
        first = jnp.sum(wide * jnp.sum(gain_w[...], axis=0, keepdims=True), axis=1, keepdims=True)
        second = jnp.sum(wide * mixed[...], axis=1, keepdims=True)
        at = lane(rows)
        values = values + pltpu.roll(dot_t(grad, up[...]), GRAD - LOW, 1)
        values = jnp.where(at == FIRST, first, values)
        values = jnp.where(at == SECOND, second, values)
        for j in range(CHIPS):
            parcel[j, :, feats : 2 * feats] = grad
    halves = split(values)
    for j in range(CHIPS):
        parcel[j, :, :feats] = product[j]
        parcel[j, :, columns:] = halves


def gather_kernel(start, got, out):
    feats = (got.shape[2] - LANES) // (1 if start else 2)
    total = got[0, :, :feats].astype(F32)
    values = join(got[0, :, -LANES:])
    for j in range(1, CHIPS):
        total = total + got[j, :, :feats].astype(F32)
        values = values + join(got[j, :, -LANES:])
    out[:, :feats] = total.astype(BF)
    out[:, feats : feats + LANES] = split(values)
    if not start:
        for j in range(CHIPS):
            at = feats + LANES + j * feats
            out[:, at : at + feats] = got[j, :, feats : 2 * feats]


def output_kernel(start, mine, theirs, x, up, gain_w, gain_low, output, mixed, stats, sums):
    rows, feats = x.shape
    if start:
        tail = mine[rows:, :feats].astype(F32) + theirs[rows:, :feats].astype(F32)
        gain_w[...] = tail[: 2 * CHIPS] + tail[2 * CHIPS :]
        tail = join(mine[rows:, feats:]) + join(theirs[rows:, feats:])
        gain_low[...] = between(tail[: 2 * CHIPS], LOW, GRAD)
    values = join(mine[:rows, feats : feats + LANES]) + join(theirs[:rows, feats : feats + LANES])
    values = between(values, 0, LANES // 2)
    sums[...] = values
    at = lane(rows)
    width = feats * 2 * CHIPS
    mean = pick(values, 0, SQUARE) / (2 * CHIPS)
    off = jnp.where(at < 2 * CHIPS, values - mean, 0.0)
    square = pick(values, SQUARE, LOW) + feats * jnp.sum(off * off, axis=1, keepdims=True)
    inv = lax.rsqrt(square / width + EPS)
    total = mine[:rows, :feats].astype(F32) + theirs[:rows, :feats].astype(F32)
    low = values
    for j in range(2 * CHIPS):
        total = total + off[:, j : j + 1] * gain_w[j : j + 1, :]
        low = low + off[:, j : j + 1] * gain_low[j : j + 1, :]
    total = inv * total
    low = between(inv * low, LOW, GRAD)
    mixed[...] = total
    stats[...] = jnp.where(at == 0, mean, jnp.where(at == 1, inv, low))
    output[...] = (x[...].astype(F32) + total + dot(low.astype(BF), up[...])).astype(BF)


def rank_grads(sums):
    return pltpu.roll(between(sums, GRAD, FIRST), LANES - (GRAD - LOW), 1)


def normed(x, stats):
    return (x.astype(F32) - pick(stats, 0, 1)) * pick(stats, 1, 2)


def backward_kernel(flags, mine, theirs, sums, x, stats, gains, gain_low, w, down, grad_out):
    rows, feats = x.shape
    width = feats * 2 * CHIPS
    values = sums[...]
    low_grad = rank_grads(values)
    low = between(stats[...], LOW, GRAD)
    low_all = jnp.sum(gain_low[...], axis=0, keepdims=True)
    first = pick(values, FIRST, FIRST + 1) + jnp.sum(low_grad * low_all, axis=1, keepdims=True)
    second = pick(values, SECOND, SECOND + 1) + jnp.sum(low_grad * low, axis=1, keepdims=True)
    xhat = normed(x[...], stats[...])
    grad_norm = dot(low_grad, down[...], precision=HIGHEST)
    here = jnp.zeros((rows, feats), F32)
    for j in range(CHIPS):
        at = feats + LANES + j * feats
        grad = mine[:, at : at + feats].astype(F32) + theirs[:, at : at + feats].astype(F32)
        grad = grad.astype(BF)
        grad_norm = grad_norm + dot_t(grad, w[:, j * feats : (j + 1) * feats])
        here = here + jnp.where(flags[OWN_BLOCK] == j, grad.astype(F32), 0.0)
    inv = pick(stats[...], 1, 2)
    grad_x = here + inv * (grad_norm * gains[...] - first / width - xhat * (second / width))
    grad_out[...] = grad_x.astype(BF)


def accumulate_kernel(gains, after, *refs):
    count = TICKS - 1
    xs, stats, sums, grads = (refs[i * count : (i + 1) * count] for i in range(4))
    acc_down, acc_up = refs[4 * count :]
    rank = acc_up.shape[0]
    down, up = 0.0, 0.0
    for j in range(count):
        u = normed(xs[j][...], stats[j][...]) * gains[...]
        down = down + t_dot(rank_grads(sums[j][...]), u, precision=HIGHEST)
        up = up + t_dot(stats[j][...].astype(BF), grads[j][...])
    acc_down[...] = down[LOW : LOW + rank]
    acc_up[...] = up[LOW : LOW + rank]


def last_kernel(flags, arrived, output, up, stats, acc_up, low_out, up_out):
    rows, feats = arrived.shape
    rank = acc_up.shape[0]
    grad = chosen_grad(flags, arrived, output)
    turned = dot_t(up[LOW : LOW + rank], grad)
    turned = jnp.concatenate([turned, jnp.zeros((rank, LANES - rows), F32)], axis=1)
    high = turned.astype(BF).astype(F32)
    halves = jnp.concatenate([high, turned - high], axis=1).astype(BF)
    for j in range(4 * CHIPS):
        low_out[j] = halves
    low = t_dot(stats[...].astype(BF), grad)
    up_out[...] = (acc_up[...] + low[LOW : LOW + rank]).astype(BF)


def finish_kernel(got, x, stats, gains, mine, theirs, up_a, up_b, down_out, up_out):
    rows = x.shape[0]
    turned = got[0].astype(F32)
    for j in range(1, 4 * CHIPS):
        turned = turned + got[j].astype(F32)
    low_grad = turned[:, :LANES] + turned[:, LANES:]
    u = normed(x[...], stats[...]) * gains[...]
    u = jnp.concatenate([u, jnp.zeros((LANES - rows, u.shape[1]), F32)])
    total = mine[...] + theirs[...] + dot(low_grad, u, precision=HIGHEST)
    down_out[...] = (total / rows).astype(BF)
    up_out[...] = ((up_a[...].astype(F32) + up_b[...].astype(F32)) / rows).astype(BF)


def back_home(array, sections, flip):
    route = []
    for s in range(sections):
        for block in range(2 * CHIPS):
            for half in range(2):
                route.append((flat(s, *owner(block, half ^ flip)), flat(s, block, half)))
    return lax.ppermute(array, AXES, route)


def on_device(
    weight,
    adapter_down_map,
    adapter_up_map,
    gain,
    prior_epoch_input,
    prior_epoch_output,
    initial_step_inputs,
    initial_step_gradients,
    sample_numbers,
):
    del prior_epoch_output
    w = weight[0]
    gains = gain
    sections = lax.axis_size("section")
    section = lax.axis_index("section")
    tensor = lax.axis_index("tensor")
    half = lax.axis_index("dp")
    toks, feats = initial_step_inputs.shape[1:]
    rank = adapter_up_map.shape[1]
    rows = 2 * toks
    flags = [
        section == 0,
        tensor,
        section == sections - 1,
        tensor % 2,
        jnp.where(tensor // CHIPS == half, tensor % CHIPS, -1),
        half,
    ]
    flags = jnp.stack([f.astype(jnp.int32) for f in flags])
    flags = (jnp.concatenate([flags, sample_numbers[0, 0, 1:]]),)

    mine = initial_step_inputs[0]
    theirs = lax.ppermute(mine, "dp", [(0, 1), (1, 0)])
    packed, chosen = call(
        prepare_kernel,
        [shape(toks + rank, feats, dtype=BF), shape(TICKS - 1, toks, feats, dtype=BF)],
        initial_step_gradients[0],
        adapter_up_map[0],
        prior_epoch_input[0, 0],
        scalars=flags,
    )
    given = to_owner(packed, sections, 0)
    chosen_theirs = lax.ppermute(
        chosen,
        AXES,
        [(flat(0, t, d), flat(0, t, 1 - d)) for t in range(2 * CHIPS) for d in range(2)],
    )

    block = shape(rows, feats, dtype=BF)
    values = shape(rows, LANES)
    xs, all_stats, all_sums, grads = [], [], [], []
    for tick in range(TICKS):
        start = tick == 0
        more = 4 * CHIPS if start else 0
        out = [block, shape(CHIPS, rows + more, feats, dtype=BF), shape(rows + more, LANES)]
        if start:
            x, product, small, down = call(
                functools.partial(forward_kernel, True),
                out + [shape(LANES, feats)],
                mine,
                theirs,
                gains,
                w,
                adapter_down_map[0].T,
                scalars=flags,
            )
        else:
            x, product, small = call(
                lambda flags, *refs, tick=tick: forward_kernel(False, flags, tick, *refs),
                out,
                arrived,
                chosen,
                chosen_theirs,
                gains,
                w,
                down,
                scalars=flags,
            )
        x_owned = to_owner(x, sections, 0)
        columns = (1 if start else 2) * feats + LANES
        parcel = shape(CHIPS, rows + more, columns, dtype=BF)
        if start:
            parcel, up, grad_arrived = call(
                functools.partial(pack_kernel, True),
                [parcel, shape(LANES, feats, dtype=BF), block],
                product,
                small,
                x_owned,
                given,
                chosen_theirs,
                scalars=flags,
            )
        else:
            parcel, grad = call(
                functools.partial(pack_kernel, False),
                [parcel, block],
                product,
                small,
                x_owned,
                grad_arrived,
                output,
                up,
                gain_w,
                mixed,
                scalars=flags,
            )
            grads.append(grad)
        got = over_chips(parcel)
        own = call(
            functools.partial(gather_kernel, start),
            shape(rows + more, feats + LANES + (0 if start else CHIPS * feats), dtype=BF),
            got,
        )
        other = swap_cores(own)
        out = [block, shape(rows, feats), values, values]
        ins = [own, other, x_owned, up]
        kernel = functools.partial(output_kernel, start)
        if start:
            gain_w, gain_low, output, mixed, stats, sums = call(
                kernel, [shape(2 * CHIPS, feats), shape(2 * CHIPS, LANES)] + out, *ins
            )
        else:
            output, mixed, stats, sums = call(kernel, out, *ins, gain_w, gain_low)
            all_sums.append(sums)
        if tick < TICKS - 1:
            arrived = to_next(output, sections)
        if not start:
            grad_x = call(
                backward_kernel,
                block,
                own,
                other,
                sums,
                xs[-1],
                all_stats[-1],
                gains,
                gain_low,
                w,
                down,
                scalars=flags,
            )
            grad_arrived = to_owner(grad_x, sections, 1)
        xs.append(x)
        all_stats.append(stats)

    acc_down, acc_up = call(
        accumulate_kernel,
        [shape(rank, feats), shape(rank, feats)],
        gains,
        grad_x,
        *xs[:-1],
        *all_stats[:-1],
        *all_sums,
        *grads,
    )
    acc_other = lax.ppermute(acc_down, "dp", [(0, 1), (1, 0)])
    turned, up_part = call(
        last_kernel,
        [shape(4 * CHIPS, rank, 2 * LANES, dtype=BF), shape(rank, feats, dtype=BF)],
        grad_arrived,
        output,
        up,
        stats,
        acc_up,
        scalars=flags,
    )
    got = lax.all_to_all(turned, ("tensor", "dp"), 0, 0)
    grad_down, grad_up = call(
        finish_kernel,
        [shape(rank, feats, dtype=BF), shape(rank, feats, dtype=BF)],
        got,
        x,
        stats,
        gains,
        acc_down,
        acc_other,
        back_home(up_part, sections, 0),
        back_home(up_part, sections, 1),
    )
    return grad_down.T[None], grad_up[None]


def solution(mesh):
    in_specs = (
        P("section", "tensor", "dp"),
        P("section", "tensor", None),
        P("section", None, "tensor"),
        P("section", "tensor"),
        P("section", "dp", None, None, "tensor"),
        P("section", "dp", None, None, "tensor"),
        P("section", "dp", "tensor"),
        P("section", "dp", "tensor"),
        P("section", "dp", None),
    )
    out_specs = (P("section", "tensor", None), P("section", None, "tensor"))
    return jax.shard_map(
        on_device, mesh=mesh, in_specs=in_specs, out_specs=out_specs, check_vma=False
    )
```

```python
import functools

import jax
import jax.numpy as jnp
from jax import lax
from jax.experimental import pallas as pl
from jax.experimental.pallas import tpu as pltpu
from jax.sharding import PartitionSpec as P

TICKS = 4
CHIPS = 4
EPS = 1e-05
AXES = ("section", "tensor", "dp")
HIGHEST = lax.Precision.HIGHEST
BF = jnp.bfloat16
F32 = jnp.float32

LANES = 128
SQUARE = 8
LOW = 16
GRAD = 32
FIRST = 48
SECOND = 49


def flat(section, tensor, dp):
    return (section * 2 * CHIPS + tensor) * 2 + dp


def owner(block, core):
    return 2 * (block % CHIPS) + core, block // CHIPS


def to_owner(array, sections, back):
    route = []
    for s in range(sections):
        for block in range(2 * CHIPS):
            for half in range(2):
                if s - back >= 0:
                    route.append((flat(s, block, half), flat(s - back, *owner(block, half))))
    return lax.ppermute(array, AXES, route)


def to_next(array, sections):
    route = []
    for s in range(sections - 1):
        for block in range(2 * CHIPS):
            for half in range(2):
                route.append((flat(s, *owner(block, half)), flat(s + 1, block, half)))
    return lax.ppermute(array, AXES, route)


def swap_cores(array):
    return lax.ppermute(array, "tensor", [(i, i ^ 1) for i in range(2 * CHIPS)])


def over_chips(array):
    groups = [[2 * i for i in range(CHIPS)], [2 * i + 1 for i in range(CHIPS)]]
    return lax.all_to_all(array, "tensor", 0, 0, axis_index_groups=groups)


def dot(a, b, **kw):
    return jnp.dot(a, b, preferred_element_type=F32, **kw)


def dot_t(a, b, **kw):
    return lax.dot_general(a, b, (((1,), (1,)), ((), ())), preferred_element_type=F32, **kw)


def t_dot(a, b, **kw):
    return lax.dot_general(a, b, (((0,), (0,)), ((), ())), preferred_element_type=F32, **kw)


def lane(rows):
    return lax.broadcasted_iota(jnp.int32, (rows, LANES), 1)


def between(values, low, high):
    at = lane(values.shape[0])
    return jnp.where((at >= low) & (at < high), values, 0.0)


def pick(values, low, high):
    return jnp.sum(between(values, low, high), axis=1, keepdims=True)


def split(values):
    high = values.astype(BF).astype(F32)
    rest = pltpu.roll(values - high, LANES // 2, 1)
    return jnp.where(lane(values.shape[0]) < LANES // 2, high, rest).astype(BF)


def join(halves):
    wide = halves.astype(F32)
    return wide + pltpu.roll(wide, LANES // 2, 1)


def call(kernel, out, *args, scalars=(), vmem=16):
    return pl.pallas_call(
        kernel,
        out_shape=out,
        in_specs=[pl.BlockSpec(memory_space=pltpu.SMEM)] * len(scalars)
        + [pl.BlockSpec(memory_space=pltpu.VMEM)] * len(args),
        out_specs=jax.tree.map(lambda _: pl.BlockSpec(memory_space=pltpu.VMEM), out),
        compiler_params=pltpu.CompilerParams(vmem_limit_bytes=vmem * 2**20),
    )(*scalars, *args)


def shape(*dims, dtype=F32):
    return jax.ShapeDtypeStruct(dims, dtype)


def own_block():
    tensor = lax.axis_index("tensor")
    return jnp.where(tensor // CHIPS == lax.axis_index("dp"), tensor % CHIPS, -1)


def replicas(mine, theirs):
    first = lax.axis_index("dp") == 0
    return jnp.concatenate([jnp.where(first, mine, theirs), jnp.where(first, theirs, mine)])


def forward_kernel(start, tick, *refs):
    place = lax.axis_index("tensor")
    if start:
        _, _, _, _, mine, theirs, gains, w, down_rows, x_out, product, small, down = refs
        x = replicas(mine[...], theirs[...])
        rank, feats = down_rows.shape
        down[:LOW] = jnp.zeros((LOW, feats), F32)
        down[LOW : LOW + rank] = down_rows[...].astype(F32)
        down[LOW + rank :] = jnp.zeros((LANES - LOW - rank, feats), F32)
    else:
        order, order_theirs, arrived, mine, theirs, gains, w, down, x_out, product, small = refs
        given = replicas(
            jnp.where(order[tick] == 0, mine[0], mine[1]),
            jnp.where(order_theirs[tick] == 0, theirs[0], theirs[1]),
        )
        x = jnp.where(lax.axis_index("section") == 0, given, arrived[...])
    x_out[...] = x
    rows, feats = x.shape
    wide = x.astype(F32)
    mid = jnp.sum(wide, axis=1, keepdims=True) / feats
    centered = wide - mid
    square = jnp.sum(centered * centered, axis=1, keepdims=True)
    scaled = centered * gains[...]
    at = lane(rows)
    low = dot_t(scaled, down[...], precision=HIGHEST)
    low = jnp.where(at == place, mid, low)
    small[0:rows] = jnp.where(at == SQUARE + place, square, low)
    left = scaled.astype(BF)
    if start:
        row = lax.broadcasted_iota(jnp.int32, (2 * CHIPS, feats), 0)
        gain_rows = jnp.where(row == place, gains[...], 0.0)
        high = gain_rows.astype(BF).astype(F32)
        left = jnp.concatenate([left, jnp.concatenate([high, gain_rows - high]).astype(BF)])
        small[rows:] = jnp.concatenate(
            [dot_t(gain_rows, down[...], precision=HIGHEST), jnp.zeros((2 * CHIPS, LANES), F32)]
        )
    for j in range(CHIPS):
        part = dot(left, w[:, j * feats : (j + 1) * feats])
        if start:
            tail = part[rows : rows + 2 * CHIPS] + part[rows + 2 * CHIPS :]
            high = tail.astype(BF).astype(F32)
            part = jnp.concatenate([part[:rows], high, tail - high])
        product[j] = part.astype(BF)


def first_core():
    return lax.axis_index("tensor") % 2 == 0


def chosen_grad(sections, arrived, output):
    kept = jnp.where(first_core(), output[...], jnp.zeros(output.shape, BF))
    return jnp.where(lax.axis_index("section") == sections - 1, kept, arrived[...])


def pack_kernel(start, sections, product, small, x, *refs):
    rows, feats = x.shape
    values = small[...]
    if start:
        given, given_up, parcel, up, grad_out = refs
        columns = feats
        toks = given.shape[0]
        rank = given_up.shape[0]
        up[:LOW] = jnp.zeros((LOW, feats), BF)
        up[LOW : LOW + rank] = given_up[...]
        up[LOW + rank :] = jnp.zeros((LANES - LOW - rank, feats), BF)
        zeros = jnp.zeros((toks, feats), BF)
        grad_out[:toks] = jnp.where(first_core(), given[...], zeros)
        grad_out[toks:] = jnp.where(first_core(), zeros, given[...])
    else:
        arrived, output, up, gain_w, mixed, parcel, grad_out = refs
        columns = 2 * feats
        grad = chosen_grad(sections, arrived, output)
        grad_out[...] = grad
        wide = grad.astype(F32)
        first = jnp.sum(wide * jnp.sum(gain_w[...], axis=0, keepdims=True), axis=1, keepdims=True)
        second = jnp.sum(wide * mixed[...], axis=1, keepdims=True)
        at = lane(rows)
        values = values + pltpu.roll(dot_t(grad, up[...]), GRAD - LOW, 1)
        values = jnp.where(at == FIRST, first, values)
        values = jnp.where(at == SECOND, second, values)
        for j in range(CHIPS):
            parcel[j, :, feats : 2 * feats] = grad
    halves = split(values)
    block = own_block()
    for j in range(CHIPS):
        parcel[j, :, :feats] = product[j]
        parcel[j, :rows, columns : columns + feats] = jnp.where(
            block == j, x[...], jnp.zeros(x.shape, BF)
        )
        if start:
            parcel[j, rows:, columns : columns + feats] = jnp.zeros((4 * CHIPS, feats), BF)
        parcel[j, :, columns + feats :] = halves


def gather_kernel(start, got, out):
    feats = (got.shape[2] - LANES) // (2 if start else 3)
    total = got[0, :, :feats].astype(F32)
    x = got[0, :, -LANES - feats : -LANES]
    values = join(got[0, :, -LANES:])
    for j in range(1, CHIPS):
        total = total + got[j, :, :feats].astype(F32)
        x = x + got[j, :, -LANES - feats : -LANES]
        values = values + join(got[j, :, -LANES:])
    out[:, :feats] = total.astype(BF)
    out[:, feats : 2 * feats] = x
    out[:, 2 * feats : 2 * feats + LANES] = split(values)
    if not start:
        for j in range(CHIPS):
            at = 2 * feats + LANES + j * feats
            out[:, at : at + feats] = got[j, :, feats : 2 * feats]


def output_kernel(start, mine, theirs, up, gain_w, gain_low, output, mixed, stats, sums):
    rows, feats = output.shape
    ends = slice(2 * feats, 2 * feats + LANES)
    if start:
        tail = mine[rows:, :feats].astype(F32) + theirs[rows:, :feats].astype(F32)
        gain_w[...] = tail[: 2 * CHIPS] + tail[2 * CHIPS :]
        tail = join(mine[rows:, ends]) + join(theirs[rows:, ends])
        gain_low[...] = between(tail[: 2 * CHIPS], LOW, GRAD)
    values = join(mine[:rows, ends]) + join(theirs[:rows, ends])
    values = between(values, 0, LANES // 2)
    sums[...] = values
    at = lane(rows)
    width = feats * 2 * CHIPS
    mean = pick(values, 0, SQUARE) / (2 * CHIPS)
    off = jnp.where(at < 2 * CHIPS, values - mean, 0.0)
    square = pick(values, SQUARE, LOW) + feats * jnp.sum(off * off, axis=1, keepdims=True)
    inv = lax.rsqrt(square / width + EPS)
    total = mine[:rows, :feats].astype(F32) + theirs[:rows, :feats].astype(F32)
    low = values
    for j in range(2 * CHIPS):
        total = total + off[:, j : j + 1] * gain_w[j : j + 1, :]
        low = low + off[:, j : j + 1] * gain_low[j : j + 1, :]
    total = inv * total
    low = between(inv * low, LOW, GRAD)
    mixed[...] = total
    stats[...] = jnp.where(at == 0, mean, jnp.where(at == 1, inv, low))
    x = mine[:rows, feats : 2 * feats].astype(F32) + theirs[:rows, feats : 2 * feats].astype(F32)
    output[...] = (x + total + dot(low.astype(BF), up[...])).astype(BF)


def rank_grads(sums):
    return pltpu.roll(between(sums, GRAD, FIRST), LANES - (GRAD - LOW), 1)


def normed(x, stats):
    return (x.astype(F32) - pick(stats, 0, 1)) * pick(stats, 1, 2)


def backward_kernel(mine, theirs, sums, x, stats, gains, gain_low, w, down, grad_out):
    rows, feats = x.shape
    width = feats * 2 * CHIPS
    values = sums[...]
    low_grad = rank_grads(values)
    low = between(stats[...], LOW, GRAD)
    low_all = jnp.sum(gain_low[...], axis=0, keepdims=True)
    first = pick(values, FIRST, FIRST + 1) + jnp.sum(low_grad * low_all, axis=1, keepdims=True)
    second = pick(values, SECOND, SECOND + 1) + jnp.sum(low_grad * low, axis=1, keepdims=True)
    xhat = normed(x[...], stats[...])
    grad_norm = dot(low_grad, down[...], precision=HIGHEST)
    here = jnp.zeros((rows, feats), F32)
    for j in range(CHIPS):
        at = 2 * feats + LANES + j * feats
        grad = mine[:, at : at + feats].astype(F32) + theirs[:, at : at + feats].astype(F32)
        grad = grad.astype(BF)
        grad_norm = grad_norm + dot_t(grad, w[:, j * feats : (j + 1) * feats])
        here = here + jnp.where(own_block() == j, grad.astype(F32), 0.0)
    inv = pick(stats[...], 1, 2)
    grad_x = here + inv * (grad_norm * gains[...] - first / width - xhat * (second / width))
    grad_out[...] = grad_x.astype(BF)


def accumulate_kernel(gains, after, *refs):
    count = TICKS - 1
    xs, stats, sums, grads = (refs[i * count : (i + 1) * count] for i in range(4))
    acc_down, acc_up = refs[4 * count :]
    rank = acc_up.shape[0]
    down, up = 0.0, 0.0
    for j in range(count):
        u = normed(xs[j][...], stats[j][...]) * gains[...]
        down = down + t_dot(rank_grads(sums[j][...]), u, precision=HIGHEST)
        up = up + t_dot(stats[j][...].astype(BF), grads[j][...])
    acc_down[...] = down[LOW : LOW + rank]
    acc_up[...] = up[LOW : LOW + rank]


def last_kernel(sections, arrived, output, up, stats, acc_up, after, low_out, up_out):
    rows, feats = arrived.shape
    rank = acc_up.shape[0]
    grad = chosen_grad(sections, arrived, output)
    turned = dot_t(up[LOW : LOW + rank], grad)
    turned = jnp.concatenate([turned, jnp.zeros((rank, LANES - rows), F32)], axis=1)
    high = turned.astype(BF).astype(F32)
    halves = jnp.concatenate([high, turned - high], axis=1).astype(BF)
    for j in range(4 * CHIPS):
        low_out[j] = halves
    low = t_dot(stats[...].astype(BF), grad)
    up_out[...] = (acc_up[...] + low[LOW : LOW + rank]).astype(BF)


def finish_kernel(got, x, stats, gains, mine, theirs, up_a, up_b, down_out, up_out):
    rows = x.shape[0]
    turned = got[0].astype(F32)
    for j in range(1, 4 * CHIPS):
        turned = turned + got[j].astype(F32)
    low_grad = turned[:, :LANES] + turned[:, LANES:]
    u = normed(x[...], stats[...]) * gains[...]
    u = jnp.concatenate([u, jnp.zeros((LANES - rows, u.shape[1]), F32)])
    total = mine[...] + theirs[...] + dot(low_grad, u, precision=HIGHEST)
    down_out[...] = (total / rows).astype(BF)
    up_out[...] = ((up_a[...].astype(F32) + up_b[...].astype(F32)) / rows).astype(BF)


def back_home(array, sections, flip):
    route = []
    for s in range(sections):
        for block in range(2 * CHIPS):
            for half in range(2):
                route.append((flat(s, *owner(block, half ^ flip)), flat(s, block, half)))
    return lax.ppermute(array, AXES, route)


def on_device(
    weight,
    adapter_down_map,
    adapter_up_map,
    gain,
    prior_epoch_input,
    prior_epoch_output,
    initial_step_inputs,
    initial_step_gradients,
    sample_numbers,
):
    del prior_epoch_output
    w = weight[0]
    gains = gain
    sections = lax.axis_size("section")
    toks, feats = initial_step_inputs.shape[1:]
    rank = adapter_up_map.shape[1]
    rows = 2 * toks

    mine = initial_step_inputs[0]
    theirs = lax.ppermute(mine, "dp", [(0, 1), (1, 0)])
    given = to_owner(initial_step_gradients[0], sections, 0)
    given_up = to_owner(adapter_up_map[0], sections, 0)
    stored = prior_epoch_input[0, 0]
    order = sample_numbers[0, 0]
    to_partner = [(flat(0, t, d), flat(0, t, 1 - d)) for t in range(2 * CHIPS) for d in range(2)]
    stored_theirs = lax.ppermute(stored, AXES, to_partner)
    order_theirs = lax.ppermute(order, AXES, to_partner)

    block = shape(rows, feats, dtype=BF)
    values = shape(rows, LANES)
    xs, all_stats, all_sums, grads = [], [], [], []
    for tick in range(TICKS):
        start = tick == 0
        more = 4 * CHIPS if start else 0
        out = [block, shape(CHIPS, rows + more, feats, dtype=BF), shape(rows + more, LANES)]
        if start:
            x, product, small, down = call(
                functools.partial(forward_kernel, True, tick),
                out + [shape(LANES, feats)],
                given,
                given_up,
                stored_theirs,
                mine,
                theirs,
                gains,
                w,
                adapter_down_map[0].T,
                scalars=(order_theirs,),
            )
        else:
            x, product, small = call(
                functools.partial(forward_kernel, False, tick),
                out,
                arrived,
                stored,
                stored_theirs,
                gains,
                w,
                down,
                scalars=(order, order_theirs),
            )
        columns = (2 if start else 3) * feats + LANES
        parcel = shape(CHIPS, rows + more, columns, dtype=BF)
        if start:
            parcel, up, grad_arrived = call(
                functools.partial(pack_kernel, True, sections),
                [parcel, shape(LANES, feats, dtype=BF), block],
                product,
                small,
                x,
                given,
                given_up,
            )
        else:
            parcel, grad = call(
                functools.partial(pack_kernel, False, sections),
                [parcel, block],
                product,
                small,
                x,
                grad_arrived,
                output,
                up,
                gain_w,
                mixed,
            )
            grads.append(grad)
        got = over_chips(parcel)
        own = call(
            functools.partial(gather_kernel, start),
            shape(rows + more, 2 * feats + LANES + (0 if start else CHIPS * feats), dtype=BF),
            got,
        )
        other = swap_cores(own)
        out = [block, shape(rows, feats), values, values]
        ins = [own, other, up]
        kernel = functools.partial(output_kernel, start)
        if start:
            gain_w, gain_low, output, mixed, stats, sums = call(
                kernel, [shape(2 * CHIPS, feats), shape(2 * CHIPS, LANES)] + out, *ins
            )
        else:
            output, mixed, stats, sums = call(kernel, out, *ins, gain_w, gain_low)
            all_sums.append(sums)
        if tick < TICKS - 1:
            arrived = to_next(output, sections)
        if not start:
            grad_x = call(
                backward_kernel,
                block,
                own,
                other,
                sums,
                xs[-1],
                all_stats[-1],
                gains,
                gain_low,
                w,
                down,
            )
            grad_arrived = to_owner(grad_x, sections, 1)
        xs.append(x)
        all_stats.append(stats)

    acc_down, acc_up = call(
        accumulate_kernel,
        [shape(rank, feats), shape(rank, feats)],
        gains,
        grad_x,
        *xs[:-1],
        *all_stats[:-1],
        *all_sums,
        *grads,
    )
    acc_other = lax.ppermute(acc_down, "dp", [(0, 1), (1, 0)])
    turned, up_part = call(
        functools.partial(last_kernel, sections),
        [shape(4 * CHIPS, rank, 2 * LANES, dtype=BF), shape(rank, feats, dtype=BF)],
        grad_arrived,
        output,
        up,
        stats,
        acc_up,
        acc_other,
    )
    got = lax.all_to_all(turned, ("tensor", "dp"), 0, 0)
    grad_down, grad_up = call(
        finish_kernel,
        [shape(rank, feats, dtype=BF), shape(rank, feats, dtype=BF)],
        got,
        x,
        stats,
        gains,
        acc_down,
        acc_other,
        back_home(up_part, sections, 0),
        back_home(up_part, sections, 1),
    )
    return grad_down.T[None], grad_up[None]


def solution(mesh):
    in_specs = (
        P("section", "tensor", "dp"),
        P("section", "tensor", None),
        P("section", None, "tensor"),
        P("section", "tensor"),
        P("section", "dp", None, None, "tensor"),
        P("section", "dp", None, None, "tensor"),
        P("section", "dp", "tensor"),
        P("section", "dp", "tensor"),
        P("section", "dp", None),
    )
    out_specs = (P("section", "tensor", None), P("section", None, "tensor"))
    return jax.shard_map(
        on_device, mesh=mesh, in_specs=in_specs, out_specs=out_specs, check_vma=False
    )
```

```python
import functools

import jax
import jax.numpy as jnp
from jax import lax
from jax.experimental import pallas as pl
from jax.experimental.pallas import tpu as pltpu
from jax.sharding import PartitionSpec as P

TICKS = 4
CHIPS = 4
EPS = 1e-05
AXES = ("section", "tensor", "dp")
HIGHEST = lax.Precision.HIGHEST
BF = jnp.bfloat16
F32 = jnp.float32

LANES = 128
SQUARE = 8
LOW = 16
GRAD = 32
FIRST = 48
SECOND = 49


def flat(section, tensor, dp):
    return (section * 2 * CHIPS + tensor) * 2 + dp


def owner(block, core):
    return 2 * (block % CHIPS) + core, block // CHIPS


def to_owner(array, sections, back):
    route = []
    for s in range(sections):
        for block in range(2 * CHIPS):
            for half in range(2):
                if s - back >= 0:
                    route.append((flat(s, block, half), flat(s - back, *owner(block, half))))
    return lax.ppermute(array, AXES, route)


def to_next(array, sections):
    route = []
    for s in range(sections - 1):
        for block in range(2 * CHIPS):
            for half in range(2):
                route.append((flat(s, *owner(block, half)), flat(s + 1, block, half)))
    return lax.ppermute(array, AXES, route)


def swap_cores(array):
    return lax.ppermute(array, "tensor", [(i, i ^ 1) for i in range(2 * CHIPS)])


def over_chips(array):
    groups = [[2 * i for i in range(CHIPS)], [2 * i + 1 for i in range(CHIPS)]]
    return lax.all_to_all(array, "tensor", 0, 0, axis_index_groups=groups)


def dot(a, b, **kw):
    return jnp.dot(a, b, preferred_element_type=F32, **kw)


def dot_t(a, b, **kw):
    return lax.dot_general(a, b, (((1,), (1,)), ((), ())), preferred_element_type=F32, **kw)


def t_dot(a, b, **kw):
    return lax.dot_general(a, b, (((0,), (0,)), ((), ())), preferred_element_type=F32, **kw)


def lane(rows):
    return lax.broadcasted_iota(jnp.int32, (rows, LANES), 1)


def between(values, low, high):
    at = lane(values.shape[0])
    return jnp.where((at >= low) & (at < high), values, 0.0)


def pick(values, low, high):
    return jnp.sum(between(values, low, high), axis=1, keepdims=True)


def split(values):
    high = values.astype(BF).astype(F32)
    rest = pltpu.roll(values - high, LANES // 2, 1)
    return jnp.where(lane(values.shape[0]) < LANES // 2, high, rest).astype(BF)


def join(halves):
    wide = halves.astype(F32)
    return wide + pltpu.roll(wide, LANES // 2, 1)


def call(kernel, out, *args, scalars=(), vmem=16):
    return pl.pallas_call(
        kernel,
        out_shape=out,
        in_specs=[pl.BlockSpec(memory_space=pltpu.SMEM)] * len(scalars)
        + [pl.BlockSpec(memory_space=pltpu.VMEM)] * len(args),
        out_specs=jax.tree.map(lambda _: pl.BlockSpec(memory_space=pltpu.VMEM), out),
        compiler_params=pltpu.CompilerParams(vmem_limit_bytes=vmem * 2**20),
    )(*scalars, *args)


def shape(*dims, dtype=F32):
    return jax.ShapeDtypeStruct(dims, dtype)


def own_block():
    tensor = lax.axis_index("tensor")
    return jnp.where(tensor // CHIPS == lax.axis_index("dp"), tensor % CHIPS, -1)


def replicas(mine, theirs):
    first = lax.axis_index("dp") == 0
    return jnp.concatenate([jnp.where(first, mine, theirs), jnp.where(first, theirs, mine)])


def forward_kernel(start, tick, *refs):
    place = lax.axis_index("tensor")
    if start:
        _, _, _, _, mine, theirs, gains, w, down_rows, x_out, product, small, down = refs
        x = replicas(mine[...], theirs[...])
        rank, feats = down_rows.shape
        down[:LOW] = jnp.zeros((LOW, feats), F32)
        down[LOW : LOW + rank] = down_rows[...].astype(F32)
        down[LOW + rank :] = jnp.zeros((LANES - LOW - rank, feats), F32)
    else:
        order, order_theirs, arrived, mine, theirs, gains, w, down, x_out, product, small = refs
        given = replicas(
            jnp.where(order[tick] == 0, mine[0], mine[1]),
            jnp.where(order_theirs[tick] == 0, theirs[0], theirs[1]),
        )
        x = jnp.where(lax.axis_index("section") == 0, given, arrived[...])
    x_out[...] = x
    rows, feats = x.shape
    wide = x.astype(F32)
    mid = jnp.sum(wide, axis=1, keepdims=True) / feats
    centered = wide - mid
    square = jnp.sum(centered * centered, axis=1, keepdims=True)
    scaled = centered * gains[...]
    at = lane(rows)
    low = dot_t(scaled, down[...], precision=HIGHEST)
    low = jnp.where(at == place, mid, low)
    small[0:rows] = jnp.where(at == SQUARE + place, square, low)
    left = scaled.astype(BF)
    if start:
        row = lax.broadcasted_iota(jnp.int32, (2 * CHIPS, feats), 0)
        gain_rows = jnp.where(row == place, gains[...], 0.0)
        high = gain_rows.astype(BF).astype(F32)
        left = jnp.concatenate([left, jnp.concatenate([high, gain_rows - high]).astype(BF)])
        small[rows:] = jnp.concatenate(
            [dot_t(gain_rows, down[...], precision=HIGHEST), jnp.zeros((2 * CHIPS, LANES), F32)]
        )
    for j in range(CHIPS):
        part = dot(left, w[:, j * feats : (j + 1) * feats])
        if start:
            tail = part[rows : rows + 2 * CHIPS] + part[rows + 2 * CHIPS :]
            high = tail.astype(BF).astype(F32)
            part = jnp.concatenate([part[:rows], high, tail - high])
        product[j] = part.astype(BF)


def first_core():
    return lax.axis_index("tensor") % 2 == 0


def chosen_grad(sections, arrived, output):
    kept = jnp.where(first_core(), output[...], jnp.zeros(output.shape, BF))
    return jnp.where(lax.axis_index("section") == sections - 1, kept, arrived[...])


def own_half(array):
    feats = array.shape[-1]
    return jnp.where(first_core(), array[..., : feats // 2], array[..., feats // 2 :])


def other_half(array):
    feats = array.shape[-1]
    return jnp.where(first_core(), array[..., feats // 2 :], array[..., : feats // 2])


def both_halves(mine, theirs):
    return jnp.concatenate(
        [jnp.where(first_core(), mine, theirs), jnp.where(first_core(), theirs, mine)], axis=-1
    )


def deal_kernel(start, sections, product, small, x, *refs):
    rows, feats = x.shape
    width = feats // 2
    if start:
        given, given_up, out, up, grad_out = refs
        toks = given.shape[0]
        rank = given_up.shape[0]
        up[:LOW] = jnp.zeros((LOW, feats), BF)
        up[LOW : LOW + rank] = given_up[...]
        up[LOW + rank :] = jnp.zeros((LANES - LOW - rank, feats), BF)
        zeros = jnp.zeros((toks, feats), BF)
        grad_out[:toks] = jnp.where(first_core(), given[...], zeros)
        grad_out[toks:] = jnp.where(first_core(), zeros, given[...])
    else:
        arrived, output, out, grad_out = refs
        grad = chosen_grad(sections, arrived, output)
        grad_out[...] = grad
        at = (CHIPS + 1) * width + LANES
        out[:, at:] = other_half(grad)
    for j in range(CHIPS):
        out[:, j * width : (j + 1) * width] = other_half(product[j])
    at = CHIPS * width
    out[:rows, at : at + width] = other_half(x[...])
    if start:
        out[rows:, at : at + width] = jnp.zeros((4 * CHIPS, width), BF)
    out[:, at + width : at + width + LANES] = split(small[...])


def pack_kernel(start, product, small, x, theirs, *refs):
    rows, feats = x.shape
    width = feats // 2
    at = CHIPS * width
    mine_x = own_half(x[...])
    theirs_x = theirs[:rows, at : at + width]
    at = at + width
    values = join(split(small[...])) + join(theirs[:, at : at + LANES])
    values = between(values, 0, LANES // 2)
    if start:
        (parcel,) = refs
    else:
        grad_part, up, gain_w, mixed, parcel, grad_out = refs
        grad = own_half(grad_part[...]).astype(F32) + theirs[:, at + LANES :].astype(F32)
        grad = grad.astype(BF)
        grad_out[...] = grad
        wide = grad.astype(F32)
        first = jnp.sum(wide * jnp.sum(gain_w[...], axis=0, keepdims=True), axis=1, keepdims=True)
        second = jnp.sum(wide * mixed[...], axis=1, keepdims=True)
        lanes = lane(rows)
        values = values + pltpu.roll(dot_t(grad, own_half(up[...])), GRAD - LOW, 1)
        values = jnp.where(lanes == FIRST, first, values)
        values = jnp.where(lanes == SECOND, second, values)
        for j in range(CHIPS):
            parcel[j, :, 2 * width + LANES :] = grad
    halves = split(values)
    block = own_block()
    for j in range(CHIPS):
        total = own_half(product[j]).astype(F32)
        total = total + theirs[:, j * width : (j + 1) * width].astype(F32)
        parcel[j, :, :width] = total.astype(BF)
        held = jnp.where(block == j, mine_x, jnp.where(block == (j ^ 1), theirs_x, 0.0).astype(BF))
        parcel[j, :rows, width : 2 * width] = held
        if start:
            parcel[j, rows:, width : 2 * width] = jnp.zeros((4 * CHIPS, width), BF)
        parcel[j, :, 2 * width : 2 * width + LANES] = halves


def output_kernel(start, got, up, *refs):
    if start:
        gain_w, gain_low, out, mixed, stats = refs
    else:
        gain_w, gain_low, out, mixed, stats = refs
    rows, width = mixed.shape
    feats = 2 * width
    total = got[0, :, :width].astype(F32)
    x = got[0, :rows, width:feats].astype(F32)
    values = join(got[0, :, feats : feats + LANES])
    for j in range(1, CHIPS):
        total = total + got[j, :, :width].astype(F32)
        x = x + got[j, :rows, width:feats].astype(F32)
        values = values + join(got[j, :, feats : feats + LANES])
    values = between(values, 0, LANES // 2)
    if start:
        gain_w[...] = total[rows : rows + 2 * CHIPS] + total[rows + 2 * CHIPS :]
        gain_low[...] = between(values[rows : rows + 2 * CHIPS], LOW, GRAD)
        total = total[:rows]
        values = values[:rows]
    at = lane(rows)
    mean = pick(values, 0, SQUARE) / (2 * CHIPS)
    off = jnp.where(at < 2 * CHIPS, values - mean, 0.0)
    square = pick(values, SQUARE, LOW) + feats * jnp.sum(off * off, axis=1, keepdims=True)
    inv = lax.rsqrt(square / (feats * 2 * CHIPS) + EPS)
    low = values
    for j in range(2 * CHIPS):
        total = total + off[:, j : j + 1] * gain_w[j : j + 1, :]
        low = low + off[:, j : j + 1] * gain_low[j : j + 1, :]
    total = inv * total
    low = between(inv * low, LOW, GRAD)
    mixed[...] = total
    stats[...] = jnp.where(at == 0, mean, jnp.where(at == 1, inv, low))
    out[:, :width] = (x + total + dot(low.astype(BF), own_half(up[...]))).astype(BF)
    if not start:
        out[:, width : width + LANES] = split(values)
        for j in range(CHIPS):
            at = width + LANES + j * width
            out[:, at : at + width] = got[j, :, feats + LANES :]


def whole_kernel(mine, theirs, output):
    width = output.shape[1] // 2
    output[...] = both_halves(mine[:, :width], theirs[:, :width])


def rank_grads(sums):
    return pltpu.roll(between(sums, GRAD, FIRST), LANES - (GRAD - LOW), 1)


def normed(x, stats):
    return (x.astype(F32) - pick(stats, 0, 1)) * pick(stats, 1, 2)


def backward_kernel(mine, theirs, x, stats, gains, gain_low, w, down, grad_out, sums):
    rows, feats = x.shape
    width = feats * 2 * CHIPS
    half = feats // 2
    ends = slice(half, half + LANES)
    values = join(mine[:, ends]) + join(theirs[:, ends])
    sums[...] = values
    low_grad = rank_grads(values)
    low = between(stats[...], LOW, GRAD)
    low_all = jnp.sum(gain_low[...], axis=0, keepdims=True)
    first = pick(values, FIRST, FIRST + 1) + jnp.sum(low_grad * low_all, axis=1, keepdims=True)
    second = pick(values, SECOND, SECOND + 1) + jnp.sum(low_grad * low, axis=1, keepdims=True)
    xhat = normed(x[...], stats[...])
    grad_norm = dot(low_grad, down[...], precision=HIGHEST)
    here = jnp.zeros((rows, feats), F32)
    for j in range(CHIPS):
        at = half + LANES + j * half
        grad = both_halves(mine[:, at : at + half], theirs[:, at : at + half])
        grad_norm = grad_norm + dot_t(grad, w[:, j * feats : (j + 1) * feats])
        here = here + jnp.where(own_block() == j, grad.astype(F32), 0.0)
    inv = pick(stats[...], 1, 2)
    grad_x = here + inv * (grad_norm * gains[...] - first / width - xhat * (second / width))
    grad_out[...] = grad_x.astype(BF)


def accumulate_kernel(gains, after, *refs):
    count = TICKS - 1
    xs, stats, sums, grads = (refs[i * count : (i + 1) * count] for i in range(4))
    acc_down, acc_up = refs[4 * count :]
    rank = acc_up.shape[0]
    down, up = 0.0, 0.0
    for j in range(count):
        u = normed(xs[j][...], stats[j][...]) * gains[...]
        down = down + t_dot(rank_grads(sums[j][...]), u, precision=HIGHEST)
        up = up + t_dot(stats[j][...].astype(BF), grads[j][...])
    acc_down[...] = down[LOW : LOW + rank]
    acc_up[...] = up[LOW : LOW + rank]


def last_kernel(sections, arrived, output, up, stats, acc_up, after, low_out, up_out):
    rows, feats = arrived.shape
    rank = acc_up.shape[0]
    grad = chosen_grad(sections, arrived, output)
    turned = dot_t(up[LOW : LOW + rank], grad)
    turned = jnp.concatenate([turned, jnp.zeros((rank, LANES - rows), F32)], axis=1)
    high = turned.astype(BF).astype(F32)
    halves = jnp.concatenate([high, turned - high], axis=1).astype(BF)
    for j in range(4 * CHIPS):
        low_out[j] = halves
    low = t_dot(stats[...].astype(BF), grad)
    zeros = jnp.zeros(acc_up.shape, F32)
    acc = jnp.concatenate(
        [jnp.where(first_core(), acc_up[...], zeros), jnp.where(first_core(), zeros, acc_up[...])],
        axis=1,
    )
    up_out[...] = (acc + low[LOW : LOW + rank]).astype(BF)


def finish_kernel(got, x, stats, gains, mine, theirs, up_a, up_b, down_out, up_out):
    rows = x.shape[0]
    turned = got[0].astype(F32)
    for j in range(1, 4 * CHIPS):
        turned = turned + got[j].astype(F32)
    low_grad = turned[:, :LANES] + turned[:, LANES:]
    u = normed(x[...], stats[...]) * gains[...]
    u = jnp.concatenate([u, jnp.zeros((LANES - rows, u.shape[1]), F32)])
    total = mine[...] + theirs[...] + dot(low_grad, u, precision=HIGHEST)
    down_out[...] = (total / rows).astype(BF)
    up_out[...] = ((up_a[...].astype(F32) + up_b[...].astype(F32)) / rows).astype(BF)


def back_home(array, sections, flip):
    route = []
    for s in range(sections):
        for block in range(2 * CHIPS):
            for half in range(2):
                route.append((flat(s, *owner(block, half ^ flip)), flat(s, block, half)))
    return lax.ppermute(array, AXES, route)


def on_device(
    weight,
    adapter_down_map,
    adapter_up_map,
    gain,
    prior_epoch_input,
    prior_epoch_output,
    initial_step_inputs,
    initial_step_gradients,
    sample_numbers,
):
    del prior_epoch_output
    w = weight[0]
    gains = gain
    sections = lax.axis_size("section")
    toks, feats = initial_step_inputs.shape[1:]
    rank = adapter_up_map.shape[1]
    rows = 2 * toks

    mine = initial_step_inputs[0]
    theirs = lax.ppermute(mine, "dp", [(0, 1), (1, 0)])
    given = to_owner(initial_step_gradients[0], sections, 0)
    given_up = to_owner(adapter_up_map[0], sections, 0)
    stored = prior_epoch_input[0, 0]
    order = sample_numbers[0, 0]
    to_partner = [(flat(0, t, d), flat(0, t, 1 - d)) for t in range(2 * CHIPS) for d in range(2)]
    stored_theirs = lax.ppermute(stored, AXES, to_partner)
    order_theirs = lax.ppermute(order, AXES, to_partner)

    block = shape(rows, feats, dtype=BF)
    values = shape(rows, LANES)
    xs, all_stats, all_sums, grads = [], [], [], []
    for tick in range(TICKS):
        start = tick == 0
        more = 4 * CHIPS if start else 0
        out = [block, shape(CHIPS, rows + more, feats, dtype=BF), shape(rows + more, LANES)]
        if start:
            x, product, small, down = call(
                functools.partial(forward_kernel, True, tick),
                out + [shape(LANES, feats)],
                given,
                given_up,
                stored_theirs,
                mine,
                theirs,
                gains,
                w,
                adapter_down_map[0].T,
                scalars=(order_theirs,),
            )
        else:
            x, product, small = call(
                functools.partial(forward_kernel, False, tick),
                out,
                arrived,
                stored,
                stored_theirs,
                gains,
                w,
                down,
                scalars=(order, order_theirs),
            )
        width = feats // 2
        ins = [product, small, x]
        columns = (CHIPS + (1 if start else 2)) * width + LANES
        dealt = shape(rows + more, columns, dtype=BF)
        if start:
            dealt, up, grad_arrived = call(
                functools.partial(deal_kernel, True, sections),
                [dealt, shape(LANES, feats, dtype=BF), block],
                *ins,
                given,
                given_up,
            )
        else:
            dealt, grad_part = call(
                functools.partial(deal_kernel, False, sections),
                [dealt, block],
                *ins,
                grad_arrived,
                output,
            )
        ins.append(swap_cores(dealt))
        columns = (2 if start else 3) * width + LANES
        parcel = shape(CHIPS, rows + more, columns, dtype=BF)
        if start:
            parcel = call(functools.partial(pack_kernel, True), parcel, *ins)
        else:
            parcel, grad = call(
                functools.partial(pack_kernel, False),
                [parcel, shape(rows, width, dtype=BF)],
                *ins,
                grad_part,
                up,
                gain_w,
                mixed,
            )
            grads.append(grad)
        got = over_chips(parcel)
        columns = width + (0 if start else LANES + CHIPS * width)
        out = [shape(rows, columns, dtype=BF), shape(rows, width), values]
        kernel = functools.partial(output_kernel, start)
        if start:
            gain_w, gain_low, own, mixed, stats = call(
                kernel, [shape(2 * CHIPS, width), shape(2 * CHIPS, LANES)] + out, got, up
            )
        else:
            own, mixed, stats = call(kernel, out, got, up, gain_w, gain_low)
        other = swap_cores(own)
        output = call(whole_kernel, block, own, other)
        if tick < TICKS - 1:
            arrived = to_next(output, sections)
        if not start:
            grad_x, sums = call(
                backward_kernel,
                [block, values],
                own,
                other,
                xs[-1],
                all_stats[-1],
                gains,
                gain_low,
                w,
                down,
            )
            all_sums.append(sums)
            grad_arrived = to_owner(grad_x, sections, 1)
        xs.append(x)
        all_stats.append(stats)

    acc_down, acc_up = call(
        accumulate_kernel,
        [shape(rank, feats), shape(rank, feats // 2)],
        gains,
        grad_x,
        *xs[:-1],
        *all_stats[:-1],
        *all_sums,
        *grads,
    )
    acc_other = lax.ppermute(acc_down, "dp", [(0, 1), (1, 0)])
    turned, up_part = call(
        functools.partial(last_kernel, sections),
        [shape(4 * CHIPS, rank, 2 * LANES, dtype=BF), shape(rank, feats, dtype=BF)],
        grad_arrived,
        output,
        up,
        stats,
        acc_up,
        acc_other,
    )
    got = lax.all_to_all(turned, ("tensor", "dp"), 0, 0)
    grad_down, grad_up = call(
        finish_kernel,
        [shape(rank, feats, dtype=BF), shape(rank, feats, dtype=BF)],
        got,
        x,
        stats,
        gains,
        acc_down,
        acc_other,
        back_home(up_part, sections, 0),
        back_home(up_part, sections, 1),
    )
    return grad_down.T[None], grad_up[None]


def solution(mesh):
    in_specs = (
        P("section", "tensor", "dp"),
        P("section", "tensor", None),
        P("section", None, "tensor"),
        P("section", "tensor"),
        P("section", "dp", None, None, "tensor"),
        P("section", "dp", None, None, "tensor"),
        P("section", "dp", "tensor"),
        P("section", "dp", "tensor"),
        P("section", "dp", None),
    )
    out_specs = (P("section", "tensor", None), P("section", None, "tensor"))
    return jax.shard_map(
        on_device, mesh=mesh, in_specs=in_specs, out_specs=out_specs, check_vma=False
    )
```

```python
import functools

import jax
import jax.numpy as jnp
from jax import lax
from jax.experimental import pallas as pl
from jax.experimental.pallas import tpu as pltpu
from jax.sharding import PartitionSpec as P

TICKS = 4
CHIPS = 4
EPS = 1e-05
AXES = ("section", "tensor", "dp")
HIGHEST = lax.Precision.HIGHEST
BF = jnp.bfloat16
F32 = jnp.float32

LANES = 128
SQUARE = 8
LOW = 16
GRAD = 32
FIRST = 48
SECOND = 49


def flat(section, tensor, dp):
    return (section * 2 * CHIPS + tensor) * 2 + dp


def owner(block, core):
    return 2 * (block % CHIPS) + core, block // CHIPS


def to_owner(array, sections, back):
    route = []
    for s in range(sections):
        for block in range(2 * CHIPS):
            for half in range(2):
                if s - back >= 0:
                    route.append((flat(s, block, half), flat(s - back, *owner(block, half))))
    return lax.ppermute(array, AXES, route)


def to_next(array, sections):
    route = []
    for s in range(sections - 1):
        for block in range(2 * CHIPS):
            for half in range(2):
                route.append((flat(s, *owner(block, half)), flat(s + 1, block, half)))
    return lax.ppermute(array, AXES, route)


def swap_cores(array):
    return lax.ppermute(array, "tensor", [(i, i ^ 1) for i in range(2 * CHIPS)])


def over_chips(array):
    groups = [[2 * i for i in range(CHIPS)], [2 * i + 1 for i in range(CHIPS)]]
    return lax.all_to_all(array, "tensor", 0, 0, axis_index_groups=groups)


def dot(a, b, **kw):
    return jnp.dot(a, b, preferred_element_type=F32, **kw)


def dot_t(a, b, **kw):
    return lax.dot_general(a, b, (((1,), (1,)), ((), ())), preferred_element_type=F32, **kw)


def t_dot(a, b, **kw):
    return lax.dot_general(a, b, (((0,), (0,)), ((), ())), preferred_element_type=F32, **kw)


def lane(rows):
    return lax.broadcasted_iota(jnp.int32, (rows, LANES), 1)


def between(values, low, high):
    at = lane(values.shape[0])
    return jnp.where((at >= low) & (at < high), values, 0.0)


def pick(values, low, high):
    return jnp.sum(between(values, low, high), axis=1, keepdims=True)


def split(values):
    high = values.astype(BF).astype(F32)
    rest = pltpu.roll(values - high, LANES // 2, 1)
    return jnp.where(lane(values.shape[0]) < LANES // 2, high, rest).astype(BF)


def join(halves):
    wide = halves.astype(F32)
    return wide + pltpu.roll(wide, LANES // 2, 1)


def call(kernel, out, *args, scalars=(), vmem=16):
    return pl.pallas_call(
        kernel,
        out_shape=out,
        in_specs=[pl.BlockSpec(memory_space=pltpu.SMEM)] * len(scalars)
        + [pl.BlockSpec(memory_space=pltpu.VMEM)] * len(args),
        out_specs=jax.tree.map(lambda _: pl.BlockSpec(memory_space=pltpu.VMEM), out),
        compiler_params=pltpu.CompilerParams(vmem_limit_bytes=vmem * 2**20),
    )(*scalars, *args)


def shape(*dims, dtype=F32):
    return jax.ShapeDtypeStruct(dims, dtype)


def own_block():
    tensor = lax.axis_index("tensor")
    return jnp.where(tensor // CHIPS == lax.axis_index("dp"), tensor % CHIPS, -1)


def replicas(mine, theirs):
    first = lax.axis_index("dp") == 0
    return jnp.concatenate([jnp.where(first, mine, theirs), jnp.where(first, theirs, mine)])


def warm_kernel(w, gains, mine, down_rows, down):
    rank, feats = down_rows.shape
    down[:LOW] = jnp.zeros((LOW, feats), F32)
    down[LOW : LOW + rank] = down_rows[...].astype(F32)
    down[LOW + rank :] = jnp.zeros((LANES - LOW - rank, feats), F32)


def prepare_kernel(order, stored, grads, after, chosen, grads_out):
    for j in range(TICKS - 1):
        chosen[j] = jnp.where(order[j + 1] == 0, stored[0], stored[1])
    grads_out[...] = grads[...]


def forward_kernel(start, tick, *refs):
    place = lax.axis_index("tensor")
    if start:
        mine, theirs, gains, w, down, x_out, product, small = refs
        x = replicas(mine[...], theirs[...])
    else:
        arrived, mine, theirs, gains, w, down, x_out, product, small = refs
        given = replicas(mine[tick - 1], theirs[tick - 1])
        x = jnp.where(lax.axis_index("section") == 0, given, arrived[...])
    x_out[...] = x
    rows, feats = x.shape
    wide = x.astype(F32)
    mid = jnp.sum(wide, axis=1, keepdims=True) / feats
    centered = wide - mid
    square = jnp.sum(centered * centered, axis=1, keepdims=True)
    scaled = centered * gains[...]
    at = lane(rows)
    low = dot_t(scaled, down[...], precision=HIGHEST)
    low = jnp.where(at == place, mid, low)
    small[0:rows] = jnp.where(at == SQUARE + place, square, low)
    left = scaled.astype(BF)
    if start:
        row = lax.broadcasted_iota(jnp.int32, (2 * CHIPS, feats), 0)
        gain_rows = jnp.where(row == place, gains[...], 0.0)
        high = gain_rows.astype(BF).astype(F32)
        left = jnp.concatenate([left, jnp.concatenate([high, gain_rows - high]).astype(BF)])
        small[rows:] = jnp.concatenate(
            [dot_t(gain_rows, down[...], precision=HIGHEST), jnp.zeros((2 * CHIPS, LANES), F32)]
        )
    for j in range(CHIPS):
        part = dot(left, w[:, j * feats : (j + 1) * feats])
        if start:
            tail = part[rows : rows + 2 * CHIPS] + part[rows + 2 * CHIPS :]
            high = tail.astype(BF).astype(F32)
            part = jnp.concatenate([part[:rows], high, tail - high])
        product[j] = part.astype(BF)


def first_core():
    return lax.axis_index("tensor") % 2 == 0


def own_half(array):
    feats = array.shape[-1]
    return jnp.where(first_core(), array[..., : feats // 2], array[..., feats // 2 :])


def other_half(array):
    feats = array.shape[-1]
    return jnp.where(first_core(), array[..., feats // 2 :], array[..., : feats // 2])


def both_halves(mine, theirs):
    return jnp.concatenate(
        [jnp.where(first_core(), mine, theirs), jnp.where(first_core(), theirs, mine)], axis=-1
    )


def deal_kernel(tick, sections, product, small, x, *refs):
    rows, feats = x.shape
    width = feats // 2
    at = CHIPS * width
    if tick == 0:
        up, out = refs
        out[rows:, at : at + width] = other_half(up[...])
    else:
        arrived, output, out, grad_out = refs
        if tick == 1:
            given = arrived[...]
            zeros = jnp.zeros(given.shape, BF)
            given = jnp.concatenate(
                [jnp.where(first_core(), given, zeros), jnp.where(first_core(), zeros, given)]
            )
        else:
            given = arrived[...]
        kept = jnp.where(first_core(), output[...], jnp.zeros(output.shape, BF))
        grad = jnp.where(lax.axis_index("section") == sections - 1, kept, given)
        grad_out[...] = grad
        out[:, at + width + LANES :] = other_half(grad)
    for j in range(CHIPS):
        out[:, j * width : (j + 1) * width] = other_half(product[j])
    out[:rows, at : at + width] = other_half(x[...])
    out[:, at + width : at + width + LANES] = split(small[...])


def pack_kernel(start, product, small, x, theirs, *refs):
    rows, feats = x.shape
    width = feats // 2
    at = CHIPS * width
    mine_x = own_half(x[...])
    theirs_x = theirs[:rows, at : at + width]
    at = at + width
    values = join(split(small[...])) + join(theirs[:, at : at + LANES])
    values = between(values, 0, LANES // 2)
    if start:
        up, parcel = refs
        mine_x = jnp.concatenate([mine_x, own_half(up[...])])
        theirs_x = theirs[:, at - width : at]
    else:
        grad_part, up, gain_w, mixed, parcel, grad_out = refs
        grad = own_half(grad_part[...]).astype(F32) + theirs[:, at + LANES :].astype(F32)
        grad = grad.astype(BF)
        grad_out[...] = grad
        wide = grad.astype(F32)
        first = jnp.sum(wide * jnp.sum(gain_w[...], axis=0, keepdims=True), axis=1, keepdims=True)
        second = jnp.sum(wide * mixed[...], axis=1, keepdims=True)
        lanes = lane(rows)
        values = values + pltpu.roll(dot_t(grad, up[...]), GRAD - LOW, 1)
        values = jnp.where(lanes == FIRST, first, values)
        values = jnp.where(lanes == SECOND, second, values)
        for j in range(CHIPS):
            parcel[j, :, 2 * width + LANES :] = grad
    halves = split(values)
    block = own_block()
    for j in range(CHIPS):
        total = own_half(product[j]).astype(F32)
        total = total + theirs[:, j * width : (j + 1) * width].astype(F32)
        parcel[j, :, :width] = total.astype(BF)
        held = jnp.where(block == j, mine_x, jnp.where(block == (j ^ 1), theirs_x, 0.0).astype(BF))
        parcel[j, :, width : 2 * width] = held
        parcel[j, :, 2 * width : 2 * width + LANES] = halves


def output_kernel(start, got, up, gain_w, gain_low, out, mixed, stats):
    rows, width = mixed.shape
    feats = 2 * width
    total = got[0, :, :width].astype(F32)
    x = got[0, :, width:feats].astype(F32)
    values = join(got[0, :, feats : feats + LANES])
    for j in range(1, CHIPS):
        total = total + got[j, :, :width].astype(F32)
        x = x + got[j, :, width:feats].astype(F32)
        values = values + join(got[j, :, feats : feats + LANES])
    values = between(values, 0, LANES // 2)
    if start:
        gain_w[...] = total[rows : rows + 2 * CHIPS] + total[rows + 2 * CHIPS :]
        gain_low[...] = between(values[rows : rows + 2 * CHIPS], LOW, GRAD)
        up[:LOW] = jnp.zeros((LOW, width), BF)
        up[LOW:GRAD] = x[rows:].astype(BF)
        up[GRAD:] = jnp.zeros((LANES - GRAD, width), BF)
        total = total[:rows]
        values = values[:rows]
        x = x[:rows]
    at = lane(rows)
    mean = pick(values, 0, SQUARE) / (2 * CHIPS)
    off = jnp.where(at < 2 * CHIPS, values - mean, 0.0)
    square = pick(values, SQUARE, LOW) + feats * jnp.sum(off * off, axis=1, keepdims=True)
    inv = lax.rsqrt(square / (feats * 2 * CHIPS) + EPS)
    low = values
    for j in range(2 * CHIPS):
        total = total + off[:, j : j + 1] * gain_w[j : j + 1, :]
        low = low + off[:, j : j + 1] * gain_low[j : j + 1, :]
    total = inv * total
    low = between(inv * low, LOW, GRAD)
    mixed[...] = total
    stats[...] = jnp.where(at == 0, mean, jnp.where(at == 1, inv, low))
    out[:, :width] = (x + total + dot(low.astype(BF), up[...])).astype(BF)
    if not start:
        out[:, width : width + LANES] = split(values)
        for j in range(CHIPS):
            at = width + LANES + j * width
            out[:, at : at + width] = got[j, :, feats + LANES :]


def whole_kernel(mine, theirs, output):
    width = output.shape[1] // 2
    output[...] = both_halves(mine[:, :width], theirs[:, :width])


def rank_grads(sums):
    return pltpu.roll(between(sums, GRAD, FIRST), LANES - (GRAD - LOW), 1)


def normed(x, stats):
    return (x.astype(F32) - pick(stats, 0, 1)) * pick(stats, 1, 2)


def backward_kernel(mine, theirs, x, stats, gains, gain_low, w, down, grad_out, sums):
    rows, feats = x.shape
    width = feats * 2 * CHIPS
    half = feats // 2
    ends = slice(half, half + LANES)
    values = join(mine[:, ends]) + join(theirs[:, ends])
    sums[...] = values
    low_grad = rank_grads(values)
    low = between(stats[...], LOW, GRAD)
    low_all = jnp.sum(gain_low[...], axis=0, keepdims=True)
    first = pick(values, FIRST, FIRST + 1) + jnp.sum(low_grad * low_all, axis=1, keepdims=True)
    second = pick(values, SECOND, SECOND + 1) + jnp.sum(low_grad * low, axis=1, keepdims=True)
    xhat = normed(x[...], stats[...])
    grad_norm = dot(low_grad, down[...], precision=HIGHEST)
    here = jnp.zeros((rows, feats), F32)
    for j in range(CHIPS):
        at = half + LANES + j * half
        grad = both_halves(mine[:, at : at + half], theirs[:, at : at + half])
        grad_norm = grad_norm + dot_t(grad, w[:, j * feats : (j + 1) * feats])
        here = here + jnp.where(own_block() == j, grad.astype(F32), 0.0)
    inv = pick(stats[...], 1, 2)
    grad_x = here + inv * (grad_norm * gains[...] - first / width - xhat * (second / width))
    grad_out[...] = grad_x.astype(BF)


def accumulate_kernel(gains, after, *refs):
    count = TICKS - 1
    xs, stats, sums, grads = (refs[i * count : (i + 1) * count] for i in range(4))
    acc_down, acc_up = refs[4 * count :]
    rank = acc_up.shape[0]
    down, up = 0.0, 0.0
    for j in range(count):
        u = normed(xs[j][...], stats[j][...]) * gains[...]
        down = down + t_dot(rank_grads(sums[j][...]), u, precision=HIGHEST)
        up = up + t_dot(stats[j][...].astype(BF), grads[j][...])
    acc_down[...] = down[LOW : LOW + rank]
    acc_up[...] = up[LOW : LOW + rank]


def last_kernel(sections, arrived, output, up, stats, acc_up, after, out, up_out):
    rows, feats = arrived.shape
    rank = up.shape[0]
    kept = jnp.where(lax.axis_index("dp") == 0, output[...], jnp.zeros(output.shape, BF))
    grad = jnp.where(lax.axis_index("section") == sections - 1, kept, arrived[...])
    turned = dot_t(up[...], grad)
    turned = jnp.concatenate([turned, jnp.zeros((rank, LANES - rows), F32)], axis=1)
    high = turned.astype(BF).astype(F32)
    parcel = jnp.concatenate([high, turned - high, acc_up[...]], axis=1).astype(BF)
    for j in range(4 * CHIPS):
        out[j] = parcel
    low = t_dot(stats[...].astype(BF), grad)
    up_out[...] = low[LOW : LOW + rank].astype(BF)


def finish_kernel(got, x, stats, gains, mine, theirs, up_mine, up_theirs, down_out, up_out):
    rows = x.shape[0]
    turned = got[0, :, : 2 * LANES].astype(F32)
    for j in range(1, 4 * CHIPS):
        turned = turned + got[j, :, : 2 * LANES].astype(F32)
    low_grad = turned[:, :LANES] + turned[:, LANES:]
    u = normed(x[...], stats[...]) * gains[...]
    u = jnp.concatenate([u, jnp.zeros((LANES - rows, u.shape[1]), F32)])
    total = mine[...] + theirs[...] + dot(low_grad, u, precision=HIGHEST)
    down_out[...] = (total / rows).astype(BF)
    tensor = lax.axis_index("tensor")
    at = 4 * (tensor % CHIPS) + tensor // CHIPS
    total = jnp.concatenate([got[at, :, 2 * LANES :], got[at + 2, :, 2 * LANES :]], axis=1)
    total = total.astype(F32) + up_mine[...].astype(F32) + up_theirs[...].astype(F32)
    up_out[...] = (total / rows).astype(BF)


def to_same(array, sections):
    return lax.ppermute(array, "section", [(s, s - 1) for s in range(1, sections)])


def last_home(array, sections):
    s = sections - 1
    route = [(flat(s, *owner(block, 0)), flat(s, block, 0)) for block in range(2 * CHIPS)]
    return lax.ppermute(array, AXES, route)


def on_device(
    weight,
    adapter_down_map,
    adapter_up_map,
    gain,
    prior_epoch_input,
    prior_epoch_output,
    initial_step_inputs,
    initial_step_gradients,
    sample_numbers,
):
    del prior_epoch_output
    w = weight[0]
    gains = gain
    sections = lax.axis_size("section")
    toks, feats = initial_step_inputs.shape[1:]
    rank = adapter_up_map.shape[1]
    rows = 2 * toks

    mine = initial_step_inputs[0]
    theirs = lax.ppermute(mine, "dp", [(0, 1), (1, 0)])
    down = call(warm_kernel, shape(LANES, feats), w, gains, mine, adapter_down_map[0].T)

    block = shape(rows, feats, dtype=BF)
    values = shape(rows, LANES)
    xs, all_stats, all_sums, grads = [], [], [], []
    for tick in range(TICKS):
        start = tick == 0
        more = 4 * CHIPS if start else 0
        out = [block, shape(CHIPS, rows + more, feats, dtype=BF), shape(rows + more, LANES)]
        if start:
            x, product, small = call(
                functools.partial(forward_kernel, True, tick),
                out,
                mine,
                theirs,
                gains,
                w,
                down,
            )
        else:
            x, product, small = call(
                functools.partial(forward_kernel, False, tick),
                out,
                arrived,
                chosen,
                chosen_theirs,
                gains,
                w,
                down,
            )
        width = feats // 2
        ins = [product, small, x]
        columns = (CHIPS + (1 if start else 2)) * width + LANES
        dealt = shape(rows + more, columns, dtype=BF)
        if start:
            dealt = call(
                functools.partial(deal_kernel, tick, sections), dealt, *ins, adapter_up_map[0]
            )
        else:
            dealt, grad_part = call(
                functools.partial(deal_kernel, tick, sections),
                [dealt, block],
                *ins,
                grad_arrived,
                output,
            )
        ins.append(swap_cores(dealt))
        columns = (2 if start else 3) * width + LANES
        parcel = shape(CHIPS, rows + more, columns, dtype=BF)
        if start:
            parcel = call(functools.partial(pack_kernel, True), parcel, *ins, adapter_up_map[0])
        else:
            parcel, grad = call(
                functools.partial(pack_kernel, False),
                [parcel, shape(rows, width, dtype=BF)],
                *ins,
                grad_part,
                up,
                gain_w,
                mixed,
            )
            grads.append(grad)
        got = over_chips(parcel)
        columns = width + (0 if start else LANES + CHIPS * width)
        out = [shape(rows, columns, dtype=BF), shape(rows, width), values]
        kernel = functools.partial(output_kernel, start)
        if start:
            up = shape(LANES, width, dtype=BF)
            up, gain_w, gain_low, own, mixed, stats = call(
                kernel, [up, shape(2 * CHIPS, width), shape(2 * CHIPS, LANES)] + out, got
            )
        else:
            own, mixed, stats = call(kernel, out, got, up, gain_w, gain_low)
        other = swap_cores(own)
        output = call(whole_kernel, block, own, other)
        if tick < TICKS - 1:
            arrived = to_next(output, sections)
        if start:
            chosen, grads_out = call(
                prepare_kernel,
                [shape(TICKS - 1, toks, feats, dtype=BF), shape(toks, feats, dtype=BF)],
                prior_epoch_input[0, 0],
                initial_step_gradients[0],
                output,
                scalars=(sample_numbers[0, 0],),
            )
            grad_arrived = to_owner(grads_out, sections, 0)
            chosen_theirs = lax.ppermute(
                chosen,
                AXES,
                [(flat(0, t, d), flat(0, t, 1 - d)) for t in range(2 * CHIPS) for d in range(2)],
            )
        else:
            grad_x, sums = call(
                backward_kernel,
                [block, values],
                own,
                other,
                xs[-1],
                all_stats[-1],
                gains,
                gain_low,
                w,
                down,
            )
            all_sums.append(sums)
            if tick < TICKS - 1:
                grad_arrived = to_owner(grad_x, sections, 1)
            else:
                grad_arrived = to_same(grad_x, sections)
        xs.append(x)
        all_stats.append(stats)

    acc_down, acc_up = call(
        accumulate_kernel,
        [shape(rank, feats), shape(rank, feats // 2)],
        gains,
        grad_x,
        *xs[:-1],
        *all_stats[:-1],
        *all_sums,
        *grads,
    )
    acc_other = lax.ppermute(acc_down, "dp", [(0, 1), (1, 0)])
    parcel, up_part = call(
        functools.partial(last_kernel, sections),
        [
            shape(4 * CHIPS, rank, 2 * LANES + feats // 2, dtype=BF),
            shape(rank, feats, dtype=BF),
        ],
        grad_arrived,
        last_home(output, sections),
        adapter_up_map[0],
        stats,
        acc_up,
        acc_other,
    )
    got = lax.all_to_all(parcel, ("tensor", "dp"), 0, 0)
    grad_down, grad_up = call(
        finish_kernel,
        [shape(rank, feats, dtype=BF), shape(rank, feats, dtype=BF)],
        got,
        x,
        stats,
        gains,
        acc_down,
        acc_other,
        up_part,
        lax.ppermute(up_part, "dp", [(0, 1), (1, 0)]),
    )
    return grad_down.T[None], grad_up[None]


def solution(mesh):
    in_specs = (
        P("section", "tensor", "dp"),
        P("section", "tensor", None),
        P("section", None, "tensor"),
        P("section", "tensor"),
        P("section", "dp", None, None, "tensor"),
        P("section", "dp", None, None, "tensor"),
        P("section", "dp", "tensor"),
        P("section", "dp", "tensor"),
        P("section", "dp", None),
    )
    out_specs = (P("section", "tensor", None), P("section", None, "tensor"))
    return jax.shard_map(
        on_device, mesh=mesh, in_specs=in_specs, out_specs=out_specs, check_vma=False
    )
```

```python
import functools

import jax
import jax.numpy as jnp
from jax import lax
from jax.experimental import pallas as pl
from jax.experimental.pallas import tpu as pltpu
from jax.sharding import PartitionSpec as P

TICKS = 4
CHIPS = 4
EPS = 1e-05
AXES = ("section", "tensor", "dp")
HIGHEST = lax.Precision.HIGHEST
BF = jnp.bfloat16
F32 = jnp.float32

LANES = 128
SQUARE = 8
LOW = 16
GRAD = 32
FIRST = 48
SECOND = 49


def flat(section, tensor, dp):
    return (section * 2 * CHIPS + tensor) * 2 + dp


def owner(block, core):
    return 2 * (block % CHIPS) + core, block // CHIPS


def to_owner(array, sections, back):
    route = []
    for s in range(sections):
        for block in range(2 * CHIPS):
            for half in range(2):
                if s - back >= 0:
                    route.append((flat(s, block, half), flat(s - back, *owner(block, half))))
    return lax.ppermute(array, AXES, route)


def to_next(array, sections, flip):
    route = []
    for s in range(sections - 1):
        for block in range(2 * CHIPS):
            for half in range(2):
                route.append((flat(s, *owner(block, half ^ flip)), flat(s + 1, block, half)))
    return lax.ppermute(array, AXES, route)


def swap_cores(array):
    return lax.ppermute(array, "tensor", [(i, i ^ 1) for i in range(2 * CHIPS)])


def over_chips(array):
    groups = [[2 * i for i in range(CHIPS)], [2 * i + 1 for i in range(CHIPS)]]
    return lax.all_to_all(array, "tensor", 0, 0, axis_index_groups=groups)


def dot(a, b, **kw):
    return jnp.dot(a, b, preferred_element_type=F32, **kw)


def dot_t(a, b, **kw):
    return lax.dot_general(a, b, (((1,), (1,)), ((), ())), preferred_element_type=F32, **kw)


def t_dot(a, b, **kw):
    return lax.dot_general(a, b, (((0,), (0,)), ((), ())), preferred_element_type=F32, **kw)


def lane(rows):
    return lax.broadcasted_iota(jnp.int32, (rows, LANES), 1)


def between(values, low, high):
    at = lane(values.shape[0])
    return jnp.where((at >= low) & (at < high), values, 0.0)


def pick(values, low, high):
    return jnp.sum(between(values, low, high), axis=1, keepdims=True)


def split(values):
    high = values.astype(BF).astype(F32)
    rest = pltpu.roll(values - high, LANES // 2, 1)
    return jnp.where(lane(values.shape[0]) < LANES // 2, high, rest).astype(BF)


def join(halves):
    wide = halves.astype(F32)
    return wide + pltpu.roll(wide, LANES // 2, 1)


def call(kernel, out, *args, scalars=(), vmem=16):
    return pl.pallas_call(
        kernel,
        out_shape=out,
        in_specs=[pl.BlockSpec(memory_space=pltpu.SMEM)] * len(scalars)
        + [pl.BlockSpec(memory_space=pltpu.VMEM)] * len(args),
        out_specs=jax.tree.map(lambda _: pl.BlockSpec(memory_space=pltpu.VMEM), out),
        compiler_params=pltpu.CompilerParams(vmem_limit_bytes=vmem * 2**20),
    )(*scalars, *args)


def shape(*dims, dtype=F32):
    return jax.ShapeDtypeStruct(dims, dtype)


def own_block():
    tensor = lax.axis_index("tensor")
    return jnp.where(tensor // CHIPS == lax.axis_index("dp"), tensor % CHIPS, -1)


def replicas(mine, theirs):
    first = lax.axis_index("dp") == 0
    return jnp.concatenate([jnp.where(first, mine, theirs), jnp.where(first, theirs, mine)])


def warm_kernel(w, gains, mine, down_rows, down):
    rank, feats = down_rows.shape
    down[:LOW] = jnp.zeros((LOW, feats), F32)
    down[LOW : LOW + rank] = down_rows[...].astype(F32)
    down[LOW + rank :] = jnp.zeros((LANES - LOW - rank, feats), F32)


def prepare_kernel(order, stored, grads, after, chosen, grads_out):
    for j in range(TICKS - 1):
        chosen[j] = jnp.where(order[j + 1] == 0, stored[0], stored[1])
    grads_out[...] = grads[...]


def forward_kernel(start, tick, *refs):
    place = lax.axis_index("tensor")
    if start:
        mine, theirs, gains, w, down, x_out, product, small = refs
        x = replicas(mine[...], theirs[...])
    else:
        near, far, mine, theirs, gains, w, down, x_out, product, small = refs
        given = replicas(mine[tick - 1], theirs[tick - 1])
        first = lax.axis_index("dp") == 0
        arrived = jnp.concatenate(
            [jnp.where(first, near[...], far[...]), jnp.where(first, far[...], near[...])], axis=1
        )
        x = jnp.where(lax.axis_index("section") == 0, given, arrived)
    x_out[...] = x
    rows, feats = x.shape
    wide = x.astype(F32)
    mid = jnp.sum(wide, axis=1, keepdims=True) / feats
    centered = wide - mid
    square = jnp.sum(centered * centered, axis=1, keepdims=True)
    scaled = centered * gains[...]
    at = lane(rows)
    low = dot_t(scaled, down[...], precision=HIGHEST)
    low = jnp.where(at == place, mid, low)
    small[0:rows] = jnp.where(at == SQUARE + place, square, low)
    left = scaled.astype(BF)
    if start:
        row = lax.broadcasted_iota(jnp.int32, (2 * CHIPS, feats), 0)
        gain_rows = jnp.where(row == place, gains[...], 0.0)
        high = gain_rows.astype(BF).astype(F32)
        left = jnp.concatenate([left, jnp.concatenate([high, gain_rows - high]).astype(BF)])
        small[rows:] = jnp.concatenate(
            [dot_t(gain_rows, down[...], precision=HIGHEST), jnp.zeros((2 * CHIPS, LANES), F32)]
        )
    for j in range(CHIPS):
        part = dot(left, w[:, j * feats : (j + 1) * feats])
        if start:
            tail = part[rows : rows + 2 * CHIPS] + part[rows + 2 * CHIPS :]
            high = tail.astype(BF).astype(F32)
            part = jnp.concatenate([part[:rows], high, tail - high])
        product[j] = part.astype(BF)


def first_core():
    return lax.axis_index("tensor") % 2 == 0


def own_half(array):
    feats = array.shape[-1]
    return jnp.where(first_core(), array[..., : feats // 2], array[..., feats // 2 :])


def other_half(array):
    feats = array.shape[-1]
    return jnp.where(first_core(), array[..., feats // 2 :], array[..., : feats // 2])


def both_halves(mine, theirs):
    return jnp.concatenate(
        [jnp.where(first_core(), mine, theirs), jnp.where(first_core(), theirs, mine)], axis=-1
    )


def deal_kernel(tick, sections, product, small, x, *refs):
    rows, feats = x.shape
    width = feats // 2
    at = CHIPS * width
    if tick == 0:
        up, out = refs
        out[rows:, at : at + width] = other_half(up[...])
    else:
        arrived, output, out, grad_out = refs
        if tick == 1:
            given = arrived[...]
            zeros = jnp.zeros(given.shape, BF)
            given = jnp.concatenate(
                [jnp.where(first_core(), given, zeros), jnp.where(first_core(), zeros, given)]
            )
        else:
            given = arrived[...]
        zeros = jnp.zeros(output.shape, BF)
        kept = jnp.concatenate(
            [jnp.where(first_core(), output[...], zeros), jnp.where(first_core(), zeros, output[...])],
            axis=1,
        )
        grad = jnp.where(lax.axis_index("section") == sections - 1, kept, given)
        grad_out[...] = grad
        out[:, at + width + LANES :] = other_half(grad)
    for j in range(CHIPS):
        out[:, j * width : (j + 1) * width] = other_half(product[j])
    out[:rows, at : at + width] = other_half(x[...])
    out[:, at + width : at + width + LANES] = split(small[...])


def pack_kernel(start, product, small, x, theirs, *refs):
    rows, feats = x.shape
    width = feats // 2
    at = CHIPS * width
    mine_x = own_half(x[...])
    theirs_x = theirs[:rows, at : at + width]
    at = at + width
    values = join(split(small[...])) + join(theirs[:, at : at + LANES])
    values = between(values, 0, LANES // 2)
    if start:
        up, parcel = refs
        mine_x = jnp.concatenate([mine_x, own_half(up[...])])
        theirs_x = theirs[:, at - width : at]
    else:
        grad_part, up, gain_w, mixed, parcel, grad_out = refs
        grad = own_half(grad_part[...]).astype(F32) + theirs[:, at + LANES :].astype(F32)
        grad = grad.astype(BF)
        grad_out[...] = grad
        wide = grad.astype(F32)
        first = jnp.sum(wide * jnp.sum(gain_w[...], axis=0, keepdims=True), axis=1, keepdims=True)
        second = jnp.sum(wide * mixed[...], axis=1, keepdims=True)
        lanes = lane(rows)
        values = values + pltpu.roll(dot_t(grad, up[...]), GRAD - LOW, 1)
        values = jnp.where(lanes == FIRST, first, values)
        values = jnp.where(lanes == SECOND, second, values)
        for j in range(CHIPS):
            parcel[j, :, 2 * width + LANES :] = grad
    halves = split(values)
    block = own_block()
    for j in range(CHIPS):
        total = own_half(product[j]).astype(F32)
        total = total + theirs[:, j * width : (j + 1) * width].astype(F32)
        parcel[j, :, :width] = total.astype(BF)
        held = jnp.where(block == j, mine_x, jnp.where(block == (j ^ 1), theirs_x, 0.0).astype(BF))
        parcel[j, :, width : 2 * width] = held
        parcel[j, :, 2 * width : 2 * width + LANES] = halves


def output_kernel(start, got, up, gain_w, gain_low, out, mixed, stats, *rest):
    rows, width = mixed.shape
    feats = 2 * width
    total = got[0, :, :width].astype(F32)
    x = got[0, :, width:feats].astype(F32)
    values = join(got[0, :, feats : feats + LANES])
    for j in range(1, CHIPS):
        total = total + got[j, :, :width].astype(F32)
        x = x + got[j, :, width:feats].astype(F32)
        values = values + join(got[j, :, feats : feats + LANES])
    values = between(values, 0, LANES // 2)
    if start:
        gain_w[...] = total[rows : rows + 2 * CHIPS] + total[rows + 2 * CHIPS :]
        gain_low[...] = between(values[rows : rows + 2 * CHIPS], LOW, GRAD)
        up[:LOW] = jnp.zeros((LOW, width), BF)
        up[LOW:GRAD] = x[rows:].astype(BF)
        up[GRAD:] = jnp.zeros((LANES - GRAD, width), BF)
        total = total[:rows]
        values = values[:rows]
        x = x[:rows]
    at = lane(rows)
    mean = pick(values, 0, SQUARE) / (2 * CHIPS)
    off = jnp.where(at < 2 * CHIPS, values - mean, 0.0)
    square = pick(values, SQUARE, LOW) + feats * jnp.sum(off * off, axis=1, keepdims=True)
    inv = lax.rsqrt(square / (feats * 2 * CHIPS) + EPS)
    low = values
    for j in range(2 * CHIPS):
        total = total + off[:, j : j + 1] * gain_w[j : j + 1, :]
        low = low + off[:, j : j + 1] * gain_low[j : j + 1, :]
    total = inv * total
    low = between(inv * low, LOW, GRAD)
    mixed[...] = total
    stats[...] = jnp.where(at == 0, mean, jnp.where(at == 1, inv, low))
    out[...] = (x + total + dot(low.astype(BF), up[...])).astype(BF)
    if not start:
        (out,) = rest
        out[:, :LANES] = split(values)
        for j in range(CHIPS):
            at = LANES + j * width
            out[:, at : at + width] = got[j, :, feats + LANES :]


def rank_grads(sums):
    return pltpu.roll(between(sums, GRAD, FIRST), LANES - (GRAD - LOW), 1)


def normed(x, stats):
    return (x.astype(F32) - pick(stats, 0, 1)) * pick(stats, 1, 2)


def backward_kernel(mine, theirs, x, stats, gains, gain_low, w, down, grad_out, sums):
    rows, feats = x.shape
    width = feats * 2 * CHIPS
    half = feats // 2
    values = join(mine[:, :LANES]) + join(theirs[:, :LANES])
    sums[...] = values
    low_grad = rank_grads(values)
    low = between(stats[...], LOW, GRAD)
    low_all = jnp.sum(gain_low[...], axis=0, keepdims=True)
    first = pick(values, FIRST, FIRST + 1) + jnp.sum(low_grad * low_all, axis=1, keepdims=True)
    second = pick(values, SECOND, SECOND + 1) + jnp.sum(low_grad * low, axis=1, keepdims=True)
    xhat = normed(x[...], stats[...])
    grad_norm = dot(low_grad, down[...], precision=HIGHEST)
    here = jnp.zeros((rows, feats), F32)
    for j in range(CHIPS):
        at = LANES + j * half
        grad = both_halves(mine[:, at : at + half], theirs[:, at : at + half])
        grad_norm = grad_norm + dot_t(grad, w[:, j * feats : (j + 1) * feats])
        here = here + jnp.where(own_block() == j, grad.astype(F32), 0.0)
    inv = pick(stats[...], 1, 2)
    grad_x = here + inv * (grad_norm * gains[...] - first / width - xhat * (second / width))
    grad_out[...] = grad_x.astype(BF)


def accumulate_kernel(gains, after, *refs):
    count = TICKS - 1
    xs, stats, sums, grads = (refs[i * count : (i + 1) * count] for i in range(4))
    acc_down, acc_up = refs[4 * count :]
    rank = acc_up.shape[0]
    down, up = 0.0, 0.0
    for j in range(count):
        u = normed(xs[j][...], stats[j][...]) * gains[...]
        down = down + t_dot(rank_grads(sums[j][...]), u, precision=HIGHEST)
        up = up + t_dot(stats[j][...].astype(BF), grads[j][...])
    acc_down[...] = down[LOW : LOW + rank]
    acc_up[...] = up[LOW : LOW + rank]


def last_kernel(sections, arrived, output, up, stats, acc_up, acc_down, out, part):
    rows, feats = arrived.shape
    rank = up.shape[0]
    first = lax.axis_index("dp") == 0
    zeros = jnp.zeros(output.shape, BF)
    kept = jnp.concatenate(
        [jnp.where(first, output[...], zeros), jnp.where(first, zeros, output[...])], axis=1
    )
    grad = jnp.where(lax.axis_index("section") == sections - 1, kept, arrived[...])
    turned = dot_t(up[...], grad)
    turned = jnp.concatenate([turned, jnp.zeros((rank, LANES - rows), F32)], axis=1)
    high = turned.astype(BF).astype(F32)
    parcel = jnp.concatenate([high, turned - high, acc_up[...]], axis=1).astype(BF)
    for j in range(4 * CHIPS):
        out[j] = parcel
    low = t_dot(stats[...].astype(BF), grad)
    part[:rank] = low[LOW : LOW + rank].astype(BF)
    high = acc_down[...].astype(BF)
    part[rank : 2 * rank] = high
    part[2 * rank :] = (acc_down[...] - high.astype(F32)).astype(BF)


def finish_kernel(got, x, stats, gains, mine, theirs, down_out, up_out):
    rows = x.shape[0]
    turned = got[0, :, : 2 * LANES].astype(F32)
    for j in range(1, 4 * CHIPS):
        turned = turned + got[j, :, : 2 * LANES].astype(F32)
    low_grad = turned[:, :LANES] + turned[:, LANES:]
    u = normed(x[...], stats[...]) * gains[...]
    u = jnp.concatenate([u, jnp.zeros((LANES - rows, u.shape[1]), F32)])
    rank = up_out.shape[0]
    total = dot(low_grad, u, precision=HIGHEST)
    for part in (mine, theirs):
        total = total + part[rank : 2 * rank].astype(F32) + part[2 * rank :].astype(F32)
    down_out[...] = (total / rows).astype(BF)
    tensor = lax.axis_index("tensor")
    at = 4 * (tensor % CHIPS) + tensor // CHIPS
    total = jnp.concatenate([got[at, :, 2 * LANES :], got[at + 2, :, 2 * LANES :]], axis=1)
    total = total.astype(F32) + mine[:rank].astype(F32) + theirs[:rank].astype(F32)
    up_out[...] = (total / rows).astype(BF)


def to_same(array, sections):
    return lax.ppermute(array, "section", [(s, s - 1) for s in range(1, sections)])


def last_home(array, sections):
    s = sections - 1
    route = [
        (flat(s, *owner(block, half)), flat(s, block, half))
        for block in range(2 * CHIPS)
        for half in range(2)
    ]
    return lax.ppermute(array, AXES, route)


def on_device(
    weight,
    adapter_down_map,
    adapter_up_map,
    gain,
    prior_epoch_input,
    prior_epoch_output,
    initial_step_inputs,
    initial_step_gradients,
    sample_numbers,
):
    del prior_epoch_output
    w = weight[0]
    gains = gain
    sections = lax.axis_size("section")
    toks, feats = initial_step_inputs.shape[1:]
    rank = adapter_up_map.shape[1]
    rows = 2 * toks

    mine = initial_step_inputs[0]
    theirs = lax.ppermute(mine, "dp", [(0, 1), (1, 0)])
    down = call(warm_kernel, shape(LANES, feats), w, gains, mine, adapter_down_map[0].T)

    block = shape(rows, feats, dtype=BF)
    values = shape(rows, LANES)
    xs, all_stats, all_sums, grads = [], [], [], []
    for tick in range(TICKS):
        start = tick == 0
        more = 4 * CHIPS if start else 0
        out = [block, shape(CHIPS, rows + more, feats, dtype=BF), shape(rows + more, LANES)]
        if start:
            x, product, small = call(
                functools.partial(forward_kernel, True, tick),
                out,
                mine,
                theirs,
                gains,
                w,
                down,
            )
        else:
            x, product, small = call(
                functools.partial(forward_kernel, False, tick),
                out,
                *arrived,
                chosen,
                chosen_theirs,
                gains,
                w,
                down,
            )
        width = feats // 2
        ins = [product, small, x]
        columns = (CHIPS + (1 if start else 2)) * width + LANES
        dealt = shape(rows + more, columns, dtype=BF)
        if start:
            dealt = call(
                functools.partial(deal_kernel, tick, sections), dealt, *ins, adapter_up_map[0]
            )
        else:
            dealt, grad_part = call(
                functools.partial(deal_kernel, tick, sections),
                [dealt, block],
                *ins,
                grad_arrived,
                output,
            )
        ins.append(swap_cores(dealt))
        columns = (2 if start else 3) * width + LANES
        parcel = shape(CHIPS, rows + more, columns, dtype=BF)
        if start:
            parcel = call(functools.partial(pack_kernel, True), parcel, *ins, adapter_up_map[0])
        else:
            parcel, grad = call(
                functools.partial(pack_kernel, False),
                [parcel, shape(rows, width, dtype=BF)],
                *ins,
                grad_part,
                up,
                gain_w,
                mixed,
            )
            grads.append(grad)
        got = over_chips(parcel)
        out = [shape(rows, width, dtype=BF), shape(rows, width), values]
        kernel = functools.partial(output_kernel, start)
        if start:
            up = shape(LANES, width, dtype=BF)
            up, gain_w, gain_low, output, mixed, stats = call(
                kernel, [up, shape(2 * CHIPS, width), shape(2 * CHIPS, LANES)] + out, got
            )
        else:
            out.append(shape(rows, LANES + CHIPS * width, dtype=BF))
            output, mixed, stats, own = call(kernel, out, got, up, gain_w, gain_low)
            other = swap_cores(own)
        if tick < TICKS - 1:
            arrived = [to_next(output, sections, flip) for flip in range(2)]
        if start:
            chosen, grads_out = call(
                prepare_kernel,
                [shape(TICKS - 1, toks, feats, dtype=BF), shape(toks, feats, dtype=BF)],
                prior_epoch_input[0, 0],
                initial_step_gradients[0],
                output,
                scalars=(sample_numbers[0, 0],),
            )
            grad_arrived = to_owner(grads_out, sections, 0)
            chosen_theirs = lax.ppermute(
                chosen,
                AXES,
                [(flat(0, t, d), flat(0, t, 1 - d)) for t in range(2 * CHIPS) for d in range(2)],
            )
        else:
            grad_x, sums = call(
                backward_kernel,
                [block, values],
                own,
                other,
                xs[-1],
                all_stats[-1],
                gains,
                gain_low,
                w,
                down,
            )
            all_sums.append(sums)
            if tick < TICKS - 1:
                grad_arrived = to_owner(grad_x, sections, 1)
            else:
                grad_arrived = to_same(grad_x, sections)
        xs.append(x)
        all_stats.append(stats)

    acc_down, acc_up = call(
        accumulate_kernel,
        [shape(rank, feats), shape(rank, feats // 2)],
        gains,
        grad_x,
        *xs[:-1],
        *all_stats[:-1],
        *all_sums,
        *grads,
    )
    parcel, part = call(
        functools.partial(last_kernel, sections),
        [
            shape(4 * CHIPS, rank, 2 * LANES + feats // 2, dtype=BF),
            shape(3 * rank, feats, dtype=BF),
        ],
        grad_arrived,
        last_home(output, sections),
        adapter_up_map[0],
        stats,
        acc_up,
        acc_down,
    )
    got = lax.all_to_all(parcel, ("tensor", "dp"), 0, 0)
    grad_down, grad_up = call(
        finish_kernel,
        [shape(rank, feats, dtype=BF), shape(rank, feats, dtype=BF)],
        got,
        x,
        stats,
        gains,
        part,
        lax.ppermute(part, "dp", [(0, 1), (1, 0)]),
    )
    return grad_down.T[None], grad_up[None]


def solution(mesh):
    in_specs = (
        P("section", "tensor", "dp"),
        P("section", "tensor", None),
        P("section", None, "tensor"),
        P("section", "tensor"),
        P("section", "dp", None, None, "tensor"),
        P("section", "dp", None, None, "tensor"),
        P("section", "dp", "tensor"),
        P("section", "dp", "tensor"),
        P("section", "dp", None),
    )
    out_specs = (P("section", "tensor", None), P("section", None, "tensor"))
    return jax.shard_map(
        on_device, mesh=mesh, in_specs=in_specs, out_specs=out_specs, check_vma=False
    )
```

```python
import functools

import jax
import jax.numpy as jnp
from jax import lax
from jax.experimental import pallas as pl
from jax.experimental.pallas import tpu as pltpu
from jax.sharding import PartitionSpec as P

TICKS = 4
CHIPS = 4
EPS = 1e-05
AXES = ("section", "tensor", "dp")
HIGHEST = lax.Precision.HIGHEST
BF = jnp.bfloat16
F32 = jnp.float32

LANES = 128
SQUARE = 8
LOW = 16
GRAD = 32
FIRST = 48
SECOND = 49


def flat(section, tensor, dp):
    return (section * 2 * CHIPS + tensor) * 2 + dp


OWNER = (0, 3, 1, 2, 2, 1, 3, 0)


def owner(block, core):
    return 2 * OWNER[block] + core, block // CHIPS


def look_up(table, at):
    return sum(jnp.where(at == i, value, 0) for i, value in enumerate(table))


def owner_chip(block):
    mine = block // CHIPS == lax.axis_index("dp")
    return jnp.where(mine, look_up(OWNER, block), -1)


def block_of(chip):
    half = lax.axis_index("dp")
    return jnp.where(half == 0, OWNER[:CHIPS].index(chip), OWNER[CHIPS:].index(chip))


def to_owner(array, sections, back):
    route = []
    for s in range(sections):
        for block in range(2 * CHIPS):
            for half in range(2):
                if s - back >= 0:
                    route.append((flat(s, block, half), flat(s - back, *owner(block, half))))
    return lax.ppermute(array, AXES, route)


def to_next(array, sections):
    route = []
    for s in range(sections - 1):
        for block in range(2 * CHIPS):
            for half in range(2):
                route.append((flat(s, *owner(block, half)), flat(s + 1, block, half)))
    return lax.ppermute(array, AXES, route)


def swap_cores(array):
    return lax.ppermute(array, "tensor", [(i, i ^ 1) for i in range(2 * CHIPS)])


def over_chips(array):
    groups = [[2 * i for i in range(CHIPS)], [2 * i + 1 for i in range(CHIPS)]]
    return lax.all_to_all(array, "tensor", 0, 0, axis_index_groups=groups)


def dot(a, b, **kw):
    return jnp.dot(a, b, preferred_element_type=F32, **kw)


def dot_t(a, b, **kw):
    return lax.dot_general(a, b, (((1,), (1,)), ((), ())), preferred_element_type=F32, **kw)


def t_dot(a, b, **kw):
    return lax.dot_general(a, b, (((0,), (0,)), ((), ())), preferred_element_type=F32, **kw)


def lane(rows):
    return lax.broadcasted_iota(jnp.int32, (rows, LANES), 1)


def between(values, low, high):
    at = lane(values.shape[0])
    return jnp.where((at >= low) & (at < high), values, 0.0)


def pick(values, low, high):
    return jnp.sum(between(values, low, high), axis=1, keepdims=True)


def split(values):
    high = values.astype(BF).astype(F32)
    rest = pltpu.roll(values - high, LANES // 2, 1)
    return jnp.where(lane(values.shape[0]) < LANES // 2, high, rest).astype(BF)


def join(halves):
    wide = halves.astype(F32)
    return wide + pltpu.roll(wide, LANES // 2, 1)


def call(kernel, out, *args, scalars=(), vmem=16):
    return pl.pallas_call(
        kernel,
        out_shape=out,
        in_specs=[pl.BlockSpec(memory_space=pltpu.SMEM)] * len(scalars)
        + [pl.BlockSpec(memory_space=pltpu.VMEM)] * len(args),
        out_specs=jax.tree.map(lambda _: pl.BlockSpec(memory_space=pltpu.VMEM), out),
        compiler_params=pltpu.CompilerParams(vmem_limit_bytes=vmem * 2**20),
    )(*scalars, *args)


def shape(*dims, dtype=F32):
    return jax.ShapeDtypeStruct(dims, dtype)


def replicas(mine, theirs):
    first = lax.axis_index("dp") == 0
    return jnp.concatenate([jnp.where(first, mine, theirs), jnp.where(first, theirs, mine)])


def warm_kernel(w, gains, mine, down_rows, down):
    rank, feats = down_rows.shape
    down[:LOW] = jnp.zeros((LOW, feats), F32)
    down[LOW : LOW + rank] = down_rows[...].astype(F32)
    down[LOW + rank :] = jnp.zeros((LANES - LOW - rank, feats), F32)


def prepare_kernel(order, stored, grads, after, chosen, grads_out):
    for j in range(TICKS - 1):
        chosen[j] = jnp.where(order[j + 1] == 0, stored[0], stored[1])
    grads_out[...] = grads[...]


def forward_kernel(start, tick, *refs):
    place = lax.axis_index("tensor")
    if start:
        mine, theirs, gains, w, down, x_out, product, small = refs
        x = replicas(mine[...], theirs[...])
    else:
        arrived, mine, theirs, gains, w, down, x_out, product, small = refs
        given = replicas(mine[tick - 1], theirs[tick - 1])
        x = jnp.where(lax.axis_index("section") == 0, given, arrived[...])
    x_out[...] = x
    rows, feats = x.shape
    wide = x.astype(F32)
    mid = jnp.sum(wide, axis=1, keepdims=True) / feats
    centered = wide - mid
    square = jnp.sum(centered * centered, axis=1, keepdims=True)
    scaled = centered * gains[...]
    at = lane(rows)
    low = dot_t(scaled, down[...], precision=HIGHEST)
    low = jnp.where(at == place, mid, low)
    small[0:rows] = jnp.where(at == SQUARE + place, square, low)
    left = scaled.astype(BF)
    if start:
        row = lax.broadcasted_iota(jnp.int32, (2 * CHIPS, feats), 0)
        gain_rows = jnp.where(row == place, gains[...], 0.0)
        high = gain_rows.astype(BF).astype(F32)
        left = jnp.concatenate([left, jnp.concatenate([high, gain_rows - high]).astype(BF)])
        small[rows:] = jnp.concatenate(
            [dot_t(gain_rows, down[...], precision=HIGHEST), jnp.zeros((2 * CHIPS, LANES), F32)]
        )
    for j in range(CHIPS):
        part = dot(left, w[:, j * feats : (j + 1) * feats])
        if start:
            tail = part[rows : rows + 2 * CHIPS] + part[rows + 2 * CHIPS :]
            high = tail.astype(BF).astype(F32)
            part = jnp.concatenate([part[:rows], high, tail - high])
        slot = jnp.where(lax.axis_index("dp") == 0, OWNER[j], OWNER[CHIPS + j])
        product[slot] = part.astype(BF)


def first_core():
    return lax.axis_index("tensor") % 2 == 0


def own_half(array):
    feats = array.shape[-1]
    return jnp.where(first_core(), array[..., : feats // 2], array[..., feats // 2 :])


def other_half(array):
    feats = array.shape[-1]
    return jnp.where(first_core(), array[..., feats // 2 :], array[..., : feats // 2])


def both_halves(mine, theirs):
    return jnp.concatenate(
        [jnp.where(first_core(), mine, theirs), jnp.where(first_core(), theirs, mine)], axis=-1
    )


def deal_kernel(tick, sections, product, small, x, *refs):
    rows, feats = x.shape
    width = feats // 2
    at = CHIPS * width
    if tick == 0:
        up, out = refs
        out[rows:, at : at + width] = other_half(up[...])
    else:
        arrived, output, out, grad_out = refs
        if tick == 1:
            given = arrived[...]
            zeros = jnp.zeros(given.shape, BF)
            given = jnp.concatenate(
                [jnp.where(first_core(), given, zeros), jnp.where(first_core(), zeros, given)]
            )
        else:
            given = arrived[...]
        kept = jnp.where(first_core(), output[...], jnp.zeros(output.shape, BF))
        grad = jnp.where(lax.axis_index("section") == sections - 1, kept, given)
        grad_out[...] = grad
        out[:, at + width + LANES :] = other_half(grad)
    for j in range(CHIPS):
        out[:, j * width : (j + 1) * width] = other_half(product[j])
    out[:rows, at : at + width] = other_half(x[...])
    out[:, at + width : at + width + LANES] = split(small[...])


def pack_kernel(start, product, small, x, theirs, *refs):
    rows, feats = x.shape
    width = feats // 2
    at = CHIPS * width
    mine_x = own_half(x[...])
    theirs_x = theirs[:rows, at : at + width]
    at = at + width
    values = join(split(small[...])) + join(theirs[:, at : at + LANES])
    values = between(values, 0, LANES // 2)
    if start:
        up, parcel = refs
        mine_x = jnp.concatenate([mine_x, own_half(up[...])])
        theirs_x = theirs[:, at - width : at]
    else:
        grad_part, up, gain_w, mixed, parcel, grad_out = refs
        grad = own_half(grad_part[...]).astype(F32) + theirs[:, at + LANES :].astype(F32)
        grad = grad.astype(BF)
        grad_out[...] = grad
        wide = grad.astype(F32)
        first = jnp.sum(wide * jnp.sum(gain_w[...], axis=0, keepdims=True), axis=1, keepdims=True)
        second = jnp.sum(wide * mixed[...], axis=1, keepdims=True)
        lanes = lane(rows)
        values = values + pltpu.roll(dot_t(grad, up[...]), GRAD - LOW, 1)
        values = jnp.where(lanes == FIRST, first, values)
        values = jnp.where(lanes == SECOND, second, values)
        for j in range(CHIPS):
            parcel[j, :, 2 * width + LANES :] = grad
    halves = split(values)
    tensor = lax.axis_index("tensor")
    mine_at, theirs_at = owner_chip(tensor), owner_chip(tensor ^ 1)
    for j in range(CHIPS):
        total = own_half(product[j]).astype(F32)
        total = total + theirs[:, j * width : (j + 1) * width].astype(F32)
        parcel[j, :, :width] = total.astype(BF)
        held = jnp.where(theirs_at == j, theirs_x, jnp.zeros(theirs_x.shape, BF))
        held = jnp.where(mine_at == j, mine_x, held)
        parcel[j, :, width : 2 * width] = held
        parcel[j, :, 2 * width : 2 * width + LANES] = halves


def output_kernel(start, got, up, gain_w, gain_low, out, stats, *mixed):
    rows = stats.shape[0]
    width = gain_w.shape[1]
    feats = 2 * width
    total = got[0, :, :width].astype(F32)
    x = got[0, :, width:feats].astype(F32)
    values = join(got[0, :, feats : feats + LANES])
    for j in range(1, CHIPS):
        total = total + got[j, :, :width].astype(F32)
        x = x + got[j, :, width:feats].astype(F32)
        values = values + join(got[j, :, feats : feats + LANES])
    values = between(values, 0, LANES // 2)
    if start:
        gain_w[...] = total[rows : rows + 2 * CHIPS] + total[rows + 2 * CHIPS :]
        gain_low[...] = between(values[rows : rows + 2 * CHIPS], LOW, GRAD)
        up[:LOW] = jnp.zeros((LOW, width), BF)
        up[LOW:GRAD] = x[rows:].astype(BF)
        up[GRAD:] = jnp.zeros((LANES - GRAD, width), BF)
        total = total[:rows]
        values = values[:rows]
        x = x[:rows]
    at = lane(rows)
    mean = pick(values, 0, SQUARE) / (2 * CHIPS)
    off = jnp.where(at < 2 * CHIPS, values - mean, 0.0)
    square = pick(values, SQUARE, LOW) + feats * jnp.sum(off * off, axis=1, keepdims=True)
    inv = lax.rsqrt(square / (feats * 2 * CHIPS) + EPS)
    low = values
    for j in range(2 * CHIPS):
        total = total + off[:, j : j + 1] * gain_w[j : j + 1, :]
        low = low + off[:, j : j + 1] * gain_low[j : j + 1, :]
    total = inv * total
    low = between(inv * low, LOW, GRAD)
    for ref in mixed:
        ref[...] = total
    stats[...] = jnp.where(at == 0, mean, jnp.where(at == 1, inv, low))
    out[:, :width] = (x + total + dot(low.astype(BF), up[...])).astype(BF)
    if not start:
        out[:, width : width + LANES] = split(values)
        for j in range(CHIPS):
            at = width + LANES + j * width
            out[:, at : at + width] = got[j, :, feats + LANES :]


def whole_kernel(mine, theirs, output):
    width = output.shape[1] // 2
    output[...] = both_halves(mine[:, :width], theirs[:, :width])


def rank_grads(sums):
    return pltpu.roll(between(sums, GRAD, FIRST), LANES - (GRAD - LOW), 1)


def normed(x, stats):
    return (x.astype(F32) - pick(stats, 0, 1)) * pick(stats, 1, 2)


def backward_kernel(mine, theirs, x, stats, gains, gain_low, w, down, grad_out, sums):
    rows, feats = x.shape
    width = feats * 2 * CHIPS
    half = feats // 2
    ends = slice(half, half + LANES)
    values = join(mine[:, ends]) + join(theirs[:, ends])
    sums[...] = values
    low_grad = rank_grads(values)
    low = between(stats[...], LOW, GRAD)
    low_all = jnp.sum(gain_low[...], axis=0, keepdims=True)
    first = pick(values, FIRST, FIRST + 1) + jnp.sum(low_grad * low_all, axis=1, keepdims=True)
    second = pick(values, SECOND, SECOND + 1) + jnp.sum(low_grad * low, axis=1, keepdims=True)
    xhat = normed(x[...], stats[...])
    grad_norm = dot(low_grad, down[...], precision=HIGHEST)
    here = jnp.zeros((rows, feats), F32)
    own_chip = owner_chip(lax.axis_index("tensor"))
    for j in range(CHIPS):
        at = half + LANES + j * half
        grad = both_halves(mine[:, at : at + half], theirs[:, at : at + half])
        at = pl.multiple_of(block_of(j) * feats, LANES)
        grad_norm = grad_norm + dot_t(grad, w[:, pl.ds(at, feats)])
        here = here + jnp.where(own_chip == j, grad.astype(F32), 0.0)
    inv = pick(stats[...], 1, 2)
    grad_x = here + inv * (grad_norm * gains[...] - first / width - xhat * (second / width))
    grad_out[...] = grad_x.astype(BF)


def accumulate_kernel(gains, after, *refs):
    count = TICKS - 1
    xs, stats, sums, grads = (refs[i * count : (i + 1) * count] for i in range(4))
    acc_down, acc_up = refs[4 * count :]
    rank = acc_up.shape[0]
    down, up = 0.0, 0.0
    for j in range(count):
        u = normed(xs[j][...], stats[j][...]) * gains[...]
        down = down + t_dot(rank_grads(sums[j][...]), u, precision=HIGHEST)
        up = up + t_dot(stats[j][...].astype(BF), grads[j][...])
    acc_down[...] = down[LOW : LOW + rank]
    acc_up[...] = up[LOW : LOW + rank]


def last_kernel(sections, arrived, output, up, stats, acc_up, after, out, up_out):
    rows, feats = arrived.shape
    rank = up.shape[0]
    kept = jnp.where(lax.axis_index("dp") == 0, output[...], jnp.zeros(output.shape, BF))
    grad = jnp.where(lax.axis_index("section") == sections - 1, kept, arrived[...])
    turned = dot_t(up[...], grad)
    turned = jnp.concatenate([turned, jnp.zeros((rank, LANES - rows), F32)], axis=1)
    high = turned.astype(BF).astype(F32)
    parcel = jnp.concatenate([high, turned - high, acc_up[...]], axis=1).astype(BF)
    for j in range(4 * CHIPS):
        out[j] = parcel
    low = t_dot(stats[...].astype(BF), grad)
    up_out[...] = low[LOW : LOW + rank].astype(BF)


def finish_kernel(got, x, stats, gains, mine, theirs, up_mine, up_theirs, down_out, up_out):
    rows = x.shape[0]
    turned = got[0, :, : 2 * LANES].astype(F32)
    for j in range(1, 4 * CHIPS):
        turned = turned + got[j, :, : 2 * LANES].astype(F32)
    low_grad = turned[:, :LANES] + turned[:, LANES:]
    u = normed(x[...], stats[...]) * gains[...]
    u = jnp.concatenate([u, jnp.zeros((LANES - rows, u.shape[1]), F32)])
    total = mine[...] + theirs[...] + dot(low_grad, u, precision=HIGHEST)
    down_out[...] = (total / rows).astype(BF)
    tensor = lax.axis_index("tensor")
    at = 4 * look_up(OWNER, tensor) + tensor // CHIPS
    total = jnp.concatenate([got[at, :, 2 * LANES :], got[at + 2, :, 2 * LANES :]], axis=1)
    total = total.astype(F32) + up_mine[...].astype(F32) + up_theirs[...].astype(F32)
    up_out[...] = (total / rows).astype(BF)


def to_same(array, sections):
    return lax.ppermute(array, "section", [(s, s - 1) for s in range(1, sections)])


def last_home(array, sections):
    s = sections - 1
    route = [(flat(s, *owner(block, 0)), flat(s, block, 0)) for block in range(2 * CHIPS)]
    return lax.ppermute(array, AXES, route)


def on_device(
    weight,
    adapter_down_map,
    adapter_up_map,
    gain,
    prior_epoch_input,
    prior_epoch_output,
    initial_step_inputs,
    initial_step_gradients,
    sample_numbers,
):
    del prior_epoch_output
    w = weight[0]
    gains = gain
    sections = lax.axis_size("section")
    toks, feats = initial_step_inputs.shape[1:]
    rank = adapter_up_map.shape[1]
    rows = 2 * toks

    mine = initial_step_inputs[0]
    theirs = lax.ppermute(mine, "dp", [(0, 1), (1, 0)])
    down = call(warm_kernel, shape(LANES, feats), w, gains, mine, adapter_down_map[0].T)

    block = shape(rows, feats, dtype=BF)
    values = shape(rows, LANES)
    xs, all_stats, all_sums, grads = [], [], [], []
    for tick in range(TICKS):
        start = tick == 0
        more = 4 * CHIPS if start else 0
        out = [block, shape(CHIPS, rows + more, feats, dtype=BF), shape(rows + more, LANES)]
        if start:
            x, product, small = call(
                functools.partial(forward_kernel, True, tick),
                out,
                mine,
                theirs,
                gains,
                w,
                down,
            )
        else:
            x, product, small = call(
                functools.partial(forward_kernel, False, tick),
                out,
                arrived,
                chosen,
                chosen_theirs,
                gains,
                w,
                down,
            )
        width = feats // 2
        ins = [product, small, x]
        columns = (CHIPS + (1 if start else 2)) * width + LANES
        dealt = shape(rows + more, columns, dtype=BF)
        if start:
            dealt = call(
                functools.partial(deal_kernel, tick, sections), dealt, *ins, adapter_up_map[0]
            )
        else:
            dealt, grad_part = call(
                functools.partial(deal_kernel, tick, sections),
                [dealt, block],
                *ins,
                grad_arrived,
                output,
            )
        ins.append(swap_cores(dealt))
        columns = (2 if start else 3) * width + LANES
        parcel = shape(CHIPS, rows + more, columns, dtype=BF)
        if start:
            parcel = call(functools.partial(pack_kernel, True), parcel, *ins, adapter_up_map[0])
        else:
            parcel, grad = call(
                functools.partial(pack_kernel, False),
                [parcel, shape(rows, width, dtype=BF)],
                *ins,
                grad_part,
                up,
                gain_w,
                mixed,
            )
            grads.append(grad)
        got = over_chips(parcel)
        columns = width + (0 if start else LANES + CHIPS * width)
        out = [shape(rows, columns, dtype=BF), values]
        if tick < TICKS - 1:
            out.append(shape(rows, width))
        kernel = functools.partial(output_kernel, start)
        if start:
            up = shape(LANES, width, dtype=BF)
            up, gain_w, gain_low, own, stats, mixed = call(
                kernel, [up, shape(2 * CHIPS, width), shape(2 * CHIPS, LANES)] + out, got
            )
        else:
            own, stats, *mixed = call(kernel, out, got, up, gain_w, gain_low)
            mixed = mixed[0] if mixed else None
        other = swap_cores(own)
        output = call(whole_kernel, block, own, other)
        if tick < TICKS - 1:
            arrived = to_next(output, sections)
        if start:
            chosen, grads_out = call(
                prepare_kernel,
                [shape(TICKS - 1, toks, feats, dtype=BF), shape(toks, feats, dtype=BF)],
                prior_epoch_input[0, 0],
                initial_step_gradients[0],
                own,
                scalars=(sample_numbers[0, 0],),
            )
            grad_arrived = to_owner(grads_out, sections, 0)
            chosen_theirs = lax.ppermute(
                chosen,
                AXES,
                [(flat(0, t, d), flat(0, t, 1 - d)) for t in range(2 * CHIPS) for d in range(2)],
            )
        else:
            grad_x, sums = call(
                backward_kernel,
                [block, values],
                own,
                other,
                xs[-1],
                all_stats[-1],
                gains,
                gain_low,
                w,
                down,
            )
            all_sums.append(sums)
            if tick < TICKS - 1:
                grad_arrived = to_owner(grad_x, sections, 1)
            else:
                grad_arrived = to_same(grad_x, sections)
        xs.append(x)
        all_stats.append(stats)

    acc_down, acc_up = call(
        accumulate_kernel,
        [shape(rank, feats), shape(rank, feats // 2)],
        gains,
        grad_x,
        *xs[:-1],
        *all_stats[:-1],
        *all_sums,
        *grads,
    )
    acc_other = lax.ppermute(acc_down, "dp", [(0, 1), (1, 0)])
    parcel, up_part = call(
        functools.partial(last_kernel, sections),
        [
            shape(4 * CHIPS, rank, 2 * LANES + feats // 2, dtype=BF),
            shape(rank, feats, dtype=BF),
        ],
        grad_arrived,
        last_home(output, sections),
        adapter_up_map[0],
        stats,
        acc_up,
        acc_other,
    )
    got = lax.all_to_all(parcel, ("tensor", "dp"), 0, 0)
    grad_down, grad_up = call(
        finish_kernel,
        [shape(rank, feats, dtype=BF), shape(rank, feats, dtype=BF)],
        got,
        x,
        stats,
        gains,
        acc_down,
        acc_other,
        up_part,
        lax.ppermute(up_part, "dp", [(0, 1), (1, 0)]),
    )
    return grad_down.T[None], grad_up[None]


def solution(mesh):
    in_specs = (
        P("section", "tensor", "dp"),
        P("section", "tensor", None),
        P("section", None, "tensor"),
        P("section", "tensor"),
        P("section", "dp", None, None, "tensor"),
        P("section", "dp", None, None, "tensor"),
        P("section", "dp", "tensor"),
        P("section", "dp", "tensor"),
        P("section", "dp", None),
    )
    out_specs = (P("section", "tensor", None), P("section", None, "tensor"))
    return jax.shard_map(
        on_device, mesh=mesh, in_specs=in_specs, out_specs=out_specs, check_vma=False
    )
```

```python
import functools

import jax
import jax.numpy as jnp
from jax import lax
from jax.experimental import pallas as pl
from jax.experimental.pallas import tpu as pltpu
from jax.sharding import PartitionSpec as P

TICKS = 4
CHIPS = 4
EPS = 1e-05
AXES = ("section", "tensor", "dp")
HIGHEST = lax.Precision.HIGHEST
BF = jnp.bfloat16
F32 = jnp.float32

LANES = 128
SQUARE = 8
LOW = 16
GRAD = 32
FIRST = 48
SECOND = 49


def flat(section, tensor, dp):
    return (section * 2 * CHIPS + tensor) * 2 + dp


OWNER = (0, 3, 1, 2, 2, 1, 3, 0)


def owner(block, core):
    return 2 * OWNER[block] + core, block // CHIPS


def look_up(table, at):
    return sum(jnp.where(at == i, value, 0) for i, value in enumerate(table))


def owner_chip(block):
    mine = block // CHIPS == lax.axis_index("dp")
    return jnp.where(mine, look_up(OWNER, block), -1)


def block_of(chip):
    half = lax.axis_index("dp")
    return jnp.where(half == 0, OWNER[:CHIPS].index(chip), OWNER[CHIPS:].index(chip))


def to_owner(array, sections, back):
    route = []
    for s in range(sections):
        for block in range(2 * CHIPS):
            for half in range(2):
                if s - back >= 0:
                    route.append((flat(s, block, half), flat(s - back, *owner(block, half))))
    return lax.ppermute(array, AXES, route)


def to_next(array, sections):
    route = []
    for s in range(sections - 1):
        for block in range(2 * CHIPS):
            for half in range(2):
                route.append((flat(s, *owner(block, half)), flat(s + 1, block, half)))
    return lax.ppermute(array, AXES, route)


def swap_cores(array):
    return lax.ppermute(array, "tensor", [(i, i ^ 1) for i in range(2 * CHIPS)])


def over_chips(array):
    groups = [[2 * i for i in range(CHIPS)], [2 * i + 1 for i in range(CHIPS)]]
    return lax.all_to_all(array, "tensor", 0, 0, axis_index_groups=groups)


def dot(a, b, **kw):
    return jnp.dot(a, b, preferred_element_type=F32, **kw)


def dot_t(a, b, **kw):
    return lax.dot_general(a, b, (((1,), (1,)), ((), ())), preferred_element_type=F32, **kw)


def t_dot(a, b, **kw):
    return lax.dot_general(a, b, (((0,), (0,)), ((), ())), preferred_element_type=F32, **kw)


def lane(rows):
    return lax.broadcasted_iota(jnp.int32, (rows, LANES), 1)


def between(values, low, high):
    at = lane(values.shape[0])
    return jnp.where((at >= low) & (at < high), values, 0.0)


def pick(values, low, high):
    return jnp.sum(between(values, low, high), axis=1, keepdims=True)


def split(values):
    high = values.astype(BF).astype(F32)
    rest = pltpu.roll(values - high, LANES // 2, 1)
    return jnp.where(lane(values.shape[0]) < LANES // 2, high, rest).astype(BF)


def join(halves):
    wide = halves.astype(F32)
    return wide + pltpu.roll(wide, LANES // 2, 1)


def call(kernel, out, *args, scalars=(), vmem=16):
    return pl.pallas_call(
        kernel,
        out_shape=out,
        in_specs=[pl.BlockSpec(memory_space=pltpu.SMEM)] * len(scalars)
        + [pl.BlockSpec(memory_space=pltpu.VMEM)] * len(args),
        out_specs=jax.tree.map(lambda _: pl.BlockSpec(memory_space=pltpu.VMEM), out),
        compiler_params=pltpu.CompilerParams(vmem_limit_bytes=vmem * 2**20),
    )(*scalars, *args)


def shape(*dims, dtype=F32):
    return jax.ShapeDtypeStruct(dims, dtype)


def replicas(mine, theirs):
    first = lax.axis_index("dp") == 0
    return jnp.concatenate([jnp.where(first, mine, theirs), jnp.where(first, theirs, mine)])


def warm_kernel(w, down_rows, down):
    rank, feats = down_rows.shape
    down[:LOW] = jnp.zeros((LOW, feats), F32)
    down[LOW : LOW + rank] = down_rows[...].astype(F32)
    down[LOW + rank :] = jnp.zeros((LANES - LOW - rank, feats), F32)


def prepare_kernel(order, stored, grads, after, chosen, grads_out):
    for j in range(TICKS - 1):
        chosen[j] = jnp.where(order[j + 1] == 0, stored[0], stored[1])
    grads_out[...] = grads[...]


def forward_kernel(start, tick, *refs):
    place = lax.axis_index("tensor")
    if start:
        mine, theirs, gains, w, down, x_out, product, small = refs
        x = replicas(mine[...], theirs[...])
    else:
        arrived, mine, theirs, gains, w, down, x_out, product, small = refs
        given = replicas(mine[tick - 1], theirs[tick - 1])
        x = jnp.where(lax.axis_index("section") == 0, given, arrived[...])
    x_out[...] = x
    rows, feats = x.shape
    wide = x.astype(F32)
    mid = jnp.sum(wide, axis=1, keepdims=True) / feats
    centered = wide - mid
    square = jnp.sum(centered * centered, axis=1, keepdims=True)
    scaled = centered * gains[...]
    at = lane(rows)
    low = dot_t(scaled, down[...], precision=HIGHEST)
    low = jnp.where(at == place, mid, low)
    small[0:rows] = jnp.where(at == SQUARE + place, square, low)
    left = scaled.astype(BF)
    if start:
        row = lax.broadcasted_iota(jnp.int32, (2 * CHIPS, feats), 0)
        gain_rows = jnp.where(row == place, gains[...], 0.0)
        high = gain_rows.astype(BF).astype(F32)
        left = jnp.concatenate([left, jnp.concatenate([high, gain_rows - high]).astype(BF)])
        small[rows:] = jnp.concatenate(
            [dot_t(gain_rows, down[...], precision=HIGHEST), jnp.zeros((2 * CHIPS, LANES), F32)]
        )
    for j in range(CHIPS):
        part = dot(left, w[:, j * feats : (j + 1) * feats])
        if start:
            tail = part[rows : rows + 2 * CHIPS] + part[rows + 2 * CHIPS :]
            high = tail.astype(BF).astype(F32)
            part = jnp.concatenate([part[:rows], high, tail - high])
        slot = jnp.where(lax.axis_index("dp") == 0, OWNER[j], OWNER[CHIPS + j])
        product[slot] = part.astype(BF)


def first_core():
    return lax.axis_index("tensor") % 2 == 0


def own_half(array):
    feats = array.shape[-1]
    return jnp.where(first_core(), array[..., : feats // 2], array[..., feats // 2 :])


def other_half(array):
    feats = array.shape[-1]
    return jnp.where(first_core(), array[..., feats // 2 :], array[..., : feats // 2])


def both_halves(mine, theirs):
    return jnp.concatenate(
        [jnp.where(first_core(), mine, theirs), jnp.where(first_core(), theirs, mine)], axis=-1
    )


def deal_kernel(tick, sections, product, small, x, *refs):
    rows, feats = x.shape
    width = feats // 2
    at = CHIPS * width
    if tick == 0:
        up, out = refs
        out[rows:, at : at + width] = other_half(up[...])
    else:
        arrived, output, out, grad_out = refs
        if tick == 1:
            given = arrived[...]
            zeros = jnp.zeros(given.shape, BF)
            given = jnp.concatenate(
                [jnp.where(first_core(), given, zeros), jnp.where(first_core(), zeros, given)]
            )
        else:
            given = arrived[...]
        kept = jnp.where(first_core(), output[...], jnp.zeros(output.shape, BF))
        grad = jnp.where(lax.axis_index("section") == sections - 1, kept, given)
        grad_out[...] = grad
        out[:, at + width + LANES :] = other_half(grad)
    for j in range(CHIPS):
        out[:, j * width : (j + 1) * width] = other_half(product[j])
    out[:rows, at : at + width] = other_half(x[...])
    out[:, at + width : at + width + LANES] = split(small[...])


def pack_kernel(start, product, small, x, theirs, *refs):
    rows, feats = x.shape
    width = feats // 2
    at = CHIPS * width
    mine_x = own_half(x[...])
    theirs_x = theirs[:rows, at : at + width]
    at = at + width
    values = join(split(small[...])) + join(theirs[:, at : at + LANES])
    values = between(values, 0, LANES // 2)
    if start:
        up, parcel = refs
        mine_x = jnp.concatenate([mine_x, own_half(up[...])])
        theirs_x = theirs[:, at - width : at]
    else:
        grad_part, up, gain_w, mixed, parcel, grad_out = refs
        grad = own_half(grad_part[...]).astype(F32) + theirs[:, at + LANES :].astype(F32)
        grad = grad.astype(BF)
        grad_out[...] = grad
        wide = grad.astype(F32)
        first = jnp.sum(wide * jnp.sum(gain_w[...], axis=0, keepdims=True), axis=1, keepdims=True)
        second = jnp.sum(wide * mixed[...], axis=1, keepdims=True)
        lanes = lane(rows)
        values = values + pltpu.roll(dot_t(grad, up[...]), GRAD - LOW, 1)
        values = jnp.where(lanes == FIRST, first, values)
        values = jnp.where(lanes == SECOND, second, values)
        for j in range(CHIPS):
            parcel[j, :, 2 * width + LANES :] = grad
    halves = split(values)
    tensor = lax.axis_index("tensor")
    mine_at, theirs_at = owner_chip(tensor), owner_chip(tensor ^ 1)
    for j in range(CHIPS):
        total = own_half(product[j]).astype(F32)
        total = total + theirs[:, j * width : (j + 1) * width].astype(F32)
        parcel[j, :, :width] = total.astype(BF)
        held = jnp.where(theirs_at == j, theirs_x, jnp.zeros(theirs_x.shape, BF))
        held = jnp.where(mine_at == j, mine_x, held)
        parcel[j, :, width : 2 * width] = held
        parcel[j, :, 2 * width : 2 * width + LANES] = halves


def output_kernel(start, got, up, gain_w, gain_low, out, stats, *mixed):
    rows = stats.shape[0]
    width = gain_w.shape[1]
    feats = 2 * width
    total = got[0, :, :width].astype(F32)
    x = got[0, :, width:feats].astype(F32)
    values = join(got[0, :, feats : feats + LANES])
    for j in range(1, CHIPS):
        total = total + got[j, :, :width].astype(F32)
        x = x + got[j, :, width:feats].astype(F32)
        values = values + join(got[j, :, feats : feats + LANES])
    values = between(values, 0, LANES // 2)
    if start:
        gain_w[...] = total[rows : rows + 2 * CHIPS] + total[rows + 2 * CHIPS :]
        gain_low[...] = between(values[rows : rows + 2 * CHIPS], LOW, GRAD)
        up[:LOW] = jnp.zeros((LOW, width), BF)
        up[LOW:GRAD] = x[rows:].astype(BF)
        up[GRAD:] = jnp.zeros((LANES - GRAD, width), BF)
        total = total[:rows]
        values = values[:rows]
        x = x[:rows]
    at = lane(rows)
    mean = pick(values, 0, SQUARE) / (2 * CHIPS)
    off = jnp.where(at < 2 * CHIPS, values - mean, 0.0)
    square = pick(values, SQUARE, LOW) + feats * jnp.sum(off * off, axis=1, keepdims=True)
    inv = lax.rsqrt(square / (feats * 2 * CHIPS) + EPS)
    low = values
    for j in range(2 * CHIPS):
        total = total + off[:, j : j + 1] * gain_w[j : j + 1, :]
        low = low + off[:, j : j + 1] * gain_low[j : j + 1, :]
    total = inv * total
    low = between(inv * low, LOW, GRAD)
    for ref in mixed:
        ref[...] = total
    stats[...] = jnp.where(at == 0, mean, jnp.where(at == 1, inv, low))
    out[:, :width] = (x + total + dot(low.astype(BF), up[...])).astype(BF)
    if not start:
        out[:, width : width + LANES] = split(values)
        for j in range(CHIPS):
            at = width + LANES + j * width
            out[:, at : at + width] = got[j, :, feats + LANES :]


def whole_kernel(mine, theirs, output):
    width = output.shape[1] // 2
    output[...] = both_halves(mine[:, :width], theirs[:, :width])


def rank_grads(sums):
    return pltpu.roll(between(sums, GRAD, FIRST), LANES - (GRAD - LOW), 1)


def normed(x, stats):
    return (x.astype(F32) - pick(stats, 0, 1)) * pick(stats, 1, 2)


def backward_kernel(mine, theirs, x, stats, gains, gain_low, w, down, grad_out, sums):
    rows, feats = x.shape
    width = feats * 2 * CHIPS
    half = feats // 2
    ends = slice(half, half + LANES)
    values = join(mine[:, ends]) + join(theirs[:, ends])
    sums[...] = values
    low_grad = rank_grads(values)
    low = between(stats[...], LOW, GRAD)
    low_all = jnp.sum(gain_low[...], axis=0, keepdims=True)
    first = pick(values, FIRST, FIRST + 1) + jnp.sum(low_grad * low_all, axis=1, keepdims=True)
    second = pick(values, SECOND, SECOND + 1) + jnp.sum(low_grad * low, axis=1, keepdims=True)
    xhat = normed(x[...], stats[...])
    grad_norm = dot(low_grad, down[...], precision=HIGHEST)
    here = jnp.zeros((rows, feats), F32)
    own_chip = owner_chip(lax.axis_index("tensor"))
    for j in range(CHIPS):
        at = half + LANES + j * half
        grad = both_halves(mine[:, at : at + half], theirs[:, at : at + half])
        at = pl.multiple_of(block_of(j) * feats, LANES)
        grad_norm = grad_norm + dot_t(grad, w[:, pl.ds(at, feats)])
        here = here + jnp.where(own_chip == j, grad.astype(F32), 0.0)
    inv = pick(stats[...], 1, 2)
    grad_x = here + inv * (grad_norm * gains[...] - first / width - xhat * (second / width))
    grad_out[...] = grad_x.astype(BF)


def accumulate_kernel(gains, after, *refs):
    count = TICKS - 1
    xs, stats, sums, grads = (refs[i * count : (i + 1) * count] for i in range(4))
    acc_down, acc_up = refs[4 * count :]
    rank = acc_up.shape[0]
    down, up = 0.0, 0.0
    for j in range(count):
        u = normed(xs[j][...], stats[j][...]) * gains[...]
        down = down + t_dot(rank_grads(sums[j][...]), u, precision=HIGHEST)
        up = up + t_dot(stats[j][...].astype(BF), grads[j][...])
    acc_down[...] = down[LOW : LOW + rank]
    acc_up[...] = up[LOW : LOW + rank]


def last_kernel(sections, arrived, output, up, stats, acc_up, after, out, up_out):
    rows, feats = arrived.shape
    rank = up.shape[0]
    kept = jnp.where(lax.axis_index("dp") == 0, output[...], jnp.zeros(output.shape, BF))
    grad = jnp.where(lax.axis_index("section") == sections - 1, kept, arrived[...])
    turned = dot_t(up[...], grad)
    turned = jnp.concatenate([turned, jnp.zeros((rank, LANES - rows), F32)], axis=1)
    high = turned.astype(BF).astype(F32)
    parcel = jnp.concatenate([high, turned - high, acc_up[...]], axis=1).astype(BF)
    for j in range(4 * CHIPS):
        out[j] = parcel
    low = t_dot(stats[...].astype(BF), grad)
    up_out[...] = low[LOW : LOW + rank].astype(BF)


def finish_kernel(got, x, stats, gains, mine, theirs, up_mine, up_theirs, down_out, up_out):
    rows = x.shape[0]
    turned = got[0, :, : 2 * LANES].astype(F32)
    for j in range(1, 4 * CHIPS):
        turned = turned + got[j, :, : 2 * LANES].astype(F32)
    low_grad = turned[:, :LANES] + turned[:, LANES:]
    u = normed(x[...], stats[...]) * gains[...]
    u = jnp.concatenate([u, jnp.zeros((LANES - rows, u.shape[1]), F32)])
    total = mine[...] + theirs[...] + dot(low_grad, u, precision=HIGHEST)
    down_out[...] = (total / rows).astype(BF)
    tensor = lax.axis_index("tensor")
    at = 4 * look_up(OWNER, tensor) + tensor // CHIPS
    total = jnp.concatenate([got[at, :, 2 * LANES :], got[at + 2, :, 2 * LANES :]], axis=1)
    total = total.astype(F32) + up_mine[...].astype(F32) + up_theirs[...].astype(F32)
    up_out[...] = (total / rows).astype(BF)


def to_same(array, sections):
    return lax.ppermute(array, "section", [(s, s - 1) for s in range(1, sections)])


def last_home(array, sections):
    s = sections - 1
    route = [(flat(s, *owner(block, 0)), flat(s, block, 0)) for block in range(2 * CHIPS)]
    return lax.ppermute(array, AXES, route)


def on_device(
    weight,
    adapter_down_map,
    adapter_up_map,
    gain,
    prior_epoch_input,
    prior_epoch_output,
    initial_step_inputs,
    initial_step_gradients,
    sample_numbers,
):
    del prior_epoch_output
    w = weight[0]
    gains = gain
    sections = lax.axis_size("section")
    toks, feats = initial_step_inputs.shape[1:]
    rank = adapter_up_map.shape[1]
    rows = 2 * toks

    mine = initial_step_inputs[0]
    theirs = lax.ppermute(mine, "dp", [(0, 1), (1, 0)])
    down = call(warm_kernel, shape(LANES, feats), w, adapter_down_map[0].T)

    block = shape(rows, feats, dtype=BF)
    values = shape(rows, LANES)
    xs, all_stats, all_sums, grads = [], [], [], []
    for tick in range(TICKS):
        start = tick == 0
        more = 4 * CHIPS if start else 0
        out = [block, shape(CHIPS, rows + more, feats, dtype=BF), shape(rows + more, LANES)]
        if start:
            x, product, small = call(
                functools.partial(forward_kernel, True, tick),
                out,
                mine,
                theirs,
                gains,
                w,
                down,
            )
        else:
            x, product, small = call(
                functools.partial(forward_kernel, False, tick),
                out,
                arrived,
                chosen,
                chosen_theirs,
                gains,
                w,
                down,
            )
        width = feats // 2
        ins = [product, small, x]
        columns = (CHIPS + (1 if start else 2)) * width + LANES
        dealt = shape(rows + more, columns, dtype=BF)
        if start:
            dealt = call(
                functools.partial(deal_kernel, tick, sections), dealt, *ins, adapter_up_map[0]
            )
        else:
            dealt, grad_part = call(
                functools.partial(deal_kernel, tick, sections),
                [dealt, block],
                *ins,
                grad_arrived,
                output,
            )
        ins.append(swap_cores(dealt))
        columns = (2 if start else 3) * width + LANES
        parcel = shape(CHIPS, rows + more, columns, dtype=BF)
        if start:
            parcel = call(functools.partial(pack_kernel, True), parcel, *ins, adapter_up_map[0])
        else:
            parcel, grad = call(
                functools.partial(pack_kernel, False),
                [parcel, shape(rows, width, dtype=BF)],
                *ins,
                grad_part,
                up,
                gain_w,
                mixed,
            )
            grads.append(grad)
        got = over_chips(parcel)
        columns = width + (0 if start else LANES + CHIPS * width)
        out = [shape(rows, columns, dtype=BF), values]
        if tick < TICKS - 1:
            out.append(shape(rows, width))
        kernel = functools.partial(output_kernel, start)
        if start:
            up = shape(LANES, width, dtype=BF)
            up, gain_w, gain_low, own, stats, mixed = call(
                kernel, [up, shape(2 * CHIPS, width), shape(2 * CHIPS, LANES)] + out, got
            )
        else:
            own, stats, *mixed = call(kernel, out, got, up, gain_w, gain_low)
            mixed = mixed[0] if mixed else None
        other = swap_cores(own)
        output = call(whole_kernel, block, own, other)
        if tick < TICKS - 1:
            arrived = to_next(output, sections)
        if start:
            chosen, grads_out = call(
                prepare_kernel,
                [shape(TICKS - 1, toks, feats, dtype=BF), shape(toks, feats, dtype=BF)],
                prior_epoch_input[0, 0],
                initial_step_gradients[0],
                own,
                scalars=(sample_numbers[0, 0],),
            )
            grad_arrived = to_owner(grads_out, sections, 0)
            chosen_theirs = lax.ppermute(
                chosen,
                AXES,
                [(flat(0, t, d), flat(0, t, 1 - d)) for t in range(2 * CHIPS) for d in range(2)],
            )
        else:
            grad_x, sums = call(
                backward_kernel,
                [block, values],
                own,
                other,
                xs[-1],
                all_stats[-1],
                gains,
                gain_low,
                w,
                down,
            )
            all_sums.append(sums)
            if tick < TICKS - 1:
                grad_arrived = to_owner(grad_x, sections, 1)
            else:
                grad_arrived = to_same(grad_x, sections)
        xs.append(x)
        all_stats.append(stats)

    acc_down, acc_up = call(
        accumulate_kernel,
        [shape(rank, feats), shape(rank, feats // 2)],
        gains,
        grad_x,
        *xs[:-1],
        *all_stats[:-1],
        *all_sums,
        *grads,
    )
    acc_other = lax.ppermute(acc_down, "dp", [(0, 1), (1, 0)])
    parcel, up_part = call(
        functools.partial(last_kernel, sections),
        [
            shape(4 * CHIPS, rank, 2 * LANES + feats // 2, dtype=BF),
            shape(rank, feats, dtype=BF),
        ],
        grad_arrived,
        last_home(output, sections),
        adapter_up_map[0],
        stats,
        acc_up,
        acc_other,
    )
    got = lax.all_to_all(parcel, ("tensor", "dp"), 0, 0)
    grad_down, grad_up = call(
        finish_kernel,
        [shape(rank, feats, dtype=BF), shape(rank, feats, dtype=BF)],
        got,
        x,
        stats,
        gains,
        acc_down,
        acc_other,
        up_part,
        lax.ppermute(up_part, "dp", [(0, 1), (1, 0)]),
    )
    return grad_down.T[None], grad_up[None]


def solution(mesh):
    in_specs = (
        P("section", "tensor", "dp"),
        P("section", "tensor", None),
        P("section", None, "tensor"),
        P("section", "tensor"),
        P("section", "dp", None, None, "tensor"),
        P("section", "dp", None, None, "tensor"),
        P("section", "dp", "tensor"),
        P("section", "dp", "tensor"),
        P("section", "dp", None),
    )
    out_specs = (P("section", "tensor", None), P("section", None, "tensor"))
    return jax.shard_map(
        on_device, mesh=mesh, in_specs=in_specs, out_specs=out_specs, check_vma=False
    )
```

```python
import functools

import jax
import jax.numpy as jnp
from jax import lax
from jax.experimental import pallas as pl
from jax.experimental.pallas import tpu as pltpu
from jax.sharding import PartitionSpec as P

TICKS = 4
CHIPS = 4
EPS = 1e-05
AXES = ("section", "tensor", "dp")
HIGHEST = lax.Precision.HIGHEST
BF = jnp.bfloat16
F32 = jnp.float32

LANES = 128
SQUARE = 8
LOW = 16
GRAD = 32
FIRST = 48
SECOND = 49


def flat(section, tensor, dp):
    return (section * 2 * CHIPS + tensor) * 2 + dp


OWNER = (0, 3, 1, 2, 2, 1, 3, 0)


def owner(block, core):
    return 2 * OWNER[block] + core, block // CHIPS


def look_up(table, at):
    return sum(jnp.where(at == i, value, 0) for i, value in enumerate(table))


def owner_chip(block):
    mine = block // CHIPS == lax.axis_index("dp")
    return jnp.where(mine, look_up(OWNER, block), -1)


def block_of(chip):
    half = lax.axis_index("dp")
    return jnp.where(half == 0, OWNER[:CHIPS].index(chip), OWNER[CHIPS:].index(chip))


def to_owner(array, sections, back):
    route = []
    for s in range(sections):
        for block in range(2 * CHIPS):
            for half in range(2):
                if s - back >= 0:
                    route.append((flat(s, block, half), flat(s - back, *owner(block, half))))
    return lax.ppermute(array, AXES, route)


def to_next(array, sections):
    route = []
    for s in range(sections - 1):
        for block in range(2 * CHIPS):
            for half in range(2):
                route.append((flat(s, *owner(block, half)), flat(s + 1, block, half)))
    return lax.ppermute(array, AXES, route)


def swap_cores(array):
    return lax.ppermute(array, "tensor", [(i, i ^ 1) for i in range(2 * CHIPS)])


def over_chips(array):
    groups = [[2 * i for i in range(CHIPS)], [2 * i + 1 for i in range(CHIPS)]]
    return lax.all_to_all(array, "tensor", 0, 0, axis_index_groups=groups)


def dot(a, b, **kw):
    return jnp.dot(a, b, preferred_element_type=F32, **kw)


def dot_t(a, b, **kw):
    return lax.dot_general(a, b, (((1,), (1,)), ((), ())), preferred_element_type=F32, **kw)


def t_dot(a, b, **kw):
    return lax.dot_general(a, b, (((0,), (0,)), ((), ())), preferred_element_type=F32, **kw)


def lane(rows):
    return lax.broadcasted_iota(jnp.int32, (rows, LANES), 1)


def between(values, low, high):
    at = lane(values.shape[0])
    return jnp.where((at >= low) & (at < high), values, 0.0)


def pick(values, low, high):
    return jnp.sum(between(values, low, high), axis=1, keepdims=True)


def split(values):
    high = values.astype(BF).astype(F32)
    rest = pltpu.roll(values - high, LANES // 2, 1)
    return jnp.where(lane(values.shape[0]) < LANES // 2, high, rest).astype(BF)


def join(halves):
    wide = halves.astype(F32)
    return wide + pltpu.roll(wide, LANES // 2, 1)


def call(kernel, out, *args, scalars=(), vmem=16):
    return pl.pallas_call(
        kernel,
        out_shape=out,
        in_specs=[pl.BlockSpec(memory_space=pltpu.SMEM)] * len(scalars)
        + [pl.BlockSpec(memory_space=pltpu.VMEM)] * len(args),
        out_specs=jax.tree.map(lambda _: pl.BlockSpec(memory_space=pltpu.VMEM), out),
        compiler_params=pltpu.CompilerParams(vmem_limit_bytes=vmem * 2**20),
    )(*scalars, *args)


def shape(*dims, dtype=F32):
    return jax.ShapeDtypeStruct(dims, dtype)


def replicas(mine, theirs):
    first = lax.axis_index("dp") == 0
    return jnp.concatenate([jnp.where(first, mine, theirs), jnp.where(first, theirs, mine)])


def warm_kernel(w, down_rows, down):
    rank, feats = down_rows.shape
    down[:LOW] = jnp.zeros((LOW, feats), F32)
    down[LOW : LOW + rank] = down_rows[...].astype(F32)
    down[LOW + rank :] = jnp.zeros((LANES - LOW - rank, feats), F32)


def prepare_kernel(order, stored, grads, after, chosen, grads_out):
    for j in range(TICKS - 1):
        chosen[j] = jnp.where(order[j + 1] == 0, stored[0], stored[1])
    grads_out[...] = grads[...]


def forward_kernel(start, tick, *refs):
    place = lax.axis_index("tensor")
    if start:
        mine, theirs, gains, w, down, x_out, product, small = refs
        x = replicas(mine[...], theirs[...])
    else:
        arrived, mine, theirs, gains, w, down, x_out, product, small = refs
        given = replicas(mine[tick - 1], theirs[tick - 1])
        x = jnp.where(lax.axis_index("section") == 0, given, arrived[...])
    x_out[...] = x
    rows, feats = x.shape
    wide = x.astype(F32)
    mid = jnp.sum(wide, axis=1, keepdims=True) / feats
    centered = wide - mid
    square = jnp.sum(centered * centered, axis=1, keepdims=True)
    scaled = centered * gains[...]
    at = lane(rows)
    low = dot_t(scaled, down[...], precision=HIGHEST)
    low = jnp.where(at == place, mid, low)
    small[0:rows] = jnp.where(at == SQUARE + place, square, low)
    left = scaled.astype(BF)
    if start:
        row = lax.broadcasted_iota(jnp.int32, (2 * CHIPS, feats), 0)
        gain_rows = jnp.where(row == place, gains[...], 0.0)
        high = gain_rows.astype(BF).astype(F32)
        left = jnp.concatenate([left, jnp.concatenate([high, gain_rows - high]).astype(BF)])
        small[rows:] = jnp.concatenate(
            [dot_t(gain_rows, down[...], precision=HIGHEST), jnp.zeros((2 * CHIPS, LANES), F32)]
        )
    for j in range(CHIPS):
        part = dot(left, w[:, j * feats : (j + 1) * feats])
        if start:
            tail = part[rows : rows + 2 * CHIPS] + part[rows + 2 * CHIPS :]
            high = tail.astype(BF).astype(F32)
            part = jnp.concatenate([part[:rows], high, tail - high])
        slot = jnp.where(lax.axis_index("dp") == 0, OWNER[j], OWNER[CHIPS + j])
        product[slot] = part.astype(BF)


def first_core():
    return lax.axis_index("tensor") % 2 == 0


def own_half(array):
    feats = array.shape[-1]
    return jnp.where(first_core(), array[..., : feats // 2], array[..., feats // 2 :])


def other_half(array):
    feats = array.shape[-1]
    return jnp.where(first_core(), array[..., feats // 2 :], array[..., : feats // 2])


def both_halves(mine, theirs):
    return jnp.concatenate(
        [jnp.where(first_core(), mine, theirs), jnp.where(first_core(), theirs, mine)], axis=-1
    )


def deal_kernel(tick, sections, product, small, x, *refs):
    rows, feats = x.shape
    width = feats // 2
    at = CHIPS * width
    if tick == 0:
        up, out = refs
        out[rows:, at : at + width] = other_half(up[...])
    else:
        arrived, output, out, grad_out = refs
        if tick == 1:
            given = arrived[...]
            zeros = jnp.zeros(given.shape, BF)
            given = jnp.concatenate(
                [jnp.where(first_core(), given, zeros), jnp.where(first_core(), zeros, given)]
            )
        else:
            given = arrived[...]
        kept = jnp.where(first_core(), output[...], jnp.zeros(output.shape, BF))
        grad = jnp.where(lax.axis_index("section") == sections - 1, kept, given)
        grad_out[...] = grad
        out[:, at + width + LANES :] = other_half(grad)
    for j in range(CHIPS):
        out[:, j * width : (j + 1) * width] = other_half(product[j])
    out[:rows, at : at + width] = other_half(x[...])
    out[:, at + width : at + width + LANES] = split(small[...])


def pack_kernel(start, product, small, x, theirs, *refs):
    rows, feats = x.shape
    width = feats // 2
    at = CHIPS * width
    mine_x = own_half(x[...])
    theirs_x = theirs[:rows, at : at + width]
    at = at + width
    values = join(split(small[...])) + join(theirs[:, at : at + LANES])
    values = between(values, 0, LANES // 2)
    if start:
        up, parcel = refs
        mine_x = jnp.concatenate([mine_x, own_half(up[...])])
        theirs_x = theirs[:, at - width : at]
    else:
        grad_part, up, gain_w, mixed, parcel, grad_out = refs
        grad = own_half(grad_part[...]).astype(F32) + theirs[:, at + LANES :].astype(F32)
        grad = grad.astype(BF)
        grad_out[...] = grad
        wide = grad.astype(F32)
        first = jnp.sum(wide * jnp.sum(gain_w[...], axis=0, keepdims=True), axis=1, keepdims=True)
        second = jnp.sum(wide * mixed[...], axis=1, keepdims=True)
        lanes = lane(rows)
        values = values + pltpu.roll(dot_t(grad, up[...]), GRAD - LOW, 1)
        values = jnp.where(lanes == FIRST, first, values)
        values = jnp.where(lanes == SECOND, second, values)
        for j in range(CHIPS):
            parcel[j, :, 2 * width + LANES :] = grad
    halves = split(values)
    tensor = lax.axis_index("tensor")
    mine_at, theirs_at = owner_chip(tensor), owner_chip(tensor ^ 1)
    for j in range(CHIPS):
        total = own_half(product[j]).astype(F32)
        total = total + theirs[:, j * width : (j + 1) * width].astype(F32)
        parcel[j, :, :width] = total.astype(BF)
        held = jnp.where(theirs_at == j, theirs_x, jnp.zeros(theirs_x.shape, BF))
        held = jnp.where(mine_at == j, mine_x, held)
        parcel[j, :, width : 2 * width] = held
        parcel[j, :, 2 * width : 2 * width + LANES] = halves


def output_kernel(start, got, up, gain_w, gain_low, out, stats, *mixed):
    rows = stats.shape[0]
    width = gain_w.shape[1]
    feats = 2 * width
    total = got[0, :, :width].astype(F32)
    x = got[0, :, width:feats].astype(F32)
    values = join(got[0, :, feats : feats + LANES])
    for j in range(1, CHIPS):
        total = total + got[j, :, :width].astype(F32)
        x = x + got[j, :, width:feats].astype(F32)
        values = values + join(got[j, :, feats : feats + LANES])
    values = between(values, 0, LANES // 2)
    if start:
        gain_w[...] = total[rows : rows + 2 * CHIPS] + total[rows + 2 * CHIPS :]
        gain_low[...] = between(values[rows : rows + 2 * CHIPS], LOW, GRAD)
        up[:LOW] = jnp.zeros((LOW, width), BF)
        up[LOW:GRAD] = x[rows:].astype(BF)
        up[GRAD:] = jnp.zeros((LANES - GRAD, width), BF)
        total = total[:rows]
        values = values[:rows]
        x = x[:rows]
    at = lane(rows)
    mean = pick(values, 0, SQUARE) / (2 * CHIPS)
    off = jnp.where(at < 2 * CHIPS, values - mean, 0.0)
    square = pick(values, SQUARE, LOW) + feats * jnp.sum(off * off, axis=1, keepdims=True)
    inv = lax.rsqrt(square / (feats * 2 * CHIPS) + EPS)
    low = values
    for j in range(2 * CHIPS):
        total = total + off[:, j : j + 1] * gain_w[j : j + 1, :]
        low = low + off[:, j : j + 1] * gain_low[j : j + 1, :]
    total = inv * total
    low = between(inv * low, LOW, GRAD)
    for ref in mixed:
        ref[...] = total
    stats[...] = jnp.where(at == 0, mean, jnp.where(at == 1, inv, low))
    out[:, :width] = (x + total + dot(low.astype(BF), up[...])).astype(BF)
    if not start:
        out[:, width : width + LANES] = split(values)
        for j in range(CHIPS):
            at = width + LANES + j * width
            out[:, at : at + width] = got[j, :, feats + LANES :]


def whole_kernel(mine, theirs, *refs):
    output = refs[-1]
    width = output.shape[1] // 2
    output[...] = both_halves(mine[:, :width], theirs[:, :width])


def rank_grads(sums):
    return pltpu.roll(between(sums, GRAD, FIRST), LANES - (GRAD - LOW), 1)


def normed(x, stats):
    return (x.astype(F32) - pick(stats, 0, 1)) * pick(stats, 1, 2)


def backward_kernel(mine, theirs, x, stats, gains, gain_low, w, down, grad_out, sums):
    rows, feats = x.shape
    width = feats * 2 * CHIPS
    half = feats // 2
    ends = slice(half, half + LANES)
    values = join(mine[:, ends]) + join(theirs[:, ends])
    sums[...] = values
    low_grad = rank_grads(values)
    low = between(stats[...], LOW, GRAD)
    low_all = jnp.sum(gain_low[...], axis=0, keepdims=True)
    first = pick(values, FIRST, FIRST + 1) + jnp.sum(low_grad * low_all, axis=1, keepdims=True)
    second = pick(values, SECOND, SECOND + 1) + jnp.sum(low_grad * low, axis=1, keepdims=True)
    xhat = normed(x[...], stats[...])
    grad_norm = dot(low_grad, down[...], precision=HIGHEST)
    here = jnp.zeros((rows, feats), F32)
    own_chip = owner_chip(lax.axis_index("tensor"))
    for j in range(CHIPS):
        at = half + LANES + j * half
        grad = both_halves(mine[:, at : at + half], theirs[:, at : at + half])
        at = pl.multiple_of(block_of(j) * feats, LANES)
        grad_norm = grad_norm + dot_t(grad, w[:, pl.ds(at, feats)])
        here = here + jnp.where(own_chip == j, grad.astype(F32), 0.0)
    inv = pick(stats[...], 1, 2)
    grad_x = here + inv * (grad_norm * gains[...] - first / width - xhat * (second / width))
    grad_out[...] = grad_x.astype(BF)


def accumulate_kernel(gains, after, *refs):
    count = TICKS - 1
    xs, stats, sums, grads = (refs[i * count : (i + 1) * count] for i in range(4))
    acc_down, acc_up = refs[4 * count :]
    rank = acc_up.shape[0]
    down, up = 0.0, 0.0
    for j in range(count):
        u = normed(xs[j][...], stats[j][...]) * gains[...]
        down = down + t_dot(rank_grads(sums[j][...]), u, precision=HIGHEST)
        up = up + t_dot(stats[j][...].astype(BF), grads[j][...])
    acc_down[...] = down[LOW : LOW + rank]
    acc_up[...] = up[LOW : LOW + rank]


def last_kernel(sections, arrived, output, up, stats, acc_up, after, out, up_out):
    rows, feats = arrived.shape
    rank = up.shape[0]
    kept = jnp.where(lax.axis_index("dp") == 0, output[...], jnp.zeros(output.shape, BF))
    grad = jnp.where(lax.axis_index("section") == sections - 1, kept, arrived[...])
    turned = dot_t(up[...], grad)
    turned = jnp.concatenate([turned, jnp.zeros((rank, LANES - rows), F32)], axis=1)
    high = turned.astype(BF).astype(F32)
    parcel = jnp.concatenate([high, turned - high, acc_up[...]], axis=1).astype(BF)
    for j in range(4 * CHIPS):
        out[j] = parcel
    low = t_dot(stats[...].astype(BF), grad)
    up_out[...] = low[LOW : LOW + rank].astype(BF)


def finish_kernel(got, x, stats, gains, mine, theirs, up_mine, up_theirs, down_out, up_out):
    rows = x.shape[0]
    turned = got[0, :, : 2 * LANES].astype(F32)
    for j in range(1, 4 * CHIPS):
        turned = turned + got[j, :, : 2 * LANES].astype(F32)
    low_grad = turned[:, :LANES] + turned[:, LANES:]
    u = normed(x[...], stats[...]) * gains[...]
    u = jnp.concatenate([u, jnp.zeros((LANES - rows, u.shape[1]), F32)])
    total = mine[...] + theirs[...] + dot(low_grad, u, precision=HIGHEST)
    down_out[...] = (total / rows).astype(BF)
    tensor = lax.axis_index("tensor")
    at = 4 * look_up(OWNER, tensor) + tensor // CHIPS
    total = jnp.concatenate([got[at, :, 2 * LANES :], got[at + 2, :, 2 * LANES :]], axis=1)
    total = total.astype(F32) + up_mine[...].astype(F32) + up_theirs[...].astype(F32)
    up_out[...] = (total / rows).astype(BF)


def to_same(array, sections):
    return lax.ppermute(array, "section", [(s, s - 1) for s in range(1, sections)])


def last_home(array, sections):
    s = sections - 1
    route = [(flat(s, *owner(block, 0)), flat(s, block, 0)) for block in range(2 * CHIPS)]
    return lax.ppermute(array, AXES, route)


def on_device(
    weight,
    adapter_down_map,
    adapter_up_map,
    gain,
    prior_epoch_input,
    prior_epoch_output,
    initial_step_inputs,
    initial_step_gradients,
    sample_numbers,
):
    del prior_epoch_output
    w = weight[0]
    gains = gain
    sections = lax.axis_size("section")
    toks, feats = initial_step_inputs.shape[1:]
    rank = adapter_up_map.shape[1]
    rows = 2 * toks

    mine = initial_step_inputs[0]
    theirs = lax.ppermute(mine, "dp", [(0, 1), (1, 0)])
    down = call(warm_kernel, shape(LANES, feats), w, adapter_down_map[0].T)

    block = shape(rows, feats, dtype=BF)
    values = shape(rows, LANES)
    xs, all_stats, all_sums, grads = [], [], [], []
    for tick in range(TICKS):
        start = tick == 0
        more = 4 * CHIPS if start else 0
        out = [block, shape(CHIPS, rows + more, feats, dtype=BF), shape(rows + more, LANES)]
        if start:
            x, product, small = call(
                functools.partial(forward_kernel, True, tick),
                out,
                mine,
                theirs,
                gains,
                w,
                down,
            )
        else:
            x, product, small = call(
                functools.partial(forward_kernel, False, tick),
                out,
                arrived,
                chosen,
                chosen_theirs,
                gains,
                w,
                down,
            )
        width = feats // 2
        ins = [product, small, x]
        columns = (CHIPS + (1 if start else 2)) * width + LANES
        dealt = shape(rows + more, columns, dtype=BF)
        if start:
            dealt = call(
                functools.partial(deal_kernel, tick, sections), dealt, *ins, adapter_up_map[0]
            )
        else:
            dealt, grad_part = call(
                functools.partial(deal_kernel, tick, sections),
                [dealt, block],
                *ins,
                grad_arrived,
                output,
            )
        ins.append(swap_cores(dealt))
        columns = (2 if start else 3) * width + LANES
        parcel = shape(CHIPS, rows + more, columns, dtype=BF)
        if start:
            parcel = call(functools.partial(pack_kernel, True), parcel, *ins, adapter_up_map[0])
        else:
            parcel, grad = call(
                functools.partial(pack_kernel, False),
                [parcel, shape(rows, width, dtype=BF)],
                *ins,
                grad_part,
                up,
                gain_w,
                mixed,
            )
            grads.append(grad)
        got = over_chips(parcel)
        columns = width + (0 if start else LANES + CHIPS * width)
        out = [shape(rows, columns, dtype=BF), values]
        if tick < TICKS - 1:
            out.append(shape(rows, width))
        kernel = functools.partial(output_kernel, start)
        if start:
            up = shape(LANES, width, dtype=BF)
            up, gain_w, gain_low, own, stats, mixed = call(
                kernel, [up, shape(2 * CHIPS, width), shape(2 * CHIPS, LANES)] + out, got
            )
        else:
            own, stats, *mixed = call(kernel, out, got, up, gain_w, gain_low)
            mixed = mixed[0] if mixed else None
        other = swap_cores(own)
        if start:
            chosen, grads_out = call(
                prepare_kernel,
                [shape(TICKS - 1, toks, feats, dtype=BF), shape(toks, feats, dtype=BF)],
                prior_epoch_input[0, 0],
                initial_step_gradients[0],
                own,
                scalars=(sample_numbers[0, 0],),
            )
            grad_arrived = to_owner(grads_out, sections, 0)
            chosen_theirs = lax.ppermute(
                chosen,
                AXES,
                [(flat(0, t, d), flat(0, t, 1 - d)) for t in range(2 * CHIPS) for d in range(2)],
            )
        else:
            grad_x, sums = call(
                backward_kernel,
                [block, values],
                own,
                other,
                xs[-1],
                all_stats[-1],
                gains,
                gain_low,
                w,
                down,
            )
            all_sums.append(sums)
            if tick < TICKS - 1:
                grad_arrived = to_owner(grad_x, sections, 1)
            else:
                grad_arrived = to_same(grad_x, sections)
        output = call(whole_kernel, block, own, other, *([] if start else [grad_x]))
        if tick < TICKS - 1:
            arrived = to_next(output, sections)
        xs.append(x)
        all_stats.append(stats)

    acc_down, acc_up = call(
        accumulate_kernel,
        [shape(rank, feats), shape(rank, feats // 2)],
        gains,
        grad_x,
        *xs[:-1],
        *all_stats[:-1],
        *all_sums,
        *grads,
    )
    acc_other = lax.ppermute(acc_down, "dp", [(0, 1), (1, 0)])
    parcel, up_part = call(
        functools.partial(last_kernel, sections),
        [
            shape(4 * CHIPS, rank, 2 * LANES + feats // 2, dtype=BF),
            shape(rank, feats, dtype=BF),
        ],
        grad_arrived,
        last_home(output, sections),
        adapter_up_map[0],
        stats,
        acc_up,
        acc_other,
    )
    got = lax.all_to_all(parcel, ("tensor", "dp"), 0, 0)
    grad_down, grad_up = call(
        finish_kernel,
        [shape(rank, feats, dtype=BF), shape(rank, feats, dtype=BF)],
        got,
        x,
        stats,
        gains,
        acc_down,
        acc_other,
        up_part,
        lax.ppermute(up_part, "dp", [(0, 1), (1, 0)]),
    )
    return grad_down.T[None], grad_up[None]


def solution(mesh):
    in_specs = (
        P("section", "tensor", "dp"),
        P("section", "tensor", None),
        P("section", None, "tensor"),
        P("section", "tensor"),
        P("section", "dp", None, None, "tensor"),
        P("section", "dp", None, None, "tensor"),
        P("section", "dp", "tensor"),
        P("section", "dp", "tensor"),
        P("section", "dp", None),
    )
    out_specs = (P("section", "tensor", None), P("section", None, "tensor"))
    return jax.shard_map(
        on_device, mesh=mesh, in_specs=in_specs, out_specs=out_specs, check_vma=False
    )
```
